256 devices in a mesh: expert: 32 (over x, y, core), dp: 8 (over z).
Axes of the slice: x: 4, y: 4, z: 8, core: 2. Of those that a mesh axis runs over, the one named last changes fastest.
Arguments:
- tokens: bfloat16 [16384, 2048], P(('expert', 'dp')), may hold values from -6 to 6
- out_grad: bfloat16 [16384, 2048], P(('expert', 'dp')), may hold values from -6 to 6
- expert_ids: int32 [16384, 8], P(('expert', 'dp')), may hold values from 0 to 31, all different within a row; in each aligned block of 64 rows (0 to 63, 64 to 127, ...) at most 24 rows name the same one
- gate_probs: float32 [16384, 8], P(('expert', 'dp')), may hold values from 0.1 to 0.5
- gu_codes: bfloat16 [32, 2048, 1536], P('expert'), may hold values from -4 to 4
- gu_scales: float32 [32, 16, 12], P('expert'), may hold values from 0.011048543 to 0.044194173
- down_codes: bfloat16 [32, 2048, 768], P('expert'), may hold values from -4 to 4
- down_scales: float32 [32, 16, 6], P('expert'), may hold values from 0.018042196 to 0.07216878
Outputs:
- token_grad: bfloat16 [16384, 2048], P(('expert', 'dp'))
- down_grad: float32 [32, 2048, 768], P('expert', 'dp')
The draws below stay inside these ranges and needn't reach their ends.
Inputs may be any that keep to these rules, and one draw needn't show every extreme that they name: `expert_ids`: each token names 8 different experts. Among the 64 tokens of one device (aligned blocks of rows) no expert is named by more than 24 tokens, and in every draw some expert is named by exactly 24 of some device's tokens.
All inputs are finite; a program needn't handle non-finite values.
Results may differ from the reference program's by a relative error of at most 0.0083.
Values may be sent and summed in bfloat16 or wider, within the bound.
No kernel may reach another device: no remote copies, remote signals or barrier semaphores. Data moves between devices by JAX's collectives and lax.ppermute only.
A program may use at most 128 MiB of HBM per device.

```python
import math
import jax
import jax.numpy as jnp
import numpy as np
from jax import lax

D = 2048
FF = 768
TOP = 8
BLOCK = 128
TOK_DEV = 64
EXPERTS = 32
MOST = 24
TOKENS = 16384


def levels(key, extent, cuts, smallest, largest):
    def one(axis_at, parts):
        heights = jax.random.uniform(jax.random.fold_in(jax.random.fold_in(key, 6), axis_at), (parts,), jnp.float32, smallest / len(cuts), largest / len(cuts))
        return jnp.repeat(jnp.exp(heights), extent[axis_at] // parts).reshape((-1,) + (1,) * (len(extent) - axis_at - 1))

    gain = one(*cuts[0])
    for cut in cuts[1:]:
        gain = gain * one(*cut)
    return gain


def shared_out(own_key, own, number, rows, amount, top, limit, skew):
    ranking = jax.random.permutation(own_key, amount)
    heavy_load, ordinary = load_shares(amount, rows * top, limit, skew, True), load_shares(amount, rows * top, limit, skew, False)
    places = jnp.arange(amount)

    def named(lengths, rotation):
        used = int((lengths > 0).sum())
        fixed = max(1, used // 4)
        passed = fixed + (places - fixed + rotation * (used - fixed)) % max(1, amount - fixed)
        return jnp.zeros((amount,), jnp.int32).at[ranking[jnp.where(places < fixed, places, passed)]].set(jnp.asarray(lengths, jnp.int32))

    lengths = jnp.where(number % 4 == 0, named(heavy_load, number // 4), named(ordinary, number - number // 4 - 1))
    mixed = jax.random.permutation(jax.random.fold_in(own, 3), amount)
    giver, sink = mixed[0:amount // 2 * 2:2], mixed[1:amount // 2 * 2:2]
    slack = jnp.minimum(lengths[giver] - 1, limit - lengths[sink]) // 2
    slack = jnp.where((giver == ranking[0]) | (sink == ranking[0]) | (lengths[sink] == 0), 0, jnp.maximum(slack, 0))
    passed = jax.random.randint(jax.random.fold_in(own, 4), (amount // 2,), 0, 1 << 20) % (slack + 1)
    lengths = lengths.at[giver].add(-passed).at[sink].add(passed)
    labels = jnp.searchsorted(jnp.cumsum(lengths), jnp.arange(rows * top), side="right").astype(jnp.int32)
    grid = labels.reshape(top, rows).T
    grid = grid[jax.random.permutation(jax.random.fold_in(own, 1), rows)]
    rotation = jax.random.randint(jax.random.fold_in(own, 2), (rows, 1), 0, top)
    return jnp.take_along_axis(grid, (jnp.arange(top)[None, :] + rotation) % top, axis=1)


def load_shares(count, total, reach, skew, full):
    loads = [(1 << 20) // math.isqrt(rank ** skew) + 1 for rank in range(1, count + 1)]
    largest = reach if full else min(reach, max(-(-total // count), total * loads[0] // sum(loads)))
    least = 1 if total - largest >= count - 1 else 0
    counts, surplus = [largest] + [least] * (count - 1), total - largest - least * (count - 1)
    while surplus > 0:
        movable = [i for i in range(1, count) if counts[i] < largest] or [i for i in range(1, count) if counts[i] < reach]
        mass, remaining = sum([loads[i] for i in movable]), surplus
        for i in movable:
            addition = min(reach - counts[i], max(1, remaining * loads[i] // mass), surplus)
            counts[i] = counts[i] + addition
            surplus = surplus - addition
    return np.array(counts)


def noise(key, extent, scale, most, cuts=(), kind=jnp.bfloat16):
    level = levels(key, extent, cuts, -0.22, 0.18) if cuts else 1.0
    values = jax.random.normal(key, extent, jnp.float32) * scale * level
    return jnp.minimum(jnp.maximum(values, -most), most).astype(kind)


def setup_inputs(seed: int = 0) -> dict:
    key_list = jax.random.split(jax.random.key(seed), 9)
    tokens = noise(key_list[0], (TOKENS, D), 1.0, 6.0, ((0, 256),))
    out_grad = noise(key_list[1], (TOKENS, D), 1.0, 6.0, ((0, 256),))
    expert_ids_keys = jax.random.split(jax.random.fold_in(key_list[2], 1), TOKENS // TOK_DEV)
    expert_ids_turns = jax.random.permutation(jax.random.fold_in(key_list[2], 3), TOKENS // TOK_DEV)
    expert_ids = jax.vmap(lambda own, number: shared_out(jax.random.fold_in(key_list[2], 2), own, number, TOK_DEV, EXPERTS, TOP, MOST, 2))(expert_ids_keys, expert_ids_turns).reshape((TOKENS, TOP))
    gate_probs = jnp.clip(0.1 + 0.4 * jax.random.uniform(key_list[3], (TOKENS, TOP), jnp.float32) ** levels(key_list[3], (TOKENS, TOP), ((0, 256),), -0.2, 0.2), 0.1, 0.5)
    gu_codes = noise(key_list[4], (EXPERTS, D, 2 * FF), 1.0, 4.0, ((0, 32),))
    gu_scales = jnp.clip(jnp.exp(math.log(0.044194173) - 1.3862944 * jax.random.uniform(key_list[5], (EXPERTS, D // BLOCK, 2 * FF // BLOCK), jnp.float32) ** levels(key_list[5], (EXPERTS, D // BLOCK, 2 * FF // BLOCK), ((0, 32),), -0.2, 0.2)), 0.011048543, 0.044194173)
    down_codes = noise(key_list[6], (EXPERTS, D, FF), 1.0, 4.0, ((0, 32),))
    down_scales = jnp.clip(jnp.exp(math.log(0.07216878) - 1.3862944 * jax.random.uniform(key_list[7], (EXPERTS, D // BLOCK, FF // BLOCK), jnp.float32) ** levels(key_list[7], (EXPERTS, D // BLOCK, FF // BLOCK), ((0, 32),), -0.2, 0.2)), 0.018042196, 0.07216878)
    return dict(tokens=tokens, out_grad=out_grad, expert_ids=expert_ids, gate_probs=gate_probs, gu_codes=gu_codes, gu_scales=gu_scales, down_codes=down_codes, down_scales=down_scales)


def dequantize(codes, scales):
    block = codes.shape[0] // scales.shape[0]
    full = jnp.repeat(jnp.repeat(scales, block, axis=0), block, axis=1)
    return (codes.astype(jnp.float32) * full).astype(jnp.bfloat16)


def silu_parts(gate_part):
    sigma = jax.nn.sigmoid(gate_part)
    return gate_part * sigma, sigma * (1.0 + gate_part * (1.0 - sigma))


def reference(tokens, out_grad, expert_ids, gate_probs, gu_codes, gu_scales, down_codes, down_scales):
    blocks = TOKENS // TOK_DEV
    pair_count = TOK_DEV * TOP
    chosen = expert_ids.reshape(blocks, pair_count)
    probs = gate_probs.reshape(blocks, pair_count)
    owner_tok = (jnp.arange(blocks, dtype=jnp.int32)[:, None] * TOK_DEV
                 + jnp.arange(pair_count, dtype=jnp.int32)[None, :] // TOP).astype(jnp.int32)
    onehot = (chosen[:, :, None] == jnp.arange(EXPERTS, dtype=jnp.int32)[None, None, :]).astype(jnp.int32)
    ranked = jnp.sum(jnp.cumsum(onehot, axis=1) * onehot, axis=2) - 1
    slot_ids = jnp.arange(MOST, dtype=jnp.int32)

    def per_expert(carry, inputs):
        expert, codes_gu, scales_gu, codes_down, scales_down = inputs
        hit = (chosen == expert)[:, None, :] & (ranked[:, None, :] == slot_ids[None, :, None])
        source = jnp.sum(jnp.where(hit, owner_tok[:, None, :], 0), axis=2).reshape(-1).astype(jnp.int32)
        weight = jnp.sum(jnp.where(hit, probs[:, None, :], 0.0), axis=2).reshape(-1)
        valid = jnp.any(hit, axis=2).reshape(-1)
        rows_in = jnp.where(valid[:, None], tokens[source], jnp.zeros((), jnp.bfloat16))
        grads_in = (weight[:, None] * out_grad[source].astype(jnp.float32)).astype(jnp.bfloat16)
        w_gu = dequantize(codes_gu, scales_gu)
        w_down = dequantize(codes_down, scales_down)
        projected = jnp.dot(rows_in, w_gu, preferred_element_type=jnp.float32)
        gate_part = projected[:, :FF]
        up_part = projected[:, FF:]
        activated, slope = silu_parts(gate_part)
        hidden = (activated * up_part).astype(jnp.bfloat16)
        d_hidden = jnp.dot(grads_in, w_down, preferred_element_type=jnp.float32)
        d_proj = jnp.concatenate([d_hidden * up_part * slope, d_hidden * activated], axis=1).astype(jnp.bfloat16)
        back = lax.dot_general(d_proj, w_gu, (((1,), (1,)), ((), ())),
                               preferred_element_type=jnp.float32).astype(jnp.bfloat16)
        carry = carry.at[source].add(jnp.where(valid[:, None], back.astype(jnp.float32), 0.0))
        down = lax.dot_general(grads_in, hidden, (((0,), (0,)), ((), ())), preferred_element_type=jnp.float32)
        return carry, down

    init = jnp.zeros((TOKENS, D), jnp.float32)
    total, down_grad = lax.scan(per_expert, init,
                                (jnp.arange(EXPERTS, dtype=jnp.int32), gu_codes, gu_scales, down_codes, down_scales))
    return total.astype(jnp.bfloat16), down_grad
```

```python
import jax
import jax.numpy as jnp
from jax import lax
from jax.experimental import pallas as pl
from jax.experimental.pallas import tpu as pltpu
from jax.sharding import PartitionSpec as P

F32 = jnp.float32
BF16 = jnp.bfloat16
SIDE = 4
CORES = 2
MOST = 24
BLK = SIDE * MOST
STEPS = ((2, 0), (2, 1), (1, 0), (1, 1), (3, 0), (3, 1), (0, 1), (0, 0))
NB = len(STEPS)
SLOTS = NB * BLK


def place(x, y, c):
    return (x * SIDE + y) * CORES + c


def route(hops, flip, first):
    pairs = []
    for x in range(SIDE):
        for y in range(SIDE):
            for c in range(CORES):
                if (c == 0) == first:
                    to = place((x + hops) % SIDE, y, c ^ flip)
                else:
                    to = place(x, (y + hops) % SIDE, c ^ flip)
                pairs.append((place(x, y, c), to))
    return pairs


def hop(a, hops, flip, first, back=False):
    pairs = route(hops, flip, first)
    if back:
        pairs = [(t, s) for s, t in pairs]
    return lax.ppermute(a, "expert", pairs)


VM = pl.BlockSpec(memory_space=pltpu.VMEM)
SM = pl.BlockSpec(memory_space=pltpu.SMEM)


def params(mib):
    return pltpu.CompilerParams(vmem_limit_bytes=mib * 2**20)


def cost(flops, nbytes):
    return pl.CostEstimate(flops=int(flops), bytes_accessed=int(nbytes), transcendentals=0)


def select_kernel(scaled, ex, meta, r0, r1, r2, r3, *rest):
    if scaled:
        outs, (rows, sel) = rest[:NB], rest[NB:]
    else:
        outs, sel_t, (rows, sel) = rest[:NB], rest[NB], rest[NB + 1 :]
    n = r0.shape[0]
    total = SIDE * n
    for j, r in enumerate((r0, r1, r2, r3)):
        rows[j * n : (j + 1) * n, :] = r[...]
    ids = meta[0:8, :]
    probs = meta[8:16, :]
    hits, weights = [], []
    for i in range(NB):
        eq = ids == ex[i]
        hits.append(jnp.max(jnp.where(eq, 1.0, 0.0), axis=0, keepdims=True))
        if scaled:
            weights.append(jnp.sum(jnp.where(eq, probs, 0.0), axis=0, keepdims=True))
    hit = jnp.concatenate(hits, axis=0)
    s_at = lax.broadcasted_iota(jnp.int32, (total, total), 0)
    t_at = lax.broadcasted_iota(jnp.int32, (total, total), 1)
    before = jnp.where((s_at < t_at) & (s_at // n == t_at // n), 1.0, 0.0).astype(BF16)
    rank = jnp.dot(hit.astype(BF16), before, preferred_element_type=F32)
    group = (lax.broadcasted_iota(jnp.int32, (NB, total), 1) // n).astype(F32)
    slot = jnp.where(hit > 0.0, rank + MOST * group, -1.0)
    at = lax.broadcasted_iota(jnp.int32, (BLK, total), 0).astype(F32)
    cols = []
    for i in range(NB):
        one = at == slot[i : i + 1, :]
        sel[i * BLK : (i + 1) * BLK, :] = jnp.where(one, 1.0, 0.0).astype(BF16)
        if scaled:
            cols.append(jnp.sum(jnp.where(one, weights[i], 0.0), axis=1, keepdims=True))
    if not scaled:
        sel_t[...] = jnp.transpose(sel[...].astype(F32)).astype(BF16)
    width = 512
    for k in range(rows.shape[1] // width):
        lo = k * width
        got = jnp.dot(sel[...], rows[:, lo : lo + width], preferred_element_type=F32)
        for i in range(NB):
            part = got[i * BLK : (i + 1) * BLK, :]
            if scaled:
                part = part * cols[i]
            outs[i][:, lo : lo + width] = part.astype(BF16)


def select(scaled, ex, meta, blocks):
    n, d = blocks[0].shape
    out = [jax.ShapeDtypeStruct((BLK, d), BF16)] * NB
    if not scaled:
        out = out + [jax.ShapeDtypeStruct((SIDE * n, SLOTS), BF16)]
    return pl.pallas_call(
        lambda *refs: select_kernel(scaled, *refs),
        out_shape=out,
        in_specs=[SM] + [VM] * 5,
        out_specs=[VM] * len(out),
        scratch_shapes=[pltpu.VMEM((SIDE * n, d), BF16), pltpu.VMEM((SLOTS, SIDE * n), BF16)],
        compiler_params=params(24),
        cost_estimate=cost(2 * SLOTS * SIDE * n * d, 2 * d * (SLOTS + SIDE * n)),
        name="select_g" if scaled else "select_x",
    )(ex, meta, *blocks)


def weights_kernel(gu, gs, dn, ds, w_gu, w_gut, w_dn):
    wide = gu[...].astype(F32) * gs[0]
    w_gu[...] = wide.astype(BF16)
    w_gut[...] = jnp.transpose(wide).astype(BF16)
    w_dn[...] = (dn[...].astype(F32) * ds[0]).astype(BF16)


def weights(gu, gs, dn, ds):
    d, f2 = gu.shape
    f = dn.shape[1]
    nblk = gs.shape[0]
    side = d // nblk
    gs_row = jnp.repeat(gs, f2 // gs.shape[1], axis=1)[:, None, :]
    ds_row = jnp.repeat(ds, f // ds.shape[1], axis=1)[:, None, :]
    return pl.pallas_call(
        weights_kernel,
        grid=(nblk,),
        out_shape=[
            jax.ShapeDtypeStruct((d, f2), BF16),
            jax.ShapeDtypeStruct((f2, d), BF16),
            jax.ShapeDtypeStruct((d, f), BF16),
        ],
        in_specs=[
            pl.BlockSpec((side, f2), lambda i: (i, 0)),
            pl.BlockSpec((1, 1, f2), lambda i: (i, 0, 0)),
            pl.BlockSpec((side, f), lambda i: (i, 0)),
            pl.BlockSpec((1, 1, f), lambda i: (i, 0, 0)),
        ],
        out_specs=[
            pl.BlockSpec((side, f2), lambda i: (i, 0)),
            pl.BlockSpec((f2, side), lambda i: (0, i)),
            pl.BlockSpec((side, f), lambda i: (i, 0)),
        ],
        compiler_params=params(16),
        cost_estimate=cost(d * f2 * 6, 2 * d * (3 * f2 + 2 * f)),
        name="weights",
    )(gu, gs_row, dn, ds_row)


def forward_kernel(*refs):
    xs, (wg, wu, hid_t, upslope, act, rows) = refs[:NB], refs[NB:]

    @pl.when(pl.program_id(0) == 0)
    def _():
        for i in range(NB):
            rows[i * BLK : (i + 1) * BLK, :] = xs[i][...]

    gate = jnp.dot(rows[...], wg[...], preferred_element_type=F32)
    up = jnp.dot(rows[...], wu[...], preferred_element_type=F32)
    s = jax.nn.sigmoid(gate)
    a = gate * s
    act[...] = a
    upslope[...] = up * (s * (1.0 + gate * (1.0 - s)))
    hid_t[...] = jnp.transpose(a * up).astype(BF16)


def forward(xs, w_gu):
    d, f2 = w_gu.shape
    f = f2 // 2
    width = 256
    steps = f // width
    return pl.pallas_call(
        forward_kernel,
        grid=(steps,),
        out_shape=[
            jax.ShapeDtypeStruct((f, SLOTS), BF16),
            jax.ShapeDtypeStruct((SLOTS, f), F32),
            jax.ShapeDtypeStruct((SLOTS, f), F32),
        ],
        in_specs=[pl.BlockSpec((BLK, d), lambda i: (0, 0))] * NB
        + [
            pl.BlockSpec((d, width), lambda i: (0, i)),
            pl.BlockSpec((d, width), lambda i: (0, i + steps)),
        ],
        out_specs=[
            pl.BlockSpec((width, SLOTS), lambda i: (i, 0)),
            pl.BlockSpec((SLOTS, width), lambda i: (0, i)),
            pl.BlockSpec((SLOTS, width), lambda i: (0, i)),
        ],
        scratch_shapes=[pltpu.VMEM((SLOTS, d), BF16)],
        compiler_params=params(32),
        cost_estimate=cost(2 * SLOTS * d * f2, 2 * d * (SLOTS + f2) + 10 * SLOTS * f),
        name="forward",
    )(*xs, w_gu, w_gu)


def down_kernel(*refs):
    gs, (hid_t, out, rows) = refs[:NB], refs[NB:]
    for i in range(NB):
        rows[i * BLK : (i + 1) * BLK, :] = gs[i][...]
    out[0] = jnp.dot(hid_t[...], rows[...], preferred_element_type=F32).astype(BF16)


def down(gs, hid_t, owners):
    d = gs[0].shape[1]
    f = hid_t.shape[0]
    width = d // owners
    return pl.pallas_call(
        down_kernel,
        grid=(owners,),
        out_shape=jax.ShapeDtypeStruct((owners, f, width), BF16),
        in_specs=[pl.BlockSpec((BLK, width), lambda i: (0, i))] * NB
        + [pl.BlockSpec((f, SLOTS), lambda i: (0, 0))],
        out_specs=pl.BlockSpec((1, f, width), lambda i: (i, 0, 0)),
        scratch_shapes=[pltpu.VMEM((SLOTS, width), BF16)],
        compiler_params=params(16),
        cost_estimate=cost(2 * SLOTS * d * f, 2 * d * (SLOTS + f) + 2 * SLOTS * f),
        name="down",
    )(*gs, hid_t)


def dproj_kernel(*refs):
    gs, (wd, upslope, act, dg, du, rows) = refs[:NB], refs[NB:]

    @pl.when(pl.program_id(0) == 0)
    def _():
        for i in range(NB):
            rows[i * BLK : (i + 1) * BLK, :] = gs[i][...]

    dh = jnp.dot(rows[...], wd[...], preferred_element_type=F32)
    dg[...] = (dh * upslope[...]).astype(BF16)
    du[...] = (dh * act[...]).astype(BF16)


def dproj(gs, w_dn, upslope, act):
    d, f = w_dn.shape
    width = 256
    return pl.pallas_call(
        dproj_kernel,
        grid=(f // width,),
        out_shape=[jax.ShapeDtypeStruct((SLOTS, f), BF16)] * 2,
        in_specs=[pl.BlockSpec((BLK, d), lambda i: (0, 0))] * NB
        + [
            pl.BlockSpec((d, width), lambda i: (0, i)),
            pl.BlockSpec((SLOTS, width), lambda i: (0, i)),
            pl.BlockSpec((SLOTS, width), lambda i: (0, i)),
        ],
        out_specs=[pl.BlockSpec((SLOTS, width), lambda i: (0, i))] * 2,
        scratch_shapes=[pltpu.VMEM((SLOTS, d), BF16)],
        compiler_params=params(32),
        cost_estimate=cost(2 * SLOTS * d * f, 2 * d * (SLOTS + f) + 12 * SLOTS * f),
        name="dproj",
    )(*gs, w_dn, upslope, act)


def back_kernel(dg, du, wg, wu, *outs):
    got = jnp.dot(dg[...], wg[...], preferred_element_type=F32)
    got = got + jnp.dot(du[...], wu[...], preferred_element_type=F32)
    for i, out in enumerate(outs):
        out[...] = got[i * BLK : (i + 1) * BLK, :].astype(BF16)


def back(dg, du, w_gut, lo, count):
    f2, d = w_gut.shape
    f = f2 // 2
    width = 512
    rows = count * BLK
    at = lo // count
    return pl.pallas_call(
        back_kernel,
        grid=(d // width,),
        out_shape=[jax.ShapeDtypeStruct((BLK, d), BF16)] * count,
        in_specs=[
            pl.BlockSpec((rows, f), lambda i: (at, 0)),
            pl.BlockSpec((rows, f), lambda i: (at, 0)),
            pl.BlockSpec((f, width), lambda i: (0, i)),
            pl.BlockSpec((f, width), lambda i: (1, i)),
        ],
        out_specs=[pl.BlockSpec((BLK, width), lambda i: (0, i))] * count,
        compiler_params=params(24),
        cost_estimate=cost(2 * rows * d * f2, 2 * d * (rows + f2) + 2 * rows * f2),
        name="back",
    )(dg, du, w_gut, w_gut)


def combine_kernel(sel_t, *refs):
    ret, (own, o1, o2, o3, rows) = refs[:NB], refs[NB:]
    n = own.shape[0]
    for i in range(NB):
        rows[i * BLK : (i + 1) * BLK, :] = ret[i][...]
    got = jnp.dot(sel_t[...], rows[...], preferred_element_type=F32)
    own[...] = got[0:n, :]
    for j, out in enumerate((o1, o2, o3)):
        out[...] = got[(j + 1) * n : (j + 2) * n, :].astype(BF16)


def combine(sel_t, ret):
    total = sel_t.shape[0]
    n = total // SIDE
    d = ret[0].shape[1]
    width = 512
    return pl.pallas_call(
        combine_kernel,
        grid=(d // width,),
        out_shape=[jax.ShapeDtypeStruct((n, d), F32)]
        + [jax.ShapeDtypeStruct((n, d), BF16)] * (SIDE - 1),
        in_specs=[pl.BlockSpec((total, SLOTS), lambda i: (0, 0))]
        + [pl.BlockSpec((BLK, width), lambda i: (0, i))] * NB,
        out_specs=[pl.BlockSpec((n, width), lambda i: (0, i))] * SIDE,
        scratch_shapes=[pltpu.VMEM((SLOTS, width), BF16)],
        compiler_params=params(16),
        cost_estimate=cost(2 * SLOTS * d * total, 2 * d * (SLOTS + 2 * total)),
        name="combine",
    )(sel_t, *ret)


def on_device(tokens, out_grad, expert_ids, gate_probs, gu_codes, gu_scales, down_codes, down_scales):
    owners = lax.axis_size("dp")
    e = lax.axis_index("expert")
    c, y, x = e % CORES, (e // CORES) % SIDE, e // (CORES * SIDE)
    named = []
    for hops, flip in STEPS:
        one = place(x, (y + hops) % SIDE, flip)
        two = place((x + hops) % SIDE, y, 1 - flip)
        named.append(jnp.where(c == 0, one, two))
    ex = jnp.stack(named).astype(F32)

    meta = jnp.concatenate([expert_ids.T.astype(F32), gate_probs.T], axis=0)
    metas = [meta] + [hop(meta, j, 0, True) for j in (1, 2, 3)]
    xs1 = [tokens] + [hop(tokens, j, 0, True) for j in (1, 2, 3)]
    gs1 = [out_grad] + [hop(out_grad, j, 0, True) for j in (1, 2, 3)]
    meta_all = jnp.concatenate(metas, axis=1)

    w_gu, w_gut, w_dn = weights(gu_codes[0], gu_scales[0], down_codes[0], down_scales[0])

    *xs, sel_t = select(False, ex, meta_all, xs1)
    xs = [hop(a, h, f, False) if (h or f) else a for a, (h, f) in zip(xs, STEPS)]
    gs = select(True, ex, meta_all, gs1)
    gs = [hop(a, h, f, False) if (h or f) else a for a, (h, f) in zip(gs, STEPS)]

    hid_t, upslope, act = forward(xs, w_gu)
    part = down(gs, hid_t, owners)
    f, width = part.shape[1:]
    total = lax.psum_scatter(part.reshape(owners * f, width), "dp", scatter_dimension=0, tiled=True)

    dg, du = dproj(gs, w_dn, upslope, act)
    half = NB // 2
    ret = list(back(dg, du, w_gut, 0, half)) + list(back(dg, du, w_gut, half, half))
    ret = [hop(a, h, f, False, True) if (h or f) else a for a, (h, f) in zip(ret, STEPS)]
    own, *others = combine(sel_t, ret)
    others = [hop(a, j, 0, True, True) for j, a in zip((1, 2, 3), others)]
    token_grad = own
    for a in others:
        token_grad = token_grad + a.astype(F32)
    down_grad = total.astype(F32).T
    return token_grad.astype(BF16), down_grad[None]


def solution(mesh):
    rows = P(("expert", "dp"), None)
    per = P("expert", None, None)
    return jax.shard_map(
        on_device,
        mesh=mesh,
        in_specs=(rows, rows, rows, rows, per, per, per, per),
        out_specs=(rows, P("expert", "dp", None)),
        check_vma=False,
    )
```

```python
import jax
import jax.numpy as jnp
from jax import lax
from jax.experimental import pallas as pl
from jax.experimental.pallas import tpu as pltpu
from jax.sharding import PartitionSpec as P

F32 = jnp.float32
BF16 = jnp.bfloat16
SIDE = 4
CORES = 2
MOST = 24
BLK = SIDE * MOST
STEPS = ((2, 0), (2, 1), (1, 0), (1, 1), (3, 0), (3, 1), (0, 1), (0, 0))
NB = len(STEPS)
SLOTS = NB * BLK
GROUP = 4


def place(x, y, c):
    return (x * SIDE + y) * CORES + c


def route(hops, flip, first):
    pairs = []
    for x in range(SIDE):
        for y in range(SIDE):
            for c in range(CORES):
                if (c == 0) == first:
                    to = place((x + hops) % SIDE, y, c ^ flip)
                else:
                    to = place(x, (y + hops) % SIDE, c ^ flip)
                pairs.append((place(x, y, c), to))
    return pairs


def hop(a, hops, flip, first, back=False):
    pairs = route(hops, flip, first)
    if back:
        pairs = [(t, s) for s, t in pairs]
    return lax.ppermute(a, "expert", pairs)


def params(mib=56):
    return pltpu.CompilerParams(vmem_limit_bytes=mib * 2**20)


def cost(flops, nbytes):
    return pl.CostEstimate(flops=int(flops), bytes_accessed=int(nbytes), transcendentals=0)


def pack_kernel(tok, grad, ids, probs, out, pad):
    n = tok.shape[0]
    top = ids.shape[0]
    out[0:n, :] = tok[...]
    out[n : 2 * n, :] = grad[...]
    out[2 * n :, :] = jnp.zeros((16, out.shape[1]), BF16)
    pad[...] = jnp.zeros_like(pad)
    pad[0:top, 0:n] = ids[...].astype(F32)
    out[2 * n :, 0:128] = pad[...].astype(BF16)
    pad[0:top, 0:n] = probs[...]
    rest = pad[...]
    for i in (1, 2, 3):
        term = rest.astype(BF16)
        out[2 * n :, i * 128 : (i + 1) * 128] = term
        rest = rest - term.astype(F32)


def pack(tok, grad, ids, probs):
    n, d = tok.shape
    return pl.pallas_call(
        pack_kernel,
        out_shape=jax.ShapeDtypeStruct((2 * n + 16, d), BF16),
        scratch_shapes=[pltpu.VMEM((16, 128), F32)],
        compiler_params=params(),
        cost_estimate=cost(0, 8 * n * d),
        name="pack",
    )(tok, grad, ids.T, probs.T)


def select_kernel(scaled, ex, *refs):
    metas, data, rest = refs[:SIDE], refs[SIDE : 2 * SIDE], refs[2 * SIDE :]
    if scaled:
        outs, (rows, sel, weight) = rest[:NB], rest[NB:]
    else:
        outs, sel_t, (rows, sel) = rest[:NB], rest[NB], rest[NB + 1 :]
    n = data[0].shape[0]
    total = SIDE * n

    @pl.when(pl.program_id(0) == 0)
    def _():
        def along(lo):
            parts = [m[:, lo : lo + 128].astype(F32) for m in metas]
            low = lax.broadcasted_iota(jnp.int32, parts[0].shape, 1) < n
            pairs = [jnp.where(low, parts[j], pltpu.roll(parts[j + 1], n, 1)) for j in (0, 2)]
            return jnp.concatenate(pairs, axis=1)[0:8, :]

        ids = along(0)
        if scaled:
            probs = (along(128) + along(256)) + along(384)
        hits, weights = [], []
        for i in range(NB):
            eq = ids == ex[i]
            hits.append(jnp.max(jnp.where(eq, 1.0, 0.0), axis=0, keepdims=True))
            if scaled:
                weights.append(jnp.sum(jnp.where(eq, probs, 0.0), axis=0, keepdims=True))
        hit = jnp.concatenate(hits, axis=0)
        s_at = lax.broadcasted_iota(jnp.int32, (total, total), 0)
        t_at = lax.broadcasted_iota(jnp.int32, (total, total), 1)
        before = jnp.where((s_at < t_at) & (s_at // n == t_at // n), 1.0, 0.0).astype(BF16)
        rank = jnp.dot(hit.astype(BF16), before, preferred_element_type=F32)
        group = (lax.broadcasted_iota(jnp.int32, (NB, total), 1) // n).astype(F32)
        slot = jnp.where(hit > 0.0, rank + MOST * group, -1.0)
        at = lax.broadcasted_iota(jnp.int32, (BLK, total), 0).astype(F32)
        for i in range(NB):
            one = at == slot[i : i + 1, :]
            sel[i * BLK : (i + 1) * BLK, :] = jnp.where(one, 1.0, 0.0).astype(BF16)
            if scaled:
                col = jnp.sum(jnp.where(one, weights[i], 0.0), axis=1, keepdims=True)
                weight[i * BLK : (i + 1) * BLK, :] = jnp.broadcast_to(col, (BLK, 128))
        if not scaled:
            sel_t[...] = jnp.transpose(sel[...].astype(F32)).astype(BF16)

    for j, r in enumerate(data):
        rows[j * n : (j + 1) * n, :] = r[...]
    got = jnp.dot(sel[...], rows[...], preferred_element_type=F32)
    for i in range(NB):
        part = got[i * BLK : (i + 1) * BLK, :]
        if scaled:
            part = part * weight[i * BLK : (i + 1) * BLK, 0:1]
        outs[i][...] = part.astype(BF16)


def select(scaled, ex, blocks):
    d = blocks[0].shape[1]
    n = (blocks[0].shape[0] - 16) // 2
    width = 512
    out = [jax.ShapeDtypeStruct((BLK, d), BF16)] * NB
    out_specs = [pl.BlockSpec((BLK, width), lambda i: (0, i))] * NB
    scratch = [pltpu.VMEM((SIDE * n, width), BF16), pltpu.VMEM((SLOTS, SIDE * n), BF16)]
    if scaled:
        scratch = scratch + [pltpu.VMEM((SLOTS, 128), F32)]
    else:
        out = out + [jax.ShapeDtypeStruct((SIDE * n, SLOTS), BF16)]
        out_specs = out_specs + [pl.BlockSpec((SIDE * n, SLOTS), lambda i: (0, 0))]
    which = 1 if scaled else 0
    return pl.pallas_call(
        lambda *refs: select_kernel(scaled, *refs),
        grid=(d // width,),
        out_shape=out,
        in_specs=[pl.BlockSpec(memory_space=pltpu.SMEM)]
        + [pl.BlockSpec((16, width), lambda i: (2 * n // 16, 0))] * SIDE
        + [pl.BlockSpec((n, width), lambda i: (which, i))] * SIDE,
        out_specs=out_specs,
        scratch_shapes=scratch,
        compiler_params=params(),
        cost_estimate=cost(2 * SLOTS * SIDE * n * d, 2 * d * (SLOTS + SIDE * n)),
        name="select_g" if scaled else "select_x",
    )(ex, *blocks, *blocks)


def weights_kernel(gu, gs, dn, ds, w_gu, w_gut, w_dn):
    wide = gu[...].astype(F32) * gs[0]
    w_gu[...] = wide.astype(BF16)
    w_gut[...] = jnp.transpose(wide).astype(BF16)
    w_dn[...] = (dn[...].astype(F32) * ds[0]).astype(BF16)


def weights(gu, gs, dn, ds):
    d, f2 = gu.shape
    f = dn.shape[1]
    nblk = gs.shape[0]
    side = d // nblk
    gs_row = jnp.repeat(gs, f2 // gs.shape[1], axis=1)[:, None, :]
    ds_row = jnp.repeat(ds, f // ds.shape[1], axis=1)[:, None, :]
    return pl.pallas_call(
        weights_kernel,
        grid=(nblk,),
        out_shape=[
            jax.ShapeDtypeStruct((d, f2), BF16),
            jax.ShapeDtypeStruct((f2, d), BF16),
            jax.ShapeDtypeStruct((d, f), BF16),
        ],
        in_specs=[
            pl.BlockSpec((side, f2), lambda i: (i, 0)),
            pl.BlockSpec((1, 1, f2), lambda i: (i, 0, 0)),
            pl.BlockSpec((side, f), lambda i: (i, 0)),
            pl.BlockSpec((1, 1, f), lambda i: (i, 0, 0)),
        ],
        out_specs=[
            pl.BlockSpec((side, f2), lambda i: (i, 0)),
            pl.BlockSpec((f2, side), lambda i: (0, i)),
            pl.BlockSpec((side, f), lambda i: (i, 0)),
        ],
        compiler_params=params(),
        cost_estimate=cost(d * f2 * 6, 2 * d * (3 * f2 + 2 * f)),
        name="weights",
    )(gu, gs_row, dn, ds_row)


def forward_kernel(*refs):
    xs, (wg, wu, hid_t, upslope, act, rows) = refs[:NB], refs[NB:]

    @pl.when(pl.program_id(0) == 0)
    def _():
        for i in range(NB):
            rows[i * BLK : (i + 1) * BLK, :] = xs[i][...]

    gate = jnp.dot(rows[...], wg[...], preferred_element_type=F32)
    up = jnp.dot(rows[...], wu[...], preferred_element_type=F32)
    s = jax.nn.sigmoid(gate)
    a = gate * s
    act[...] = a
    upslope[...] = up * (s * (1.0 + gate * (1.0 - s)))
    hid_t[...] = jnp.transpose(a * up).astype(BF16)


def forward(xs, w_gu):
    d, f2 = w_gu.shape
    f = f2 // 2
    width = 256
    steps = f // width
    return pl.pallas_call(
        forward_kernel,
        grid=(steps,),
        out_shape=[
            jax.ShapeDtypeStruct((f, SLOTS), BF16),
            jax.ShapeDtypeStruct((SLOTS, f), F32),
            jax.ShapeDtypeStruct((SLOTS, f), F32),
        ],
        in_specs=[pl.BlockSpec((BLK, d), lambda i: (0, 0))] * NB
        + [
            pl.BlockSpec((d, width), lambda i: (0, i)),
            pl.BlockSpec((d, width), lambda i: (0, i + steps)),
        ],
        out_specs=[
            pl.BlockSpec((width, SLOTS), lambda i: (i, 0)),
            pl.BlockSpec((SLOTS, width), lambda i: (0, i)),
            pl.BlockSpec((SLOTS, width), lambda i: (0, i)),
        ],
        scratch_shapes=[pltpu.VMEM((SLOTS, d), BF16)],
        compiler_params=params(),
        cost_estimate=cost(2 * SLOTS * d * f2, 2 * d * (SLOTS + f2) + 10 * SLOTS * f),
        name="forward",
    )(*xs, w_gu, w_gu)


def ring_kernel(stage, at, *refs):
    gs, refs = refs[:NB], refs[NB:]
    hid_t, refs = refs[0], refs[1:]
    rows = refs[-1]
    for i in range(NB):
        rows[i * BLK : (i + 1) * BLK, :] = gs[i][...]
    got = jnp.dot(hid_t[...], rows[...], preferred_element_type=F32)
    half = got.shape[0] // 2
    if stage == 0:
        right, left = refs[:2]
        right[...] = got[:half, :].astype(BF16)
        left[...] = got[half:, :].astype(BF16)
    elif stage < 4:
        from_left, from_right, right, left = refs[:4]
        step = pl.program_id(0)

        @pl.when(step == 0)
        def _():
            if stage == 1:
                right[:half, :] = (got[:half, :] + from_left[...].astype(F32)).astype(BF16)
                right[half:, :] = got[half:, :].astype(BF16)
            else:
                right[...] = (got + from_left[...].astype(F32)).astype(BF16)

        @pl.when(step == 1)
        def _():
            if stage == 1:
                left[:half, :] = got[:half, :].astype(BF16)
                left[half:, :] = (got[half:, :] + from_right[...].astype(F32)).astype(BF16)
            else:
                left[...] = (got + from_right[...].astype(F32)).astype(BF16)
    else:
        from_left, from_right, out = refs[:3]
        total = got + from_left[...].astype(F32) + from_right[...].astype(F32)
        out[...] = jnp.transpose(total)


def ring(stage, at, gs, hid_t, arrived, width):
    f = hid_t.shape[0]
    count = 2 if 0 < stage < 4 else 1
    if stage == 0:
        out = [jax.ShapeDtypeStruct((f // 2, width), BF16)] * 2
    elif stage < 4:
        out = [jax.ShapeDtypeStruct((f, width), BF16)] * 2
    else:
        out = [jax.ShapeDtypeStruct((width, f), F32)]
    whole = lambda i, at: (0, 0)
    return pl.pallas_call(
        lambda *refs: ring_kernel(stage, *refs),
        grid_spec=pltpu.PrefetchScalarGridSpec(
            num_scalar_prefetch=1,
            grid=(count,),
            in_specs=[pl.BlockSpec((BLK, width), lambda i, at: (0, at[i]))] * NB
            + [pl.BlockSpec((f, SLOTS), whole)]
            + [pl.BlockSpec(a.shape, whole) for a in arrived],
            out_specs=[pl.BlockSpec(o.shape, whole) for o in out],
            scratch_shapes=[pltpu.VMEM((SLOTS, width), BF16)],
        ),
        out_shape=out,
        compiler_params=params(),
        cost_estimate=cost(2 * SLOTS * width * f * count, 2 * SLOTS * f + 4 * count * f * width),
        name="ring",
    )(at, *gs, hid_t, *arrived)


def zhop(a, by):
    n = lax.axis_size("dp")
    return lax.ppermute(a, "dp", [(i, (i + by) % n) for i in range(n)])


def back_kernel(fsteps, *refs):
    gs, refs = refs[:GROUP], refs[GROUP:]
    wd, upslope, act, wg, wu = refs[:5]
    outs, (rows, dg, du) = refs[5 : 5 + GROUP], refs[5 + GROUP :]
    step = pl.program_id(0)

    @pl.when(step == 0)
    def _():
        for i in range(GROUP):
            rows[i * BLK : (i + 1) * BLK, :] = gs[i][...]

    @pl.when(step < fsteps)
    def _():
        dh = jnp.dot(rows[...], wd[...], preferred_element_type=F32)
        width = wd.shape[1]
        cols = pl.ds(pl.multiple_of(step * width, width), width)
        dg[:, cols] = (dh * upslope[...]).astype(BF16)
        du[:, cols] = (dh * act[...]).astype(BF16)

    @pl.when(step >= fsteps)
    def _():
        got = jnp.dot(dg[...], wg[...], preferred_element_type=F32)
        got = got + jnp.dot(du[...], wu[...], preferred_element_type=F32)
        for i in range(GROUP):
            outs[i][...] = got[i * BLK : (i + 1) * BLK, :].astype(BF16)


def back(gs, w_dn, upslope, act, w_gut, at):
    d, f = w_dn.shape
    fw, dw = 256, 512
    fsteps = f // fw
    rows = GROUP * BLK
    first = lambda i: jnp.minimum(i, fsteps - 1)
    second = lambda i: jnp.maximum(i - fsteps, 0)
    return pl.pallas_call(
        lambda *refs: back_kernel(fsteps, *refs),
        grid=(fsteps + d // dw,),
        out_shape=[jax.ShapeDtypeStruct((BLK, d), BF16)] * GROUP,
        in_specs=[pl.BlockSpec((BLK, d), lambda i: (0, 0))] * GROUP
        + [
            pl.BlockSpec((d, fw), lambda i: (0, first(i))),
            pl.BlockSpec((rows, fw), lambda i: (at, first(i))),
            pl.BlockSpec((rows, fw), lambda i: (at, first(i))),
            pl.BlockSpec((f, dw), lambda i: (0, second(i))),
            pl.BlockSpec((f, dw), lambda i: (1, second(i))),
        ],
        out_specs=[pl.BlockSpec((BLK, dw), lambda i: (0, second(i)))] * GROUP,
        scratch_shapes=[
            pltpu.VMEM((rows, d), BF16),
            pltpu.VMEM((rows, f), BF16),
            pltpu.VMEM((rows, f), BF16),
        ],
        compiler_params=params(),
        cost_estimate=cost(6 * rows * d * f, 2 * d * (2 * rows + 3 * f) + 8 * rows * f),
        name="back",
    )(*gs, w_dn, upslope, act, w_gut, w_gut)


def combine_kernel(sel_t, *refs):
    ret, (own, o1, o2, o3, rows) = refs[:NB], refs[NB:]
    n = own.shape[0]
    for i in range(NB):
        rows[i * BLK : (i + 1) * BLK, :] = ret[i][...]
    got = jnp.dot(sel_t[...], rows[...], preferred_element_type=F32)
    own[...] = got[0:n, :]
    for j, out in enumerate((o1, o2, o3)):
        out[...] = got[(j + 1) * n : (j + 2) * n, :].astype(BF16)


def combine(sel_t, ret):
    total = sel_t.shape[0]
    n = total // SIDE
    d = ret[0].shape[1]
    width = 512
    return pl.pallas_call(
        combine_kernel,
        grid=(d // width,),
        out_shape=[jax.ShapeDtypeStruct((n, d), F32)]
        + [jax.ShapeDtypeStruct((n, d), BF16)] * (SIDE - 1),
        in_specs=[pl.BlockSpec((total, SLOTS), lambda i: (0, 0))]
        + [pl.BlockSpec((BLK, width), lambda i: (0, i))] * NB,
        out_specs=[pl.BlockSpec((n, width), lambda i: (0, i))] * SIDE,
        scratch_shapes=[pltpu.VMEM((SLOTS, width), BF16)],
        compiler_params=params(),
        cost_estimate=cost(2 * SLOTS * d * total, 2 * d * (SLOTS + 2 * total)),
        name="combine",
    )(sel_t, *ret)


def on_device(tokens, out_grad, expert_ids, gate_probs, gu_codes, gu_scales, down_codes, down_scales):
    owners = lax.axis_size("dp")
    width = tokens.shape[1] // owners
    z = lax.axis_index("dp")
    e = lax.axis_index("expert")
    c, y, x = e % CORES, (e // CORES) % SIDE, e // (CORES * SIDE)
    named = []
    for hops, flip in STEPS:
        one = place(x, (y + hops) % SIDE, flip)
        two = place((x + hops) % SIDE, y, 1 - flip)
        named.append(jnp.where(c == 0, one, two))
    ex = jnp.stack(named).astype(F32)

    mine = pack(tokens, out_grad, expert_ids, gate_probs)
    blocks = [mine] + [hop(mine, j, 0, True) for j in (1, 2, 3)]
    w = weights(gu_codes[0], gu_scales[0], down_codes[0], down_scales[0])
    blocks, (w_gu, w_gut, w_dn) = lax.optimization_barrier((blocks, w))

    *xs, sel_t = select(False, ex, blocks)
    xs = [hop(a, h, f, False) if (h or f) else a for a, (h, f) in zip(xs, STEPS)]
    gs = select(True, ex, blocks)
    gs = [hop(a, h, f, False) if (h or f) else a for a, (h, f) in zip(gs, STEPS)]

    hid_t, upslope, act = forward(xs, w_gu)

    ret = []
    for at in range(NB // GROUP):
        ret += back(gs[at * GROUP : (at + 1) * GROUP], w_dn, upslope, act, w_gut, at)
    ret = [hop(a, h, f, False, True) if (h or f) else a for a, (h, f) in zip(ret, STEPS)]

    chunk = lambda *by: jnp.stack([(z + k) % owners for k in by]).astype(jnp.int32)
    arrived = []
    for stage, by in enumerate(((4,), (3, 5), (2, 6), (1, 7), (0,))):
        sums = ring(stage, chunk(*by), gs, hid_t, arrived, width)
        if stage < 4:
            arrived = [zhop(sums[0], 1), zhop(sums[1], owners - 1)]
    down_grad = sums[0]

    own, *others = combine(sel_t, ret)
    others = [hop(a, j, 0, True, True) for j, a in zip((1, 2, 3), others)]
    token_grad = own
    for a in others:
        token_grad = token_grad + a.astype(F32)
    return token_grad.astype(BF16), down_grad[None]


def solution(mesh):
    rows = P(("expert", "dp"), None)
    per = P("expert", None, None)
    return jax.shard_map(
        on_device,
        mesh=mesh,
        in_specs=(rows, rows, rows, rows, per, per, per, per),
        out_specs=(rows, P("expert", "dp", None)),
        check_vma=False,
    )
```

```python
import jax
import jax.numpy as jnp
from jax import lax
from jax.experimental import pallas as pl
from jax.experimental.pallas import tpu as pltpu
from jax.sharding import PartitionSpec as P

F32 = jnp.float32
BF16 = jnp.bfloat16
SIDE = 4
CORES = 2
MOST = 24
BLK = SIDE * MOST
STEPS = ((1, 0), (3, 0), (0, 1), (1, 1), (2, 0), (2, 1), (3, 1), (0, 0))
NB = len(STEPS)
SLOTS = NB * BLK
GROUP = 4


def place(x, y, c):
    return (x * SIDE + y) * CORES + c


def route(hops, flip, first):
    pairs = []
    for x in range(SIDE):
        for y in range(SIDE):
            for c in range(CORES):
                if (c == 0) == first:
                    to = place((x + hops) % SIDE, y, c ^ flip)
                else:
                    to = place(x, (y + hops) % SIDE, c ^ flip)
                pairs.append((place(x, y, c), to))
    return pairs


def hop(a, hops, flip, first, back=False):
    pairs = route(hops, flip, first)
    if back:
        pairs = [(t, s) for s, t in pairs]
    return lax.ppermute(a, "expert", pairs)


VM = pl.BlockSpec(memory_space=pltpu.VMEM)
SM = pl.BlockSpec(memory_space=pltpu.SMEM)


def params(mib=28):
    return pltpu.CompilerParams(vmem_limit_bytes=mib * 2**20)


def cost(flops, nbytes):
    return pl.CostEstimate(flops=int(flops), bytes_accessed=int(nbytes), transcendentals=0)


def gather(blocks, rows):
    at = 0
    for b in blocks:
        rows[at : at + b.shape[0], :] = b[...]
        at += b.shape[0]


def pack_kernel(tok, ids, probs, out, pad):
    n = tok.shape[0]
    top = ids.shape[0]
    out[0:n, :] = tok[...]
    out[n:, :] = jnp.zeros((16, out.shape[1]), BF16)
    pad[...] = jnp.zeros_like(pad)
    pad[0:top, 0:n] = ids[...].astype(F32)
    out[n:, 0:128] = pad[...].astype(BF16)
    pad[0:top, 0:n] = probs[...]
    rest = pad[...]
    for i in (1, 2, 3):
        term = rest.astype(BF16)
        out[n:, i * 128 : (i + 1) * 128] = term
        rest = rest - term.astype(F32)


def pack(tok, ids, probs):
    n, d = tok.shape
    return pl.pallas_call(
        pack_kernel,
        out_shape=jax.ShapeDtypeStruct((n + 16, d), BF16),
        scratch_shapes=[pltpu.VMEM((16, 128), F32)],
        compiler_params=params(),
        cost_estimate=cost(0, 4 * n * d),
        name="pack",
    )(tok, ids.T, probs.T)


def slots(ex, metas, n):
    total = SIDE * n

    def along(lo):
        parts = [metas[j, :, lo : lo + 128].astype(F32) for j in range(SIDE)]
        low = lax.broadcasted_iota(jnp.int32, parts[0].shape, 1) < n
        pairs = [jnp.where(low, parts[j], pltpu.roll(parts[j + 1], n, 1)) for j in (0, 2)]
        return jnp.concatenate(pairs, axis=1)[0:8, :]

    ids = along(0)
    probs = (along(128) + along(256)) + along(384)
    hits, weights = [], []
    for i in range(NB):
        eq = ids == ex[i]
        hits.append(jnp.max(jnp.where(eq, 1.0, 0.0), axis=0, keepdims=True))
        weights.append(jnp.sum(jnp.where(eq, probs, 0.0), axis=0, keepdims=True))
    hit = jnp.concatenate(hits, axis=0)
    s_at = lax.broadcasted_iota(jnp.int32, (total, total), 0)
    t_at = lax.broadcasted_iota(jnp.int32, (total, total), 1)
    before = jnp.where((s_at < t_at) & (s_at // n == t_at // n), 1.0, 0.0).astype(BF16)
    rank = jnp.dot(hit.astype(BF16), before, preferred_element_type=F32)
    group = (lax.broadcasted_iota(jnp.int32, (NB, total), 1) // n).astype(F32)
    return jnp.where(hit > 0.0, rank + MOST * group, -1.0), weights


def select_kernel(scaled, ex, *refs):
    packed, refs = refs[:SIDE], refs[SIDE:]
    if scaled:
        grads, refs = refs[:SIDE], refs[SIDE:]
        outs, (sel_t, rows, metas, sel) = refs[:NB], refs[NB:]
    else:
        outs, (rows, metas, sel) = refs[:NB], refs[NB:]
    n = rows.shape[0] // SIDE
    d = rows.shape[1]
    total = SIDE * n
    for j in range(SIDE):
        metas[j] = packed[j][n:, 0 : metas.shape[2]]
        rows[j * n : (j + 1) * n, :] = grads[j][...] if scaled else packed[j][0:n, :]
    slot, weights = slots(ex, metas, n)
    at = lax.broadcasted_iota(jnp.int32, (BLK, total), 0).astype(F32)
    scale = []
    for i in range(NB):
        one = at == slot[i : i + 1, :]
        sel[i * BLK : (i + 1) * BLK, :] = jnp.where(one, 1.0, 0.0).astype(BF16)
        if scaled:
            scale.append(jnp.sum(jnp.where(one, weights[i], 0.0), axis=1, keepdims=True))
    width = 512
    for k in range(d // width):
        cols = slice(k * width, (k + 1) * width)
        got = jnp.dot(sel[...], rows[:, cols], preferred_element_type=F32)
        for i in range(NB):
            part = got[i * BLK : (i + 1) * BLK, :]
            if scaled:
                part = part * scale[i]
            outs[i][:, cols] = part.astype(BF16)
    if scaled:
        sel_t[...] = jnp.transpose(sel[...].astype(F32)).astype(BF16)


def select(ex, packed, grads=()):
    scaled = len(grads) > 0
    n, d = packed[0].shape[0] - 16, packed[0].shape[1]
    total = SIDE * n
    out = [jax.ShapeDtypeStruct((BLK, d), BF16)] * NB
    if scaled:
        out = out + [jax.ShapeDtypeStruct((total, SLOTS), BF16)]
    return pl.pallas_call(
        lambda *refs: select_kernel(scaled, *refs),
        out_shape=out,
        in_specs=[SM] + [VM] * (SIDE + len(grads)),
        out_specs=[VM] * len(out),
        scratch_shapes=[
            pltpu.VMEM((total, d), BF16),
            pltpu.VMEM((SIDE, 16, 512), BF16),
            pltpu.VMEM((SLOTS, total), BF16),
        ],
        compiler_params=params(),
        cost_estimate=cost(2 * SLOTS * total * d, 2 * d * (SLOTS + total)),
        name="select_g" if scaled else "select_x",
    )(ex, *packed, *grads)


def weights_kernel(per, gs, ds, gu, dn, w_gu, w_dn):
    side = gu.shape[0] // per
    step = pl.program_id(0)
    for i in range(per):
        at = slice(i * side, (i + 1) * side)
        for codes, scales, out in ((gu, gs, w_gu), (dn, ds, w_dn)):
            for j in range(codes.shape[1] // side):
                cols = slice(j * side, (j + 1) * side)
                out[at, cols] = (codes[at, cols].astype(F32) * scales[step * per + i, j]).astype(BF16)


def weights(gu, gs, dn, ds):
    d, f2 = gu.shape
    f = dn.shape[1]
    nblk = gs.shape[0]
    per = 2
    side = d // nblk * per
    blocks = [pl.BlockSpec((side, f2), lambda i: (i, 0)), pl.BlockSpec((side, f), lambda i: (i, 0))]
    return pl.pallas_call(
        lambda *refs: weights_kernel(per, *refs),
        grid=(nblk // per,),
        out_shape=[jax.ShapeDtypeStruct((d, f2), BF16), jax.ShapeDtypeStruct((d, f), BF16)],
        in_specs=[SM] * 2 + blocks,
        out_specs=blocks,
        compiler_params=params(),
        cost_estimate=cost(d * f2 * 6, 4 * d * (f2 + f)),
        name="weights",
    )(gs, ds, gu, dn)


def forward_kernel(*refs):
    xs, (w_gu, hid_t, upslope, act, rows) = refs[:NB], refs[NB:]
    f = hid_t.shape[0]
    width = 256
    gather(xs, rows)
    for k in range(f // width):
        lo, hi = k * width, (k + 1) * width
        gate = jnp.dot(rows[...], w_gu[:, lo:hi], preferred_element_type=F32)
        up = jnp.dot(rows[...], w_gu[:, f + lo : f + hi], preferred_element_type=F32)
        s = jax.nn.sigmoid(gate)
        a = gate * s
        act[:, lo:hi] = a
        upslope[:, lo:hi] = up * (s * (1.0 + gate * (1.0 - s)))
        hid_t[lo:hi, :] = jnp.transpose(a * up).astype(BF16)


def forward(xs, w_gu):
    d, f2 = w_gu.shape
    f = f2 // 2
    return pl.pallas_call(
        forward_kernel,
        out_shape=[
            jax.ShapeDtypeStruct((f, SLOTS), BF16),
            jax.ShapeDtypeStruct((SLOTS, f), F32),
            jax.ShapeDtypeStruct((SLOTS, f), F32),
        ],
        in_specs=[VM] * (NB + 1),
        out_specs=[VM] * 3,
        scratch_shapes=[pltpu.VMEM((SLOTS, d), BF16)],
        compiler_params=params(),
        cost_estimate=cost(2 * SLOTS * d * f2, 2 * d * (SLOTS + f2) + 10 * SLOTS * f),
        name="forward",
    )(*xs, w_gu)


def ring_kernel(stage, by, at, *refs):
    gs, hid_t, refs = refs[:NB], refs[NB], refs[NB + 1 :]
    arrived = () if stage == 0 else refs[:2]
    refs = refs[len(arrived) :]
    outs, rows = refs[:-1], refs[-1]
    f, width = hid_t.shape[0], rows.shape[2]
    half = f // 2
    for k, steps in enumerate(by):
        cols = pl.ds(pl.multiple_of(at[steps] * width, width), width)
        for i in range(NB):
            rows[k, i * BLK : (i + 1) * BLK, :] = gs[i][:, cols]
        got = jnp.dot(hid_t[...], rows[k], preferred_element_type=F32)
        if stage == 0:
            outs[0][...] = got[:half, :].astype(BF16)
            outs[1][...] = got[half:, :].astype(BF16)
        elif stage == 1:
            mine = slice(k * half, (k + 1) * half)
            rest = slice((1 - k) * half, (2 - k) * half)
            outs[k][mine, :] = (got[mine, :] + arrived[k][...].astype(F32)).astype(BF16)
            outs[k][rest, :] = got[rest, :].astype(BF16)
        elif stage < 4:
            outs[k][...] = (got + arrived[k][...].astype(F32)).astype(BF16)
        else:
            total = got + arrived[0][...].astype(F32) + arrived[1][...].astype(F32)
            outs[0][...] = jnp.transpose(total)


def ring(stage, by, at, gs, hid_t, arrived, width):
    f = hid_t.shape[0]
    count = len(by)
    if stage == 0:
        out = [jax.ShapeDtypeStruct((f // 2, width), BF16)] * 2
    elif stage < 4:
        out = [jax.ShapeDtypeStruct((f, width), BF16)] * 2
    else:
        out = [jax.ShapeDtypeStruct((width, f), F32)]
    return pl.pallas_call(
        lambda *refs: ring_kernel(stage, by, *refs),
        out_shape=out,
        in_specs=[SM] + [VM] * (NB + 1 + len(arrived)),
        out_specs=[VM] * len(out),
        scratch_shapes=[pltpu.VMEM((count, SLOTS, width), BF16)],
        compiler_params=params(),
        cost_estimate=cost(2 * SLOTS * width * f * count, 2 * SLOTS * f + 4 * count * f * width),
        name="ring",
    )(at, *gs, hid_t, *arrived)


def zhop(a, by):
    n = lax.axis_size("dp")
    return lax.ppermute(a, "dp", [(i, (i + by) % n) for i in range(n)])


def back_kernel(at, *refs):
    gs, refs = refs[:GROUP], refs[GROUP:]
    (w_dn, upslope, act, w_gu), refs = refs[:4], refs[4:]
    outs, (rows, dp) = refs[:GROUP], refs[GROUP:]
    count = GROUP * BLK
    d, f = w_dn.shape
    mine = slice(at * count, (at + 1) * count)
    gather(gs, rows)
    fw, dw = 256, 512
    for k in range(f // fw):
        lo, hi = k * fw, (k + 1) * fw
        dh = jnp.dot(rows[...], w_dn[:, lo:hi], preferred_element_type=F32)
        dp[:, lo:hi] = (dh * upslope[mine, lo:hi]).astype(BF16)
        dp[:, f + lo : f + hi] = (dh * act[mine, lo:hi]).astype(BF16)
    for k in range(d // dw):
        cols = slice(k * dw, (k + 1) * dw)
        got = lax.dot_general(
            dp[...], w_gu[cols, :], (((1,), (1,)), ((), ())), preferred_element_type=F32
        )
        for i in range(GROUP):
            outs[i][:, cols] = got[i * BLK : (i + 1) * BLK, :].astype(BF16)


def back(gs, w_dn, upslope, act, w_gu, at):
    d, f = w_dn.shape
    rows = GROUP * BLK
    return pl.pallas_call(
        lambda *refs: back_kernel(at, *refs),
        out_shape=[jax.ShapeDtypeStruct((BLK, d), BF16)] * GROUP,
        in_specs=[VM] * (GROUP + 4),
        out_specs=[VM] * GROUP,
        scratch_shapes=[pltpu.VMEM((rows, d), BF16), pltpu.VMEM((rows, 2 * f), BF16)],
        compiler_params=params(),
        cost_estimate=cost(6 * rows * d * f, 2 * d * (2 * rows + 3 * f) + 8 * rows * f),
        name="back",
    )(*gs, w_dn, upslope, act, w_gu)


def combine_kernel(sel_t, *refs):
    ret, refs = refs[:NB], refs[NB:]
    outs, rows = refs[:SIDE], refs[SIDE]
    n, d = outs[0].shape
    gather(ret, rows)
    width = 512
    for k in range(d // width):
        cols = slice(k * width, (k + 1) * width)
        got = jnp.dot(sel_t[...], rows[:, cols], preferred_element_type=F32)
        outs[0][:, cols] = got[0:n, :]
        for j in range(1, SIDE):
            outs[j][:, cols] = got[j * n : (j + 1) * n, :].astype(BF16)


def combine(sel_t, ret):
    total = sel_t.shape[0]
    n = total // SIDE
    d = ret[0].shape[1]
    return pl.pallas_call(
        combine_kernel,
        out_shape=[jax.ShapeDtypeStruct((n, d), F32)]
        + [jax.ShapeDtypeStruct((n, d), BF16)] * (SIDE - 1),
        in_specs=[VM] * (NB + 1),
        out_specs=[VM] * SIDE,
        scratch_shapes=[pltpu.VMEM((SLOTS, d), BF16)],
        compiler_params=params(),
        cost_estimate=cost(2 * SLOTS * d * total, 2 * d * (SLOTS + 2 * total)),
        name="combine",
    )(sel_t, *ret)


def on_device(tokens, out_grad, expert_ids, gate_probs, gu_codes, gu_scales, down_codes, down_scales):
    owners = lax.axis_size("dp")
    width = tokens.shape[1] // owners
    z = lax.axis_index("dp")
    e = lax.axis_index("expert")
    c, y, x = e % CORES, (e // CORES) % SIDE, e // (CORES * SIDE)
    named = []
    for hops, flip in STEPS:
        one = place(x, (y + hops) % SIDE, flip)
        two = place((x + hops) % SIDE, y, 1 - flip)
        named.append(jnp.where(c == 0, one, two))
    ex = jnp.stack(named).astype(F32)

    at = ((z + jnp.arange(owners)) % owners).astype(jnp.int32)

    mine = pack(tokens, expert_ids, gate_probs)
    packed = [mine] + [hop(mine, j, 0, True) for j in (2, 1, 3)]
    grads = [out_grad] + [hop(out_grad, j, 0, True) for j in (2, 1, 3)]
    w = weights(gu_codes[0], gu_scales[0], down_codes[0], down_scales[0])
    packed, (w_gu, w_dn) = lax.optimization_barrier((packed, w))

    xs = select(ex, packed)
    xs, grads = lax.optimization_barrier((xs, grads))
    xs = [hop(a, h, f, False) if (h or f) else a for a, (h, f) in zip(xs, STEPS)]
    *gs, sel_t = select(ex, packed, grads)
    gs = [hop(a, h, f, False) if (h or f) else a for a, (h, f) in zip(gs, STEPS)]

    hid_t, upslope, act = forward(xs, w_gu)

    late = back(gs[GROUP:], w_dn, upslope, act, w_gu, 1)
    near, hid_t, late = lax.optimization_barrier((gs[:GROUP], hid_t, late))
    gs = near + gs[GROUP:]

    arrived, sums = [], None
    stages = ((4,), (3, 5), (2, 6), (1, 7), (0,))
    ret = None
    for stage, by in enumerate(stages):
        sums = ring(stage, by, at, gs, hid_t, arrived, width)
        if stage < 4:
            arrived = [zhop(sums[0], 1), zhop(sums[1], owners - 1)]
        if stage == 0:
            ret = back(near, w_dn, upslope, act, w_gu, 0) + late
            ret = [hop(a, h, f, False, True) if (h or f) else a for a, (h, f) in zip(ret, STEPS)]
    down_grad = sums[0]

    own, *others = combine(sel_t, ret)
    others = [hop(a, j, 0, True, True) for j, a in zip((2, 1, 3), others)]
    token_grad = own
    for a in others:
        token_grad = token_grad + a.astype(F32)
    return token_grad.astype(BF16), down_grad[None]


def solution(mesh):
    rows = P(("expert", "dp"), None)
    per = P("expert", None, None)
    return jax.shard_map(
        on_device,
        mesh=mesh,
        in_specs=(rows, rows, rows, rows, per, per, per, per),
        out_specs=(rows, P("expert", "dp", None)),
        check_vma=False,
    )
```

```python
import jax
import jax.numpy as jnp
from jax import lax
from jax.experimental import pallas as pl
from jax.experimental.pallas import tpu as pltpu
from jax.sharding import PartitionSpec as P

F32 = jnp.float32
BF16 = jnp.bfloat16
SIDE = 4
CORES = 2
MOST = 24
BLK = SIDE * MOST
STEPS = ((1, 0), (3, 0), (0, 1), (1, 1), (2, 0), (2, 1), (3, 1), (0, 0))
NB = len(STEPS)
SLOTS = NB * BLK
GROUP = 4


def place(x, y, c):
    return (x * SIDE + y) * CORES + c


def route(hops, flip, first):
    pairs = []
    for x in range(SIDE):
        for y in range(SIDE):
            for c in range(CORES):
                if (c == 0) == first:
                    to = place((x + hops) % SIDE, y, c ^ flip)
                else:
                    to = place(x, (y + hops) % SIDE, c ^ flip)
                pairs.append((place(x, y, c), to))
    return pairs


def hop(a, hops, flip, first, back=False):
    pairs = route(hops, flip, first)
    if back:
        pairs = [(t, s) for s, t in pairs]
    return lax.ppermute(a, "expert", pairs)


VM = pl.BlockSpec(memory_space=pltpu.VMEM)
SM = pl.BlockSpec(memory_space=pltpu.SMEM)
HBM = pl.BlockSpec(memory_space=pltpu.HBM)


def params(mib=28):
    return pltpu.CompilerParams(vmem_limit_bytes=mib * 2**20)


def cost(flops, nbytes):
    return pl.CostEstimate(flops=int(flops), bytes_accessed=int(nbytes), transcendentals=0)


def gather(blocks, rows):
    at = 0
    for b in blocks:
        rows[at : at + b.shape[0], :] = b[...]
        at += b.shape[0]


def pack_kernel(tok, ids, probs, out, got, pad, sems):
    n = tok.shape[0]
    top = ids.shape[0]
    copies = [
        pltpu.make_async_copy(tok, out.at[0:n, :], sems.at[0]),
        pltpu.make_async_copy(ids, got.at[0], sems.at[1]),
    ]
    copies.append(pltpu.make_async_copy(probs, pad.at[1], sems.at[2]))
    for c in copies:
        c.start()
    out[n:, :] = jnp.zeros((16, out.shape[1]), BF16)
    pad[0] = jnp.zeros(pad.shape[1:], F32)
    for c in copies[1:]:
        c.wait()
    pad[0] = got[0].astype(F32)
    zero = jnp.zeros((16 - top, n), F32)
    out[n:, 0:n] = jnp.concatenate([pad[0], zero], axis=0).astype(BF16)
    rest = jnp.concatenate([pad[1], zero], axis=0)
    for i in (1, 2, 3):
        term = rest.astype(BF16)
        out[n:, i * 128 : i * 128 + n] = term
        rest = rest - term.astype(F32)
    copies[0].wait()


def pack(tok, ids, probs):
    n, d = tok.shape
    top = ids.shape[1]
    return pl.pallas_call(
        pack_kernel,
        out_shape=jax.ShapeDtypeStruct((n + 16, d), BF16),
        in_specs=[HBM] * 3,
        out_specs=VM,
        scratch_shapes=[
            pltpu.VMEM((1, top, n), jnp.int32),
            pltpu.VMEM((2, top, n), F32),
            pltpu.SemaphoreType.DMA((3,)),
        ],
        compiler_params=params(),
        cost_estimate=cost(0, 4 * n * d),
        name="pack",
    )(tok, ids.T, probs.T)


def experts(here):
    e = here[0]
    c, y, x = lax.rem(e, CORES), lax.rem(lax.div(e, CORES), SIDE), lax.div(e, CORES * SIDE)
    found = []
    for hops, flip in STEPS:
        one = place(x, lax.rem(y + hops, SIDE), flip)
        two = place(lax.rem(x + hops, SIDE), y, 1 - flip)
        found.append(jnp.where(c == 0, one, two).astype(F32))
    return found


def slots(ex, metas, n):
    total = SIDE * n

    def along(lo):
        parts = [metas[j, :, lo : lo + 128].astype(F32) for j in range(SIDE)]
        low = lax.broadcasted_iota(jnp.int32, parts[0].shape, 1) < n
        pairs = [jnp.where(low, parts[j], pltpu.roll(parts[j + 1], n, 1)) for j in (0, 2)]
        return jnp.concatenate(pairs, axis=1)[0:8, :]

    ids = along(0)
    probs = (along(128) + along(256)) + along(384)
    hits, weights = [], []
    for i in range(NB):
        eq = ids == ex[i]
        hits.append(jnp.max(jnp.where(eq, 1.0, 0.0), axis=0, keepdims=True))
        weights.append(jnp.sum(jnp.where(eq, probs, 0.0), axis=0, keepdims=True))
    hit = jnp.concatenate(hits, axis=0)
    s_at = lax.broadcasted_iota(jnp.int32, (total, total), 0)
    t_at = lax.broadcasted_iota(jnp.int32, (total, total), 1)
    before = jnp.where((s_at < t_at) & (s_at // n == t_at // n), 1.0, 0.0).astype(BF16)
    rank = jnp.dot(hit.astype(BF16), before, preferred_element_type=F32)
    group = (lax.broadcasted_iota(jnp.int32, (NB, total), 1) // n).astype(F32)
    return jnp.where(hit > 0.0, rank + MOST * group, -1.0), weights


def select_kernel(scaled, here, *refs):
    packed, refs = refs[:SIDE], refs[SIDE:]
    if scaled:
        grads, refs = refs[:SIDE], refs[SIDE:]
        outs, (sel_t, rows, metas, sel) = refs[:NB], refs[NB:]
    else:
        outs, (rows, metas, sel) = refs[:NB], refs[NB:]
    n = rows.shape[0] // SIDE
    d = rows.shape[1]
    total = SIDE * n
    for j in range(SIDE):
        metas[j] = packed[j][n:, 0 : metas.shape[2]]
        rows[j * n : (j + 1) * n, :] = grads[j][...] if scaled else packed[j][0:n, :]
    slot, weights = slots(experts(here), metas, n)
    at = lax.broadcasted_iota(jnp.int32, (BLK, total), 0).astype(F32)
    scale = []
    for i in range(NB):
        one = at == slot[i : i + 1, :]
        sel[i * BLK : (i + 1) * BLK, :] = jnp.where(one, 1.0, 0.0).astype(BF16)
        if scaled:
            scale.append(jnp.sum(jnp.where(one, weights[i], 0.0), axis=1, keepdims=True))
    width = 512
    for k in range(d // width):
        cols = slice(k * width, (k + 1) * width)
        got = jnp.dot(sel[...], rows[:, cols], preferred_element_type=F32)
        for i in range(NB):
            part = got[i * BLK : (i + 1) * BLK, :]
            if scaled:
                part = part * scale[i]
            outs[i][:, cols] = part.astype(BF16)
    if scaled:
        sel_t[...] = jnp.transpose(sel[...].astype(F32)).astype(BF16)


def select(here, packed, grads=()):
    scaled = len(grads) > 0
    n, d = packed[0].shape[0] - 16, packed[0].shape[1]
    total = SIDE * n
    out = [jax.ShapeDtypeStruct((BLK, d), BF16)] * NB
    if scaled:
        out = out + [jax.ShapeDtypeStruct((total, SLOTS), BF16)]
    return pl.pallas_call(
        lambda *refs: select_kernel(scaled, *refs),
        out_shape=out,
        in_specs=[SM] + [VM] * (SIDE + len(grads)),
        out_specs=[VM] * len(out),
        scratch_shapes=[
            pltpu.VMEM((total, d), BF16),
            pltpu.VMEM((SIDE, 16, 512), BF16),
            pltpu.VMEM((SLOTS, total), BF16),
        ],
        compiler_params=params(),
        cost_estimate=cost(2 * SLOTS * total * d, 2 * d * (SLOTS + total)),
        name="select_g" if scaled else "select_x",
    )(here, *packed, *grads)


def weights_kernel(per, gs, ds, gu, dn, w_gu, w_dn):
    side = gu.shape[0] // per
    step = pl.program_id(0)
    for i in range(per):
        at = slice(i * side, (i + 1) * side)
        for codes, scales, out in ((gu, gs, w_gu), (dn, ds, w_dn)):
            for j in range(codes.shape[1] // side):
                cols = slice(j * side, (j + 1) * side)
                scale = scales[j, 0, step * per + i]
                out[at, cols] = (codes[at, cols].astype(F32) * scale).astype(BF16)


def weights(gu, dn, gs, ds):
    d, f2 = gu.shape
    f = dn.shape[1]
    nblk = gs.shape[1]
    per = 2
    side = d // nblk * per
    blocks = [pl.BlockSpec((side, f2), lambda i: (i, 0)), pl.BlockSpec((side, f), lambda i: (i, 0))]
    return pl.pallas_call(
        lambda *refs: weights_kernel(per, *refs),
        grid=(nblk // per,),
        out_shape=[jax.ShapeDtypeStruct((d, f2), BF16), jax.ShapeDtypeStruct((d, f), BF16)],
        in_specs=[SM] * 2 + blocks,
        out_specs=blocks,
        compiler_params=params(),
        cost_estimate=cost(d * f2 * 6, 4 * d * (f2 + f)),
        name="weights",
    )(gs.transpose(2, 0, 1), ds.transpose(2, 0, 1), gu, dn)


def forward_kernel(*refs):
    xs, (w_gu, hid_t, upslope, act, rows) = refs[:NB], refs[NB:]
    f = hid_t.shape[0]
    width = 256
    gather(xs, rows)
    for k in range(f // width):
        lo, hi = k * width, (k + 1) * width
        gate = jnp.dot(rows[...], w_gu[:, lo:hi], preferred_element_type=F32)
        up = jnp.dot(rows[...], w_gu[:, f + lo : f + hi], preferred_element_type=F32)
        s = jax.nn.sigmoid(gate)
        a = gate * s
        act[:, lo:hi] = a
        upslope[:, lo:hi] = up * (s * (1.0 + gate * (1.0 - s)))
        hid_t[lo:hi, :] = jnp.transpose(a * up).astype(BF16)


def forward(xs, w_gu):
    d, f2 = w_gu.shape
    f = f2 // 2
    return pl.pallas_call(
        forward_kernel,
        out_shape=[
            jax.ShapeDtypeStruct((f, SLOTS), BF16),
            jax.ShapeDtypeStruct((SLOTS, f), F32),
            jax.ShapeDtypeStruct((SLOTS, f), F32),
        ],
        in_specs=[VM] * (NB + 1),
        out_specs=[VM] * 3,
        scratch_shapes=[pltpu.VMEM((SLOTS, d), BF16)],
        compiler_params=params(),
        cost_estimate=cost(2 * SLOTS * d * f2, 2 * d * (SLOTS + f2) + 10 * SLOTS * f),
        name="forward",
    )(*xs, w_gu)


def ring_kernel(stage, by, owners, here, *refs):
    gs, hid_t, refs = refs[:NB], refs[NB], refs[NB + 1 :]
    arrived = () if stage == 0 else refs[:2]
    refs = refs[len(arrived) :]
    outs, rows = refs[:-1], refs[-1]
    f, width = hid_t.shape[0], rows.shape[2]
    half = f // 2
    for k, steps in enumerate(by):
        cols = pl.ds(pl.multiple_of(lax.rem(here[1] + steps, owners) * width, width), width)
        for i in range(NB):
            rows[k, i * BLK : (i + 1) * BLK, :] = gs[i][:, cols]
        got = jnp.dot(hid_t[...], rows[k], preferred_element_type=F32)
        if stage == 0:
            outs[0][...] = got[:half, :].astype(BF16)
            outs[1][...] = got[half:, :].astype(BF16)
        elif stage == 1:
            mine = slice(k * half, (k + 1) * half)
            rest = slice((1 - k) * half, (2 - k) * half)
            outs[k][mine, :] = (got[mine, :] + arrived[k][...].astype(F32)).astype(BF16)
            outs[k][rest, :] = got[rest, :].astype(BF16)
        elif stage < 4:
            outs[k][...] = (got + arrived[k][...].astype(F32)).astype(BF16)
        else:
            total = got + arrived[0][...].astype(F32) + arrived[1][...].astype(F32)
            outs[0][...] = jnp.transpose(total)


def ring(stage, by, here, gs, hid_t, arrived, owners):
    f = hid_t.shape[0]
    count = len(by)
    width = gs[0].shape[1] // owners
    if stage == 0:
        out = [jax.ShapeDtypeStruct((f // 2, width), BF16)] * 2
    elif stage < 4:
        out = [jax.ShapeDtypeStruct((f, width), BF16)] * 2
    else:
        out = [jax.ShapeDtypeStruct((width, f), F32)]
    return pl.pallas_call(
        lambda *refs: ring_kernel(stage, by, owners, *refs),
        out_shape=out,
        in_specs=[SM] + [VM] * (NB + 1 + len(arrived)),
        out_specs=[VM] * len(out),
        scratch_shapes=[pltpu.VMEM((count, SLOTS, width), BF16)],
        compiler_params=params(),
        cost_estimate=cost(2 * SLOTS * width * f * count, 2 * SLOTS * f + 4 * count * f * width),
        name="ring",
    )(here, *gs, hid_t, *arrived)


def zhop(a, by):
    n = lax.axis_size("dp")
    return lax.ppermute(a, "dp", [(i, (i + by) % n) for i in range(n)])


def back_kernel(at, *refs):
    gs, refs = refs[:GROUP], refs[GROUP:]
    (w_dn, upslope, act, w_gu), refs = refs[:4], refs[4:]
    outs, (rows, dp) = refs[:GROUP], refs[GROUP:]
    count = GROUP * BLK
    d, f = w_dn.shape
    mine = slice(at * count, (at + 1) * count)
    gather(gs, rows)
    fw, dw = 256, 512
    for k in range(f // fw):
        lo, hi = k * fw, (k + 1) * fw
        dh = jnp.dot(rows[...], w_dn[:, lo:hi], preferred_element_type=F32)
        dp[:, lo:hi] = (dh * upslope[mine, lo:hi]).astype(BF16)
        dp[:, f + lo : f + hi] = (dh * act[mine, lo:hi]).astype(BF16)
    for k in range(d // dw):
        cols = slice(k * dw, (k + 1) * dw)
        got = lax.dot_general(
            dp[...], w_gu[cols, :], (((1,), (1,)), ((), ())), preferred_element_type=F32
        )
        for i in range(GROUP):
            outs[i][:, cols] = got[i * BLK : (i + 1) * BLK, :].astype(BF16)


def back(gs, w_dn, upslope, act, w_gu, at):
    d, f = w_dn.shape
    rows = GROUP * BLK
    return pl.pallas_call(
        lambda *refs: back_kernel(at, *refs),
        out_shape=[jax.ShapeDtypeStruct((BLK, d), BF16)] * GROUP,
        in_specs=[VM] * (GROUP + 4),
        out_specs=[VM] * GROUP,
        scratch_shapes=[pltpu.VMEM((rows, d), BF16), pltpu.VMEM((rows, 2 * f), BF16)],
        compiler_params=params(),
        cost_estimate=cost(6 * rows * d * f, 2 * d * (2 * rows + 3 * f) + 8 * rows * f),
        name="back",
    )(*gs, w_dn, upslope, act, w_gu)


def combine_kernel(sel_t, *refs):
    ret, refs = refs[:NB], refs[NB:]
    outs, rows = refs[:SIDE], refs[SIDE]
    n, d = outs[0].shape
    gather(ret, rows)
    width = 512
    for k in range(d // width):
        cols = slice(k * width, (k + 1) * width)
        got = jnp.dot(sel_t[...], rows[:, cols], preferred_element_type=F32)
        outs[0][:, cols] = got[0:n, :]
        for j in range(1, SIDE):
            outs[j][:, cols] = got[j * n : (j + 1) * n, :].astype(BF16)


def combine(sel_t, ret):
    total = sel_t.shape[0]
    n = total // SIDE
    d = ret[0].shape[1]
    return pl.pallas_call(
        combine_kernel,
        out_shape=[jax.ShapeDtypeStruct((n, d), F32)]
        + [jax.ShapeDtypeStruct((n, d), BF16)] * (SIDE - 1),
        in_specs=[VM] * (NB + 1),
        out_specs=[VM] * SIDE,
        scratch_shapes=[pltpu.VMEM((SLOTS, d), BF16)],
        compiler_params=params(),
        cost_estimate=cost(2 * SLOTS * d * total, 2 * d * (SLOTS + 2 * total)),
        name="combine",
    )(sel_t, *ret)


def on_device(tokens, out_grad, expert_ids, gate_probs, gu_codes, gu_scales, down_codes, down_scales):
    owners = lax.axis_size("dp")
    here = jnp.stack([lax.axis_index("expert"), lax.axis_index("dp")]).astype(jnp.int32)
    tokens, here = lax.optimization_barrier((tokens, here))

    mine = pack(tokens, expert_ids, gate_probs)
    packed = [mine] + [hop(mine, j, 0, True) for j in (2, 1, 3)]
    grads = [out_grad] + [hop(out_grad, j, 0, True) for j in (2, 1, 3)]
    w = weights(gu_codes[0], down_codes[0], gu_scales, down_scales)
    packed, (w_gu, w_dn) = lax.optimization_barrier((packed, w))

    xs = select(here, packed)
    xs, grads = lax.optimization_barrier((xs, grads))
    xs = [hop(a, h, f, False) if (h or f) else a for a, (h, f) in zip(xs, STEPS)]
    *gs, sel_t = select(here, packed, grads)
    gs = [hop(a, h, f, False) if (h or f) else a for a, (h, f) in zip(gs, STEPS)]

    hid_t, upslope, act = forward(xs, w_gu)

    late = back(gs[GROUP:], w_dn, upslope, act, w_gu, 1)
    near, hid_t, late = lax.optimization_barrier((gs[:GROUP], hid_t, late))
    gs = near + gs[GROUP:]

    arrived, sums = [], None
    stages = ((4,), (3, 5), (2, 6), (1, 7), (0,))
    ret = None
    for stage, by in enumerate(stages):
        sums = ring(stage, by, here, gs, hid_t, arrived, owners)
        if stage < 4:
            arrived = [zhop(sums[0], 1), zhop(sums[1], owners - 1)]
        if stage == 0:
            ret = back(near, w_dn, upslope, act, w_gu, 0) + late
            ret = [hop(a, h, f, False, True) if (h or f) else a for a, (h, f) in zip(ret, STEPS)]
    down_grad = sums[0]

    own, *others = combine(sel_t, ret)
    others = [hop(a, j, 0, True, True) for j, a in zip((2, 1, 3), others)]
    token_grad = own
    for a in others:
        token_grad = token_grad + a.astype(F32)
    return token_grad.astype(BF16), down_grad[None]


def solution(mesh):
    rows = P(("expert", "dp"), None)
    per = P("expert", None, None)
    return jax.shard_map(
        on_device,
        mesh=mesh,
        in_specs=(rows, rows, rows, rows, per, per, per, per),
        out_specs=(rows, P("expert", "dp", None)),
        check_vma=False,
    )
```

```python
import jax
import jax.numpy as jnp
from jax import lax
from jax.experimental import pallas as pl
from jax.experimental.pallas import tpu as pltpu
from jax.sharding import PartitionSpec as P

F32 = jnp.float32
BF16 = jnp.bfloat16
SIDE = 4
CORES = 2
MOST = 24
BLK = SIDE * MOST
STEPS = ((1, 0), (3, 0), (0, 1), (1, 1), (2, 0), (2, 1), (3, 1), (0, 0))
NB = len(STEPS)
SLOTS = NB * BLK
GROUP = 4


def place(x, y, c):
    return (x * SIDE + y) * CORES + c


def route(hops, flip, first):
    pairs = []
    for x in range(SIDE):
        for y in range(SIDE):
            for c in range(CORES):
                if (c == 0) == first:
                    to = place((x + hops) % SIDE, y, c ^ flip)
                else:
                    to = place(x, (y + hops) % SIDE, c ^ flip)
                pairs.append((place(x, y, c), to))
    return pairs


def hop(a, hops, flip, first, back=False):
    pairs = route(hops, flip, first)
    if back:
        pairs = [(t, s) for s, t in pairs]
    return lax.ppermute(a, "expert", pairs)


VM = pl.BlockSpec(memory_space=pltpu.VMEM)
SM = pl.BlockSpec(memory_space=pltpu.SMEM)
HBM = pl.BlockSpec(memory_space=pltpu.HBM)


def params(mib=28):
    return pltpu.CompilerParams(vmem_limit_bytes=mib * 2**20)


def cost(flops, nbytes):
    return pl.CostEstimate(flops=int(flops), bytes_accessed=int(nbytes), transcendentals=0)


def gather(blocks, rows):
    at = 0
    for b in blocks:
        rows[at : at + b.shape[0], :] = b[...]
        at += b.shape[0]


def pack_kernel(tok, ids, probs, out, got, pad, sems):
    n = tok.shape[0]
    top = ids.shape[0]
    copies = [
        pltpu.make_async_copy(tok, out.at[0:n, :], sems.at[0]),
        pltpu.make_async_copy(ids, got.at[0], sems.at[1]),
    ]
    copies.append(pltpu.make_async_copy(probs, pad.at[1], sems.at[2]))
    for c in copies:
        c.start()
    out[n:, :] = jnp.zeros((16, out.shape[1]), BF16)
    pad[0] = jnp.zeros(pad.shape[1:], F32)
    for c in copies[1:]:
        c.wait()
    pad[0] = got[0].astype(F32)
    zero = jnp.zeros((16 - top, n), F32)
    out[n:, 0:n] = jnp.concatenate([pad[0], zero], axis=0).astype(BF16)
    rest = jnp.concatenate([pad[1], zero], axis=0)
    for i in (1, 2, 3):
        term = rest.astype(BF16)
        out[n:, i * 128 : i * 128 + n] = term
        rest = rest - term.astype(F32)
    copies[0].wait()


def pack(tok, ids, probs):
    n, d = tok.shape
    top = ids.shape[1]
    return pl.pallas_call(
        pack_kernel,
        out_shape=jax.ShapeDtypeStruct((n + 16, d), BF16),
        in_specs=[HBM] * 3,
        out_specs=VM,
        scratch_shapes=[
            pltpu.VMEM((1, top, n), jnp.int32),
            pltpu.VMEM((2, top, n), F32),
            pltpu.SemaphoreType.DMA((3,)),
        ],
        compiler_params=params(56),
        cost_estimate=cost(0, 4 * n * d),
        name="pack",
    )(tok, ids.T, probs.T)


def experts(here):
    e = here[0]
    c, y, x = lax.rem(e, CORES), lax.rem(lax.div(e, CORES), SIDE), lax.div(e, CORES * SIDE)
    found = []
    for hops, flip in STEPS:
        one = place(x, lax.rem(y + hops, SIDE), flip)
        two = place(lax.rem(x + hops, SIDE), y, 1 - flip)
        found.append(jnp.where(c == 0, one, two).astype(F32))
    return found


def slots(ex, metas, n):
    total = SIDE * n

    def along(lo):
        parts = [metas[j, :, lo : lo + 128].astype(F32) for j in range(SIDE)]
        low = lax.broadcasted_iota(jnp.int32, parts[0].shape, 1) < n
        pairs = [jnp.where(low, parts[j], pltpu.roll(parts[j + 1], n, 1)) for j in (0, 2)]
        return jnp.concatenate(pairs, axis=1)[0:8, :]

    ids = along(0)
    probs = (along(128) + along(256)) + along(384)
    hits, weights = [], []
    for i in range(NB):
        eq = ids == ex[i]
        hits.append(jnp.max(jnp.where(eq, 1.0, 0.0), axis=0, keepdims=True))
        weights.append(jnp.sum(jnp.where(eq, probs, 0.0), axis=0, keepdims=True))
    hit = jnp.concatenate(hits, axis=0)
    s_at = lax.broadcasted_iota(jnp.int32, (total, total), 0)
    t_at = lax.broadcasted_iota(jnp.int32, (total, total), 1)
    before = jnp.where((s_at < t_at) & (s_at // n == t_at // n), 1.0, 0.0).astype(BF16)
    rank = jnp.dot(hit.astype(BF16), before, preferred_element_type=F32)
    group = (lax.broadcasted_iota(jnp.int32, (NB, total), 1) // n).astype(F32)
    return jnp.where(hit > 0.0, rank + MOST * group, -1.0), weights


def select_kernel(scaled, here, *refs):
    packed, refs = refs[:SIDE], refs[SIDE:]
    if scaled:
        grads, refs = refs[:SIDE], refs[SIDE:]
        outs, (sel_t, rows, metas, sel) = refs[:NB], refs[NB:]
    else:
        outs, (rows, metas, sel) = refs[:NB], refs[NB:]
    n = rows.shape[0] // SIDE
    d = rows.shape[1]
    total = SIDE * n
    for j in range(SIDE):
        metas[j] = packed[j][n:, 0 : metas.shape[2]]
        rows[j * n : (j + 1) * n, :] = grads[j][...] if scaled else packed[j][0:n, :]
    slot, weights = slots(experts(here), metas, n)
    at = lax.broadcasted_iota(jnp.int32, (BLK, total), 0).astype(F32)
    scale = []
    for i in range(NB):
        one = at == slot[i : i + 1, :]
        sel[i * BLK : (i + 1) * BLK, :] = jnp.where(one, 1.0, 0.0).astype(BF16)
        if scaled:
            scale.append(jnp.sum(jnp.where(one, weights[i], 0.0), axis=1, keepdims=True))
    width = 512
    for k in range(d // width):
        cols = slice(k * width, (k + 1) * width)
        got = jnp.dot(sel[...], rows[:, cols], preferred_element_type=F32)
        for i in range(NB):
            part = got[i * BLK : (i + 1) * BLK, :]
            if scaled:
                part = part * scale[i]
            outs[i][:, cols] = part.astype(BF16)
    if scaled:
        sel_t[...] = jnp.transpose(sel[...].astype(F32)).astype(BF16)


def select(here, packed, grads=()):
    scaled = len(grads) > 0
    n, d = packed[0].shape[0] - 16, packed[0].shape[1]
    total = SIDE * n
    out = [jax.ShapeDtypeStruct((BLK, d), BF16)] * NB
    if scaled:
        out = out + [jax.ShapeDtypeStruct((total, SLOTS), BF16)]
    return pl.pallas_call(
        lambda *refs: select_kernel(scaled, *refs),
        out_shape=out,
        in_specs=[SM] + [VM] * (SIDE + len(grads)),
        out_specs=[VM] * len(out),
        scratch_shapes=[
            pltpu.VMEM((total, d), BF16),
            pltpu.VMEM((SIDE, 16, 512), BF16),
            pltpu.VMEM((SLOTS, total), BF16),
        ],
        compiler_params=params(),
        cost_estimate=cost(2 * SLOTS * total * d, 2 * d * (SLOTS + total)),
        name="select_g" if scaled else "select_x",
    )(here, *packed, *grads)


def weights_kernel(per, gs, ds, gu, dn, w_gu, w_dn):
    side = gu.shape[0] // per
    step = pl.program_id(0)
    for i in range(per):
        at = slice(i * side, (i + 1) * side)
        for codes, scales, out in ((gu, gs, w_gu), (dn, ds, w_dn)):
            for j in range(codes.shape[1] // side):
                cols = slice(j * side, (j + 1) * side)
                scale = scales[j, 0, step * per + i]
                out[at, cols] = (codes[at, cols].astype(F32) * scale).astype(BF16)


def weights(gu, dn, gs, ds):
    d, f2 = gu.shape
    f = dn.shape[1]
    nblk = gs.shape[1]
    per = 2
    side = d // nblk * per
    blocks = [pl.BlockSpec((side, f2), lambda i: (i, 0)), pl.BlockSpec((side, f), lambda i: (i, 0))]
    return pl.pallas_call(
        lambda *refs: weights_kernel(per, *refs),
        grid=(nblk // per,),
        out_shape=[jax.ShapeDtypeStruct((d, f2), BF16), jax.ShapeDtypeStruct((d, f), BF16)],
        in_specs=[SM] * 2 + blocks,
        out_specs=blocks,
        compiler_params=params(),
        cost_estimate=cost(d * f2 * 6, 4 * d * (f2 + f)),
        name="weights",
    )(gs.transpose(2, 0, 1), ds.transpose(2, 0, 1), gu, dn)


def forward_kernel(*refs):
    xs, (w_gu, hid_t, upslope, act, rows) = refs[:NB], refs[NB:]
    f = hid_t.shape[0]
    width = 256
    gather(xs, rows)
    for k in range(f // width):
        lo, hi = k * width, (k + 1) * width
        gate = jnp.dot(rows[...], w_gu[:, lo:hi], preferred_element_type=F32)
        up = jnp.dot(rows[...], w_gu[:, f + lo : f + hi], preferred_element_type=F32)
        s = jax.nn.sigmoid(gate)
        a = gate * s
        act[:, lo:hi] = a
        upslope[:, lo:hi] = up * (s * (1.0 + gate * (1.0 - s)))
        hid_t[lo:hi, :] = jnp.transpose(a * up).astype(BF16)


def forward(xs, w_gu):
    d, f2 = w_gu.shape
    f = f2 // 2
    return pl.pallas_call(
        forward_kernel,
        out_shape=[
            jax.ShapeDtypeStruct((f, SLOTS), BF16),
            jax.ShapeDtypeStruct((SLOTS, f), F32),
            jax.ShapeDtypeStruct((SLOTS, f), F32),
        ],
        in_specs=[VM] * (NB + 1),
        out_specs=[VM] * 3,
        scratch_shapes=[pltpu.VMEM((SLOTS, d), BF16)],
        compiler_params=params(),
        cost_estimate=cost(2 * SLOTS * d * f2, 2 * d * (SLOTS + f2) + 10 * SLOTS * f),
        name="forward",
    )(*xs, w_gu)


def ring_kernel(by, owners, here, *refs):
    gs, hid_t, refs = refs[:NB], refs[NB], refs[NB + 1 :]
    arrived, out, rows = refs[:-2], refs[-2], refs[-1]
    width = rows.shape[1]
    cols = pl.ds(pl.multiple_of(lax.rem(here[1] + by, owners) * width, width), width)
    for i in range(NB):
        rows[i * BLK : (i + 1) * BLK, :] = gs[i][:, cols]
    f = hid_t.shape[0]
    half = f // 2
    got = jnp.dot(hid_t[...], rows[...], preferred_element_type=F32)
    if len(arrived) == 2:
        got = got + arrived[0][...].astype(F32) + arrived[1][...].astype(F32)
        out[...] = jnp.transpose(got)
    elif arrived[0].shape[0] < f:
        mine, rest = slice(0, half), slice(half, f)
        if 2 * by > owners:
            mine, rest = rest, mine
        out[mine, :] = (got[mine, :] + arrived[0][...].astype(F32)).astype(BF16)
        out[rest, :] = got[rest, :].astype(BF16)
    else:
        out[...] = (got + arrived[0][...].astype(F32)).astype(BF16)


def ring_first_kernel(part, owners, here, *refs):
    gs, hid_t, out, rows = refs[:NB], refs[NB], refs[NB + 1], refs[NB + 2]
    width = rows.shape[1]
    cols = pl.ds(pl.multiple_of(lax.rem(here[1] + owners // 2, owners) * width, width), width)
    for i in range(NB):
        rows[i * BLK : (i + 1) * BLK, :] = gs[i][:, cols]
    n = out.shape[0]
    mine = hid_t[part * n : (part + 1) * n, :]
    out[...] = jnp.dot(mine, rows[...], preferred_element_type=F32).astype(BF16)


def ring(by, part, here, gs, hid_t, arrived, owners):
    f = hid_t.shape[0]
    width = gs[0].shape[1] // owners
    if not arrived:
        out = jax.ShapeDtypeStruct((f // 2, width), BF16)
        kernel = lambda *refs: ring_first_kernel(part, owners, *refs)
    else:
        kernel = lambda *refs: ring_kernel(by, owners, *refs)
        last = len(arrived) == 2
        out = jax.ShapeDtypeStruct((width, f) if last else (f, width), F32 if last else BF16)
    return pl.pallas_call(
        kernel,
        out_shape=out,
        in_specs=[SM] + [VM] * (NB + 1 + len(arrived)),
        out_specs=VM,
        scratch_shapes=[pltpu.VMEM((SLOTS, width), BF16)],
        compiler_params=params(),
        cost_estimate=cost(2 * SLOTS * width * f, 2 * SLOTS * (f + width) + 4 * f * width),
        name="ring",
    )(here, *gs, hid_t, *arrived)


def zhop(a, by):
    n = lax.axis_size("dp")
    return lax.ppermute(a, "dp", [(i, (i + by) % n) for i in range(n)])


def back_kernel(at, *refs):
    gs, refs = refs[:GROUP], refs[GROUP:]
    (w_dn, upslope, act, w_gu), refs = refs[:4], refs[4:]
    outs, (rows, dp) = refs[:GROUP], refs[GROUP:]
    count = GROUP * BLK
    d, f = w_dn.shape
    mine = slice(at * count, (at + 1) * count)
    gather(gs, rows)
    fw, dw = 256, 512
    for k in range(f // fw):
        lo, hi = k * fw, (k + 1) * fw
        dh = jnp.dot(rows[...], w_dn[:, lo:hi], preferred_element_type=F32)
        dp[:, lo:hi] = (dh * upslope[mine, lo:hi]).astype(BF16)
        dp[:, f + lo : f + hi] = (dh * act[mine, lo:hi]).astype(BF16)
    for k in range(d // dw):
        cols = slice(k * dw, (k + 1) * dw)
        got = lax.dot_general(
            dp[...], w_gu[cols, :], (((1,), (1,)), ((), ())), preferred_element_type=F32
        )
        for i in range(GROUP):
            outs[i][:, cols] = got[i * BLK : (i + 1) * BLK, :].astype(BF16)


def back(gs, w_dn, upslope, act, w_gu, at):
    d, f = w_dn.shape
    rows = GROUP * BLK
    return pl.pallas_call(
        lambda *refs: back_kernel(at, *refs),
        out_shape=[jax.ShapeDtypeStruct((BLK, d), BF16)] * GROUP,
        in_specs=[VM] * (GROUP + 4),
        out_specs=[VM] * GROUP,
        scratch_shapes=[pltpu.VMEM((rows, d), BF16), pltpu.VMEM((rows, 2 * f), BF16)],
        compiler_params=params(),
        cost_estimate=cost(6 * rows * d * f, 2 * d * (2 * rows + 3 * f) + 8 * rows * f),
        name="back",
    )(*gs, w_dn, upslope, act, w_gu)


def combine_kernel(sel_t, *refs):
    ret, refs = refs[:NB], refs[NB:]
    outs, rows = refs[:SIDE], refs[SIDE]
    n, d = outs[0].shape
    gather(ret, rows)
    width = 512
    for k in range(d // width):
        cols = slice(k * width, (k + 1) * width)
        got = jnp.dot(sel_t[...], rows[:, cols], preferred_element_type=F32)
        outs[0][:, cols] = got[0:n, :]
        for j in range(1, SIDE):
            outs[j][:, cols] = got[j * n : (j + 1) * n, :].astype(BF16)


def combine(sel_t, ret):
    total = sel_t.shape[0]
    n = total // SIDE
    d = ret[0].shape[1]
    return pl.pallas_call(
        combine_kernel,
        out_shape=[jax.ShapeDtypeStruct((n, d), F32)]
        + [jax.ShapeDtypeStruct((n, d), BF16)] * (SIDE - 1),
        in_specs=[VM] * (NB + 1),
        out_specs=[VM] * SIDE,
        scratch_shapes=[pltpu.VMEM((SLOTS, d), BF16)],
        compiler_params=params(),
        cost_estimate=cost(2 * SLOTS * d * total, 2 * d * (SLOTS + 2 * total)),
        name="combine",
    )(sel_t, *ret)


def on_device(tokens, out_grad, expert_ids, gate_probs, gu_codes, gu_scales, down_codes, down_scales):
    owners = lax.axis_size("dp")
    here = jnp.stack([lax.axis_index("expert"), lax.axis_index("dp")]).astype(jnp.int32)
    tokens, here = lax.optimization_barrier((tokens, here))

    mine = pack(tokens, expert_ids, gate_probs)
    packed = [mine] + [hop(mine, j, 0, True) for j in (2, 1, 3)]
    grads = [out_grad] + [hop(out_grad, j, 0, True) for j in (2, 1, 3)]
    xs = select(here, packed)
    xs, codes = lax.optimization_barrier((xs, (gu_codes, down_codes)))
    xs = [hop(a, h, f, False) if (h or f) else a for a, (h, f) in zip(xs, STEPS)]
    *gs, sel_t = select(here, packed, grads)
    w_gu, w_dn = weights(codes[0][0], codes[1][0], gu_scales, down_scales)

    hid_t, upslope, act = forward(xs, w_gu)

    near, hid_t = lax.optimization_barrier((gs[:GROUP], hid_t))
    gs = near + gs[GROUP:]
    gs = [hop(a, h, f, False) if (h or f) else a for a, (h, f) in zip(gs, STEPS)]
    late = back(gs[GROUP:], w_dn, upslope, act, w_gu, 1)
    near, hid_t, late = lax.optimization_barrier((gs[:GROUP], hid_t, late))
    gs = near + gs[GROUP:]

    right = left = ()
    for by in range(owners // 2, 0, -1):
        right = (zhop(ring(by, 0, here, gs, hid_t, right, owners), 1),)
        left = (zhop(ring(owners - by, 1, here, gs, hid_t, left, owners), owners - 1),)
    ret = back(near, w_dn, upslope, act, w_gu, 0) + late
    ret = [hop(a, h, f, False, True) if (h or f) else a for a, (h, f) in zip(ret, STEPS)]
    down_grad = ring(0, 0, here, gs, hid_t, right + left, owners)

    own, *others = combine(sel_t, ret)
    others = [hop(a, j, 0, True, True) for j, a in zip((2, 1, 3), others)]
    token_grad = own
    for a in others:
        token_grad = token_grad + a.astype(F32)
    return token_grad.astype(BF16), down_grad[None]


def solution(mesh):
    rows = P(("expert", "dp"), None)
    per = P("expert", None, None)
    return jax.shard_map(
        on_device,
        mesh=mesh,
        in_specs=(rows, rows, rows, rows, per, per, per, per),
        out_specs=(rows, P("expert", "dp", None)),
        check_vma=False,
    )
```

```python
import jax
import jax.numpy as jnp
from jax import lax
from jax.experimental import pallas as pl
from jax.experimental.pallas import tpu as pltpu
from jax.sharding import PartitionSpec as P

F32 = jnp.float32
BF16 = jnp.bfloat16
SIDE = 4
CORES = 2
MOST = 24
BLK = SIDE * MOST
STEPS = ((2, 1), (1, 1), (3, 1), (0, 1), (2, 0), (1, 0), (3, 0), (0, 0))
NB = len(STEPS)
SLOTS = NB * BLK
GROUP = 4


def place(x, y, c):
    return (x * SIDE + y) * CORES + c


def route(hops, flip, first):
    pairs = []
    for x in range(SIDE):
        for y in range(SIDE):
            for c in range(CORES):
                if (c == 0) == first:
                    to = place((x + hops) % SIDE, y, c ^ flip)
                else:
                    to = place(x, (y + hops) % SIDE, c ^ flip)
                pairs.append((place(x, y, c), to))
    return pairs


def hop(a, hops, flip, first, back=False):
    pairs = route(hops, flip, first)
    if back:
        pairs = [(t, s) for s, t in pairs]
    return lax.ppermute(a, "expert", pairs)


VM = pl.BlockSpec(memory_space=pltpu.VMEM)
SM = pl.BlockSpec(memory_space=pltpu.SMEM)
HBM = pl.BlockSpec(memory_space=pltpu.HBM)


def params(mib=28):
    return pltpu.CompilerParams(vmem_limit_bytes=mib * 2**20)


def cost(flops, nbytes):
    return pl.CostEstimate(flops=int(flops), bytes_accessed=int(nbytes), transcendentals=0)


def gather(blocks, rows):
    at = 0
    for b in blocks:
        rows[at : at + b.shape[0], :] = b[...]
        at += b.shape[0]


def pack_kernel(tok, grad, ids, probs, out, got, pad, sems):
    n = tok.shape[0]
    tail = slice(2 * n, 2 * n + 16)
    top = ids.shape[0]
    copies = [
        pltpu.make_async_copy(ids, got.at[0], sems.at[0]),
        pltpu.make_async_copy(probs, pad.at[1], sems.at[1]),
        pltpu.make_async_copy(tok, out.at[0:n, :], sems.at[2]),
        pltpu.make_async_copy(grad, out.at[n : 2 * n, :], sems.at[3]),
    ]
    for c in copies:
        c.start()
    out[tail, :] = jnp.zeros((16, out.shape[1]), BF16)
    pad[0] = jnp.zeros(pad.shape[1:], F32)
    for c in copies[:2]:
        c.wait()
    pad[0] = got[0].astype(F32)
    zero = jnp.zeros((16 - top, n), F32)
    out[tail, 0:n] = jnp.concatenate([pad[0], zero], axis=0).astype(BF16)
    rest = jnp.concatenate([pad[1], zero], axis=0)
    for i in (1, 2, 3):
        term = rest.astype(BF16)
        out[tail, i * 128 : i * 128 + n] = term
        rest = rest - term.astype(F32)
    for c in copies[2:]:
        c.wait()


def pack(tok, grad, ids, probs):
    n, d = tok.shape
    top = ids.shape[1]
    return pl.pallas_call(
        pack_kernel,
        out_shape=jax.ShapeDtypeStruct((2 * n + 16, d), BF16),
        in_specs=[HBM] * 4,
        out_specs=VM,
        scratch_shapes=[
            pltpu.VMEM((1, top, n), jnp.int32),
            pltpu.VMEM((2, top, n), F32),
            pltpu.SemaphoreType.DMA((4,)),
        ],
        compiler_params=params(56),
        cost_estimate=cost(0, 4 * n * d),
        name="pack",
    )(tok, grad, ids.T, probs.T)


def experts(here):
    e = here[0]
    c, y, x = lax.rem(e, CORES), lax.rem(lax.div(e, CORES), SIDE), lax.div(e, CORES * SIDE)
    found = []
    for hops, flip in STEPS:
        one = place(x, lax.rem(y + hops, SIDE), flip)
        two = place(lax.rem(x + hops, SIDE), y, 1 - flip)
        found.append(jnp.where(c == 0, one, two).astype(F32))
    return found


def slots(ex, metas, n):
    total = SIDE * n

    def along(lo):
        parts = [metas[j, :, lo : lo + 128].astype(F32) for j in range(SIDE)]
        low = lax.broadcasted_iota(jnp.int32, parts[0].shape, 1) < n
        pairs = [jnp.where(low, parts[j], pltpu.roll(parts[j + 1], n, 1)) for j in (0, 2)]
        return jnp.concatenate(pairs, axis=1)[0:8, :]

    ids = along(0)
    probs = (along(128) + along(256)) + along(384)
    hits, weights = [], []
    for i in range(NB):
        eq = ids == ex[i]
        hits.append(jnp.max(jnp.where(eq, 1.0, 0.0), axis=0, keepdims=True))
        weights.append(jnp.sum(jnp.where(eq, probs, 0.0), axis=0, keepdims=True))
    hit = jnp.concatenate(hits, axis=0)
    s_at = lax.broadcasted_iota(jnp.int32, (total, total), 0)
    t_at = lax.broadcasted_iota(jnp.int32, (total, total), 1)
    before = jnp.where((s_at < t_at) & (s_at // n == t_at // n), 1.0, 0.0).astype(BF16)
    rank = jnp.dot(hit.astype(BF16), before, preferred_element_type=F32)
    group = (lax.broadcasted_iota(jnp.int32, (NB, total), 1) // n).astype(F32)
    return jnp.where(hit > 0.0, rank + MOST * group, -1.0), weights


def select_kernel(scaled, here, *refs):
    packed, refs = refs[:SIDE], refs[SIDE:]
    if scaled:
        outs, (sel_t, rows, metas, sel) = refs[:NB], refs[NB:]
    else:
        outs, (rows, metas, sel) = refs[:NB], refs[NB:]
    n = rows.shape[0] // SIDE
    d = rows.shape[1]
    total = SIDE * n
    for j in range(SIDE):
        metas[j] = packed[j][2 * n :, 0 : metas.shape[2]]
        rows[j * n : (j + 1) * n, :] = packed[j][n : 2 * n, :] if scaled else packed[j][0:n, :]
    slot, weights = slots(experts(here), metas, n)
    at = lax.broadcasted_iota(jnp.int32, (BLK, total), 0).astype(F32)
    scale = []
    for i in range(NB):
        one = at == slot[i : i + 1, :]
        sel[i * BLK : (i + 1) * BLK, :] = jnp.where(one, 1.0, 0.0).astype(BF16)
        if scaled:
            scale.append(jnp.sum(jnp.where(one, weights[i], 0.0), axis=1, keepdims=True))
    width = 512
    for k in range(d // width):
        cols = slice(k * width, (k + 1) * width)
        got = jnp.dot(sel[...], rows[:, cols], preferred_element_type=F32)
        for i in range(NB):
            part = got[i * BLK : (i + 1) * BLK, :]
            if scaled:
                part = part * scale[i]
            outs[i][:, cols] = part.astype(BF16)
    if scaled:
        sel_t[...] = jnp.transpose(sel[...].astype(F32)).astype(BF16)


def select(scaled, here, packed):
    n, d = (packed[0].shape[0] - 16) // 2, packed[0].shape[1]
    total = SIDE * n
    out = [jax.ShapeDtypeStruct((BLK, d), BF16)] * NB
    if scaled:
        out = out + [jax.ShapeDtypeStruct((total, SLOTS), BF16)]
    return pl.pallas_call(
        lambda *refs: select_kernel(scaled, *refs),
        out_shape=out,
        in_specs=[SM] + [VM] * SIDE,
        out_specs=[VM] * len(out),
        scratch_shapes=[
            pltpu.VMEM((total, d), BF16),
            pltpu.VMEM((SIDE, 16, 512), BF16),
            pltpu.VMEM((SLOTS, total), BF16),
        ],
        compiler_params=params(),
        cost_estimate=cost(2 * SLOTS * total * d, 2 * d * (SLOTS + total)),
        name="select_g" if scaled else "select_x",
    )(here, *packed)


def weights_kernel(per, gs, ds, gu, dn, w_gu, w_dn):
    side = gu.shape[0] // per
    step = pl.program_id(0)
    for i in range(per):
        at = slice(i * side, (i + 1) * side)
        for codes, scales, out in ((gu, gs, w_gu), (dn, ds, w_dn)):
            for j in range(codes.shape[1] // side):
                cols = slice(j * side, (j + 1) * side)
                scale = scales[j, 0, step * per + i]
                out[at, cols] = (codes[at, cols].astype(F32) * scale).astype(BF16)


def weights(gu, dn, gs, ds):
    d, f2 = gu.shape
    f = dn.shape[1]
    nblk = gs.shape[1]
    per = 2
    side = d // nblk * per
    blocks = [pl.BlockSpec((side, f2), lambda i: (i, 0)), pl.BlockSpec((side, f), lambda i: (i, 0))]
    return pl.pallas_call(
        lambda *refs: weights_kernel(per, *refs),
        grid=(nblk // per,),
        out_shape=[jax.ShapeDtypeStruct((d, f2), BF16), jax.ShapeDtypeStruct((d, f), BF16)],
        in_specs=[SM] * 2 + blocks,
        out_specs=blocks,
        compiler_params=params(),
        cost_estimate=cost(d * f2 * 6, 4 * d * (f2 + f)),
        name="weights",
    )(gs.transpose(2, 0, 1), ds.transpose(2, 0, 1), gu, dn)


def forward_kernel(*refs):
    xs, (w_gu, hid_t, upslope, act, rows) = refs[:NB], refs[NB:]
    f = hid_t.shape[0]
    width = 256
    gather(xs, rows)
    for k in range(f // width):
        lo, hi = k * width, (k + 1) * width
        gate = jnp.dot(rows[...], w_gu[:, lo:hi], preferred_element_type=F32)
        up = jnp.dot(rows[...], w_gu[:, f + lo : f + hi], preferred_element_type=F32)
        s = jax.nn.sigmoid(gate)
        a = gate * s
        act[:, lo:hi] = a
        upslope[:, lo:hi] = up * (s * (1.0 + gate * (1.0 - s)))
        hid_t[lo:hi, :] = jnp.transpose(a * up).astype(BF16)


def forward(xs, w_gu):
    d, f2 = w_gu.shape
    f = f2 // 2
    return pl.pallas_call(
        forward_kernel,
        out_shape=[
            jax.ShapeDtypeStruct((f, SLOTS), BF16),
            jax.ShapeDtypeStruct((SLOTS, f), F32),
            jax.ShapeDtypeStruct((SLOTS, f), F32),
        ],
        in_specs=[VM] * (NB + 1),
        out_specs=[VM] * 3,
        scratch_shapes=[pltpu.VMEM((SLOTS, d), BF16)],
        compiler_params=params(),
        cost_estimate=cost(2 * SLOTS * d * f2, 2 * d * (SLOTS + f2) + 10 * SLOTS * f),
        name="forward",
    )(*xs, w_gu)


def ring_kernel(by, owners, here, *refs):
    gs, hid_t, refs = refs[:NB], refs[NB], refs[NB + 1 :]
    arrived, out, rows = refs[:-2], refs[-2], refs[-1]
    width = rows.shape[1]
    cols = pl.ds(pl.multiple_of(lax.rem(here[1] + by, owners) * width, width), width)
    for i in range(NB):
        rows[i * BLK : (i + 1) * BLK, :] = gs[i][:, cols]
    f = hid_t.shape[0]
    half = f // 2
    got = jnp.dot(hid_t[...], rows[...], preferred_element_type=F32)
    if len(arrived) == 2:
        got = got + arrived[0][...].astype(F32) + arrived[1][...].astype(F32)
        out[...] = jnp.transpose(got)
    elif arrived[0].shape[0] < f:
        mine, rest = slice(0, half), slice(half, f)
        if 2 * by > owners:
            mine, rest = rest, mine
        out[mine, :] = (got[mine, :] + arrived[0][...].astype(F32)).astype(BF16)
        out[rest, :] = got[rest, :].astype(BF16)
    else:
        out[...] = (got + arrived[0][...].astype(F32)).astype(BF16)


def ring_first_kernel(part, owners, here, *refs):
    gs, hid_t, out, rows = refs[:NB], refs[NB], refs[NB + 1], refs[NB + 2]
    width = rows.shape[1]
    cols = pl.ds(pl.multiple_of(lax.rem(here[1] + owners // 2, owners) * width, width), width)
    for i in range(NB):
        rows[i * BLK : (i + 1) * BLK, :] = gs[i][:, cols]
    n = out.shape[0]
    mine = hid_t[part * n : (part + 1) * n, :]
    out[...] = jnp.dot(mine, rows[...], preferred_element_type=F32).astype(BF16)


def ring(by, part, here, gs, hid_t, arrived, owners):
    f = hid_t.shape[0]
    width = gs[0].shape[1] // owners
    if not arrived:
        out = jax.ShapeDtypeStruct((f // 2, width), BF16)
        kernel = lambda *refs: ring_first_kernel(part, owners, *refs)
    else:
        kernel = lambda *refs: ring_kernel(by, owners, *refs)
        last = len(arrived) == 2
        out = jax.ShapeDtypeStruct((width, f) if last else (f, width), F32 if last else BF16)
    return pl.pallas_call(
        kernel,
        out_shape=out,
        in_specs=[SM] + [VM] * (NB + 1 + len(arrived)),
        out_specs=VM,
        scratch_shapes=[pltpu.VMEM((SLOTS, width), BF16)],
        compiler_params=params(),
        cost_estimate=cost(2 * SLOTS * width * f, 2 * SLOTS * (f + width) + 4 * f * width),
        name="ring",
    )(here, *gs, hid_t, *arrived)


def zhop(a, by):
    n = lax.axis_size("dp")
    return lax.ppermute(a, "dp", [(i, (i + by) % n) for i in range(n)])


def back_kernel(at, *refs):
    gs, refs = refs[:GROUP], refs[GROUP:]
    (w_dn, upslope, act, w_gu), refs = refs[:4], refs[4:]
    out, rows, dp = refs
    count = GROUP * BLK
    d, f = w_dn.shape
    mine = slice(at * count, (at + 1) * count)
    gather(gs, rows)
    fw, dw = 256, 512
    for k in range(f // fw):
        lo, hi = k * fw, (k + 1) * fw
        dh = jnp.dot(rows[...], w_dn[:, lo:hi], preferred_element_type=F32)
        dp[:, lo:hi] = (dh * upslope[mine, lo:hi]).astype(BF16)
        dp[:, f + lo : f + hi] = (dh * act[mine, lo:hi]).astype(BF16)
    for k in range(d // dw):
        cols = slice(k * dw, (k + 1) * dw)
        got = lax.dot_general(
            dp[...], w_gu[cols, :], (((1,), (1,)), ((), ())), preferred_element_type=F32
        )
        out[:, cols] = got.astype(BF16)


def back(gs, w_dn, upslope, act, w_gu, at):
    d, f = w_dn.shape
    rows = GROUP * BLK
    return pl.pallas_call(
        lambda *refs: back_kernel(at, *refs),
        out_shape=jax.ShapeDtypeStruct((rows, d), BF16),
        in_specs=[VM] * (GROUP + 4),
        out_specs=VM,
        scratch_shapes=[pltpu.VMEM((rows, d), BF16), pltpu.VMEM((rows, 2 * f), BF16)],
        compiler_params=params(),
        cost_estimate=cost(6 * rows * d * f, 2 * d * (2 * rows + 3 * f) + 8 * rows * f),
        name="back",
    )(*gs, w_dn, upslope, act, w_gu)


def pair_kernel(mine, theirs, *outs):
    for i, out in enumerate(outs):
        at = slice(i * BLK, (i + 1) * BLK)
        out[0:BLK, :] = mine[at, :]
        out[BLK:, :] = theirs[at, :]


def pair(mine, theirs):
    d = mine.shape[1]
    return pl.pallas_call(
        pair_kernel,
        out_shape=[jax.ShapeDtypeStruct((2 * BLK, d), BF16)] * GROUP,
        in_specs=[VM] * 2,
        out_specs=[VM] * GROUP,
        compiler_params=params(),
        cost_estimate=cost(0, 8 * GROUP * BLK * d),
        name="pair",
    )(mine, theirs)


def combine_kernel(sel_t, *refs):
    ret, refs = refs[:GROUP], refs[GROUP:]
    outs, rows = refs[:SIDE], refs[SIDE]
    n, d = outs[0].shape
    for i, r in enumerate(ret):
        near, far = (GROUP + i) * BLK, i * BLK
        rows[near : near + BLK, :] = r[0:BLK, :]
        rows[far : far + BLK, :] = r[BLK:, :]
    width = 512
    for k in range(d // width):
        cols = slice(k * width, (k + 1) * width)
        got = jnp.dot(sel_t[...], rows[:, cols], preferred_element_type=F32)
        outs[0][:, cols] = got[0:n, :]
        for j in range(1, SIDE):
            outs[j][:, cols] = got[j * n : (j + 1) * n, :].astype(BF16)


def combine(sel_t, ret):
    total = sel_t.shape[0]
    n = total // SIDE
    d = ret[0].shape[1]
    return pl.pallas_call(
        combine_kernel,
        out_shape=[jax.ShapeDtypeStruct((n, d), F32)]
        + [jax.ShapeDtypeStruct((n, d), BF16)] * (SIDE - 1),
        in_specs=[VM] * (GROUP + 1),
        out_specs=[VM] * SIDE,
        scratch_shapes=[pltpu.VMEM((SLOTS, d), BF16)],
        compiler_params=params(),
        cost_estimate=cost(2 * SLOTS * d * total, 2 * d * (SLOTS + 2 * total)),
        name="combine",
    )(sel_t, *ret)


def on_device(tokens, out_grad, expert_ids, gate_probs, gu_codes, gu_scales, down_codes, down_scales):
    owners = lax.axis_size("dp")
    here = jnp.stack([lax.axis_index("expert"), lax.axis_index("dp")]).astype(jnp.int32)
    tokens, here = lax.optimization_barrier((tokens, here))

    mine = pack(tokens, out_grad, expert_ids, gate_probs)
    packed = [mine] + [hop(mine, j, 0, True) for j in (2, 1, 3)]
    w = weights(gu_codes[0], down_codes[0], gu_scales, down_scales)
    packed, (w_gu, w_dn) = lax.optimization_barrier((packed, w))
    xs = select(False, here, packed)
    xs = [hop(a, h, f, False) if (h or f) else a for a, (h, f) in zip(xs, STEPS)]
    *gs, sel_t = select(True, here, packed)

    hid_t, upslope, act = forward(xs, w_gu)

    last, hid_t = lax.optimization_barrier((gs[GROUP + 1 :], hid_t))
    gs = gs[: GROUP + 1] + last
    gs = [hop(a, h, f, False) if (h or f) else a for a, (h, f) in zip(gs, STEPS)]

    right = (zhop(ring(owners // 2, 0, here, gs, hid_t, (), owners), 1),)
    left = ring(owners // 2, 1, here, gs, hid_t, (), owners)
    left = (zhop(left, owners - 1),)
    theirs = gs[:GROUP]
    theirs = back(theirs, w_dn, upslope, act, w_gu, 0)
    theirs = hop(theirs, 0, 1, False)
    mine = back(gs[GROUP:], w_dn, upslope, act, w_gu, 1)
    mine, right, left = lax.optimization_barrier((mine, right, left))
    ret = pair(mine, theirs)
    ret = [hop(a, h, 0, False, True) if h else a for a, (h, _) in zip(ret, STEPS)]
    for by in range(owners // 2 - 1, 0, -1):
        right = (zhop(ring(by, 0, here, gs, hid_t, right, owners), 1),)
        left = (zhop(ring(owners - by, 1, here, gs, hid_t, left, owners), owners - 1),)
    down_grad = ring(0, 0, here, gs, hid_t, right + left, owners)

    own, *others = combine(sel_t, ret)
    others = [hop(a, j, 0, True, True) for j, a in zip((2, 1, 3), others)]
    token_grad = own
    for a in others:
        token_grad = token_grad + a.astype(F32)
    return token_grad.astype(BF16), down_grad[None]


def solution(mesh):
    rows = P(("expert", "dp"), None)
    per = P("expert", None, None)
    return jax.shard_map(
        on_device,
        mesh=mesh,
        in_specs=(rows, rows, rows, rows, per, per, per, per),
        out_specs=(rows, P("expert", "dp", None)),
        check_vma=False,
    )
```

```python
import jax
import jax.numpy as jnp
from jax import lax
from jax.experimental import pallas as pl
from jax.experimental.pallas import tpu as pltpu
from jax.sharding import PartitionSpec as P

F32 = jnp.float32
BF16 = jnp.bfloat16
SIDE = 4
CORES = 2
MOST = 24
BLK = SIDE * MOST
STEPS = ((2, 1), (1, 1), (3, 1), (0, 1), (2, 0), (1, 0), (3, 0), (0, 0))
NB = len(STEPS)
SLOTS = NB * BLK
GROUP = 4


def place(x, y, c):
    return (x * SIDE + y) * CORES + c


def route(hops, flip, first):
    pairs = []
    for x in range(SIDE):
        for y in range(SIDE):
            for c in range(CORES):
                if (c == 0) == first:
                    to = place((x + hops) % SIDE, y, c ^ flip)
                else:
                    to = place(x, (y + hops) % SIDE, c ^ flip)
                pairs.append((place(x, y, c), to))
    return pairs


def hop(a, hops, flip, first, back=False):
    pairs = route(hops, flip, first)
    if back:
        pairs = [(t, s) for s, t in pairs]
    return lax.ppermute(a, "expert", pairs)


VM = pl.BlockSpec(memory_space=pltpu.VMEM)
SM = pl.BlockSpec(memory_space=pltpu.SMEM)
HBM = pl.BlockSpec(memory_space=pltpu.HBM)


def params(mib=28):
    return pltpu.CompilerParams(vmem_limit_bytes=mib * 2**20)


def cost(flops, nbytes):
    return pl.CostEstimate(flops=int(flops), bytes_accessed=int(nbytes), transcendentals=0)


def gather(blocks, rows, cols=slice(None)):
    theirs, blocks = blocks[0], blocks[1:]
    half = theirs.shape[0]
    rows[0:half, :] = theirs[:, cols]
    for i, b in enumerate(blocks):
        rows[half + i * BLK : half + (i + 1) * BLK, :] = b[0:BLK, cols]


def pack_kernel(tok, grad, ids, probs, out, got, pad, sems):
    n = tok.shape[0]
    tail = slice(2 * n, 2 * n + 16)
    top = ids.shape[0]
    copies = [
        pltpu.make_async_copy(ids, got.at[0], sems.at[0]),
        pltpu.make_async_copy(probs, pad.at[1], sems.at[1]),
        pltpu.make_async_copy(tok, out.at[0:n, :], sems.at[2]),
        pltpu.make_async_copy(grad, out.at[n : 2 * n, :], sems.at[3]),
    ]
    for c in copies:
        c.start()
    out[tail, :] = jnp.zeros((16, out.shape[1]), BF16)
    pad[0] = jnp.zeros(pad.shape[1:], F32)
    for c in copies[:2]:
        c.wait()
    pad[0] = got[0].astype(F32)
    zero = jnp.zeros((16 - top, n), F32)
    out[tail, 0:n] = jnp.concatenate([pad[0], zero], axis=0).astype(BF16)
    rest = jnp.concatenate([pad[1], zero], axis=0)
    for i in (1, 2, 3):
        term = rest.astype(BF16)
        out[tail, i * 128 : i * 128 + n] = term
        rest = rest - term.astype(F32)
    for c in copies[2:]:
        c.wait()


def pack(tok, grad, ids, probs):
    n, d = tok.shape
    top = ids.shape[1]
    return pl.pallas_call(
        pack_kernel,
        out_shape=jax.ShapeDtypeStruct((2 * n + 16, d), BF16),
        in_specs=[HBM] * 4,
        out_specs=VM,
        scratch_shapes=[
            pltpu.VMEM((1, top, n), jnp.int32),
            pltpu.VMEM((2, top, n), F32),
            pltpu.SemaphoreType.DMA((4,)),
        ],
        compiler_params=params(56),
        cost_estimate=cost(0, 4 * n * d),
        name="pack",
    )(tok, grad, ids.T, probs.T)


def experts(here):
    e = here[0]
    c, y, x = lax.rem(e, CORES), lax.rem(lax.div(e, CORES), SIDE), lax.div(e, CORES * SIDE)
    found = []
    for hops, flip in STEPS:
        one = place(x, lax.rem(y + hops, SIDE), flip)
        two = place(lax.rem(x + hops, SIDE), y, 1 - flip)
        found.append(jnp.where(c == 0, one, two).astype(F32))
    return found


def slots(ex, metas, n):
    total = SIDE * n

    def along(lo):
        parts = [metas[j, :, lo : lo + 128].astype(F32) for j in range(SIDE)]
        low = lax.broadcasted_iota(jnp.int32, parts[0].shape, 1) < n
        pairs = [jnp.where(low, parts[j], pltpu.roll(parts[j + 1], n, 1)) for j in (0, 2)]
        return jnp.concatenate(pairs, axis=1)[0:8, :]

    ids = along(0)
    probs = (along(128) + along(256)) + along(384)
    hits, weights = [], []
    for i in range(NB):
        eq = ids == ex[i]
        hits.append(jnp.max(jnp.where(eq, 1.0, 0.0), axis=0, keepdims=True))
        weights.append(jnp.sum(jnp.where(eq, probs, 0.0), axis=0, keepdims=True))
    hit = jnp.concatenate(hits, axis=0)
    s_at = lax.broadcasted_iota(jnp.int32, (total, total), 0)
    t_at = lax.broadcasted_iota(jnp.int32, (total, total), 1)
    before = jnp.where((s_at < t_at) & (s_at // n == t_at // n), 1.0, 0.0).astype(BF16)
    rank = jnp.dot(hit.astype(BF16), before, preferred_element_type=F32)
    group = (lax.broadcasted_iota(jnp.int32, (NB, total), 1) // n).astype(F32)
    return jnp.where(hit > 0.0, rank + MOST * group, -1.0), weights


def select_kernel(scaled, here, *refs):
    packed, refs = refs[:SIDE], refs[SIDE:]
    if scaled:
        outs, (sel_t, rows, metas, sel) = refs[:GROUP], refs[GROUP:]
    else:
        outs, (rows, metas, sel) = refs[:GROUP], refs[GROUP:]
    n = rows.shape[0] // SIDE
    d = rows.shape[1]
    total = SIDE * n
    for j in range(SIDE):
        metas[j] = packed[j][2 * n :, 0 : metas.shape[2]]
        rows[j * n : (j + 1) * n, :] = packed[j][n : 2 * n, :] if scaled else packed[j][0:n, :]
    slot, weights = slots(experts(here), metas, n)
    at = lax.broadcasted_iota(jnp.int32, (BLK, total), 0).astype(F32)
    scale = []
    for i in range(NB):
        one = at == slot[i : i + 1, :]
        sel[i * BLK : (i + 1) * BLK, :] = jnp.where(one, 1.0, 0.0).astype(BF16)
        if scaled:
            scale.append(jnp.sum(jnp.where(one, weights[i], 0.0), axis=1, keepdims=True))
    width = 512
    for k in range(d // width):
        cols = slice(k * width, (k + 1) * width)
        got = jnp.dot(sel[...], rows[:, cols], preferred_element_type=F32)
        for i in range(NB):
            part = got[i * BLK : (i + 1) * BLK, :]
            if scaled:
                part = part * scale[i]
            lo = 0 if i >= GROUP else BLK
            outs[i % GROUP][lo : lo + BLK, cols] = part.astype(BF16)
    if scaled:
        sel_t[...] = jnp.transpose(sel[...].astype(F32)).astype(BF16)


def select(scaled, here, packed):
    n, d = (packed[0].shape[0] - 16) // 2, packed[0].shape[1]
    total = SIDE * n
    out = [jax.ShapeDtypeStruct((2 * BLK, d), BF16)] * GROUP
    if scaled:
        out = out + [jax.ShapeDtypeStruct((total, SLOTS), BF16)]
    return pl.pallas_call(
        lambda *refs: select_kernel(scaled, *refs),
        out_shape=out,
        in_specs=[SM] + [VM] * SIDE,
        out_specs=[VM] * len(out),
        scratch_shapes=[
            pltpu.VMEM((total, d), BF16),
            pltpu.VMEM((SIDE, 16, 512), BF16),
            pltpu.VMEM((SLOTS, total), BF16),
        ],
        compiler_params=params(),
        cost_estimate=cost(2 * SLOTS * total * d, 2 * d * (SLOTS + total)),
        name="select_g" if scaled else "select_x",
    )(here, *packed)


def weights_kernel(per, gs, ds, gu, dn, w_gu, w_dn):
    side = gu.shape[0] // per
    step = pl.program_id(0)
    for i in range(per):
        at = slice(i * side, (i + 1) * side)
        for codes, scales, out in ((gu, gs, w_gu), (dn, ds, w_dn)):
            for j in range(codes.shape[1] // side):
                cols = slice(j * side, (j + 1) * side)
                scale = scales[j, 0, step * per + i]
                out[at, cols] = (codes[at, cols].astype(F32) * scale).astype(BF16)


def weights(gu, dn, gs, ds):
    d, f2 = gu.shape
    f = dn.shape[1]
    nblk = gs.shape[1]
    per = 2
    side = d // nblk * per
    blocks = [pl.BlockSpec((side, f2), lambda i: (i, 0)), pl.BlockSpec((side, f), lambda i: (i, 0))]
    return pl.pallas_call(
        lambda *refs: weights_kernel(per, *refs),
        grid=(nblk // per,),
        out_shape=[jax.ShapeDtypeStruct((d, f2), BF16), jax.ShapeDtypeStruct((d, f), BF16)],
        in_specs=[SM] * 2 + blocks,
        out_specs=blocks,
        compiler_params=params(),
        cost_estimate=cost(d * f2 * 6, 4 * d * (f2 + f)),
        name="weights",
    )(gs.transpose(2, 0, 1), ds.transpose(2, 0, 1), gu, dn)


def forward_kernel(*refs):
    xs, (w_gu, hid_t, upslope, act, rows) = refs[: GROUP + 1], refs[GROUP + 1 :]
    f = hid_t.shape[0]
    width = 256
    gather(xs, rows)
    for k in range(f // width):
        lo, hi = k * width, (k + 1) * width
        gate = jnp.dot(rows[...], w_gu[:, lo:hi], preferred_element_type=F32)
        up = jnp.dot(rows[...], w_gu[:, f + lo : f + hi], preferred_element_type=F32)
        s = jax.nn.sigmoid(gate)
        a = gate * s
        act[:, lo:hi] = a
        upslope[:, lo:hi] = up * (s * (1.0 + gate * (1.0 - s)))
        hid_t[lo:hi, :] = jnp.transpose(a * up).astype(BF16)


def forward(xs, w_gu):
    d, f2 = w_gu.shape
    f = f2 // 2
    return pl.pallas_call(
        forward_kernel,
        out_shape=[
            jax.ShapeDtypeStruct((f, SLOTS), BF16),
            jax.ShapeDtypeStruct((SLOTS, f), F32),
            jax.ShapeDtypeStruct((SLOTS, f), F32),
        ],
        in_specs=[VM] * (GROUP + 2),
        out_specs=[VM] * 3,
        scratch_shapes=[pltpu.VMEM((SLOTS, d), BF16)],
        compiler_params=params(),
        cost_estimate=cost(2 * SLOTS * d * f2, 2 * d * (SLOTS + f2) + 10 * SLOTS * f),
        name="forward",
    )(*xs, w_gu)


def ring_kernel(by, owners, here, *refs):
    gs, hid_t, refs = refs[: GROUP + 1], refs[GROUP + 1], refs[GROUP + 2 :]
    arrived, out, rows = refs[:-2], refs[-2], refs[-1]
    width = rows.shape[1]
    cols = pl.ds(pl.multiple_of(lax.rem(here[1] + by, owners) * width, width), width)
    gather(gs, rows, cols)
    f = hid_t.shape[0]
    half = f // 2
    got = jnp.dot(hid_t[...], rows[...], preferred_element_type=F32)
    if len(arrived) == 2:
        got = got + arrived[0][...].astype(F32) + arrived[1][...].astype(F32)
        out[...] = jnp.transpose(got)
    elif arrived[0].shape[0] < f:
        mine, rest = slice(0, half), slice(half, f)
        if 2 * by > owners:
            mine, rest = rest, mine
        out[mine, :] = (got[mine, :] + arrived[0][...].astype(F32)).astype(BF16)
        out[rest, :] = got[rest, :].astype(BF16)
    else:
        out[...] = (got + arrived[0][...].astype(F32)).astype(BF16)


def ring_first_kernel(part, owners, here, *refs):
    gs, (hid_t, out, rows) = refs[: GROUP + 1], refs[GROUP + 1 :]
    width = rows.shape[1]
    cols = pl.ds(pl.multiple_of(lax.rem(here[1] + owners // 2, owners) * width, width), width)
    gather(gs, rows, cols)
    n = out.shape[0]
    mine = hid_t[part * n : (part + 1) * n, :]
    out[...] = jnp.dot(mine, rows[...], preferred_element_type=F32).astype(BF16)


def ring(by, part, here, gs, hid_t, arrived, owners):
    f = hid_t.shape[0]
    width = gs[0].shape[1] // owners
    if not arrived:
        out = jax.ShapeDtypeStruct((f // 2, width), BF16)
        kernel = lambda *refs: ring_first_kernel(part, owners, *refs)
    else:
        kernel = lambda *refs: ring_kernel(by, owners, *refs)
        last = len(arrived) == 2
        out = jax.ShapeDtypeStruct((width, f) if last else (f, width), F32 if last else BF16)
    return pl.pallas_call(
        kernel,
        out_shape=out,
        in_specs=[SM] + [VM] * (GROUP + 2 + len(arrived)),
        out_specs=VM,
        scratch_shapes=[pltpu.VMEM((SLOTS, width), BF16)],
        compiler_params=params(),
        cost_estimate=cost(2 * SLOTS * width * f, 2 * SLOTS * (f + width) + 4 * f * width),
        name="ring",
    )(here, *gs, hid_t, *arrived)


def zhop(a, by):
    n = lax.axis_size("dp")
    return lax.ppermute(a, "dp", [(i, (i + by) % n) for i in range(n)])


def back_kernel(at, *refs):
    gs, refs = refs[:-7], refs[-7:]
    w_dn, upslope, act, w_gu, out, rows, dp = refs
    count = GROUP * BLK
    d, f = w_dn.shape
    mine = slice(at * count, (at + 1) * count)
    if len(gs) == 1:
        rows[...] = gs[0][...]
    else:
        for i, g in enumerate(gs):
            rows[i * BLK : (i + 1) * BLK, :] = g[0:BLK, :]
    fw, dw = 256, 512
    for k in range(f // fw):
        lo, hi = k * fw, (k + 1) * fw
        dh = jnp.dot(rows[...], w_dn[:, lo:hi], preferred_element_type=F32)
        dp[:, lo:hi] = (dh * upslope[mine, lo:hi]).astype(BF16)
        dp[:, f + lo : f + hi] = (dh * act[mine, lo:hi]).astype(BF16)
    for k in range(d // dw):
        cols = slice(k * dw, (k + 1) * dw)
        got = lax.dot_general(
            dp[...], w_gu[cols, :], (((1,), (1,)), ((), ())), preferred_element_type=F32
        )
        out[:, cols] = got.astype(BF16)


def back(gs, w_dn, upslope, act, w_gu, at):
    d, f = w_dn.shape
    rows = GROUP * BLK
    return pl.pallas_call(
        lambda *refs: back_kernel(at, *refs),
        out_shape=jax.ShapeDtypeStruct((rows, d), BF16),
        in_specs=[VM] * (len(gs) + 4),
        out_specs=VM,
        scratch_shapes=[pltpu.VMEM((rows, d), BF16), pltpu.VMEM((rows, 2 * f), BF16)],
        compiler_params=params(),
        cost_estimate=cost(6 * rows * d * f, 2 * d * (2 * rows + 3 * f) + 8 * rows * f),
        name="back",
    )(*gs, w_dn, upslope, act, w_gu)


def second_kernel(*refs):
    blocks, out = refs[:-1], refs[-1]
    for i, b in enumerate(blocks):
        out[i * BLK : (i + 1) * BLK, :] = b[BLK:, :]


def second(blocks):
    d = blocks[0].shape[1]
    return pl.pallas_call(
        second_kernel,
        out_shape=jax.ShapeDtypeStruct((len(blocks) * BLK, d), BF16),
        in_specs=[VM] * len(blocks),
        out_specs=VM,
        compiler_params=params(),
        cost_estimate=cost(0, 4 * len(blocks) * BLK * d),
        name="second",
    )(*blocks)


def spread(blocks):
    return [hop(a, h, 0, False) if h else a for a, (h, _) in zip(blocks, STEPS)]


def pair_kernel(mine, theirs, *outs):
    for i, out in enumerate(outs):
        at = slice(i * BLK, (i + 1) * BLK)
        out[0:BLK, :] = mine[at, :]
        out[BLK:, :] = theirs[at, :]


def pair(mine, theirs):
    d = mine.shape[1]
    return pl.pallas_call(
        pair_kernel,
        out_shape=[jax.ShapeDtypeStruct((2 * BLK, d), BF16)] * GROUP,
        in_specs=[VM] * 2,
        out_specs=[VM] * GROUP,
        compiler_params=params(),
        cost_estimate=cost(0, 8 * GROUP * BLK * d),
        name="pair",
    )(mine, theirs)


def combine_kernel(sel_t, *refs):
    ret, refs = refs[:GROUP], refs[GROUP:]
    outs, rows = refs[:SIDE], refs[SIDE]
    n, d = outs[0].shape
    for i, r in enumerate(ret):
        near, far = (GROUP + i) * BLK, i * BLK
        rows[near : near + BLK, :] = r[0:BLK, :]
        rows[far : far + BLK, :] = r[BLK:, :]
    width = 512
    for k in range(d // width):
        cols = slice(k * width, (k + 1) * width)
        got = jnp.dot(sel_t[...], rows[:, cols], preferred_element_type=F32)
        outs[0][:, cols] = got[0:n, :]
        for j in range(1, SIDE):
            outs[j][:, cols] = got[j * n : (j + 1) * n, :].astype(BF16)


def combine(sel_t, ret):
    total = sel_t.shape[0]
    n = total // SIDE
    d = ret[0].shape[1]
    return pl.pallas_call(
        combine_kernel,
        out_shape=[jax.ShapeDtypeStruct((n, d), F32)]
        + [jax.ShapeDtypeStruct((n, d), BF16)] * (SIDE - 1),
        in_specs=[VM] * (GROUP + 1),
        out_specs=[VM] * SIDE,
        scratch_shapes=[pltpu.VMEM((SLOTS, d), BF16)],
        compiler_params=params(),
        cost_estimate=cost(2 * SLOTS * d * total, 2 * d * (SLOTS + 2 * total)),
        name="combine",
    )(sel_t, *ret)


def on_device(tokens, out_grad, expert_ids, gate_probs, gu_codes, gu_scales, down_codes, down_scales):
    owners = lax.axis_size("dp")
    here = jnp.stack([lax.axis_index("expert"), lax.axis_index("dp")]).astype(jnp.int32)
    tokens, here = lax.optimization_barrier((tokens, here))

    mine = pack(tokens, out_grad, expert_ids, gate_probs)
    packed = [mine] + [hop(mine, j, 0, True) for j in (2, 1, 3)]
    w = weights(gu_codes[0], down_codes[0], gu_scales, down_scales)
    packed, (w_gu, w_dn) = lax.optimization_barrier((packed, w))
    xs = spread(select(False, here, packed))
    *gs, sel_t = select(True, here, packed)
    gs = spread(gs)
    xs, gs[0] = lax.optimization_barrier((xs, gs[0]))
    xs = [hop(second(xs), 0, 1, False)] + xs
    hid_t, upslope, act = forward(xs, w_gu)
    gs, hid_t = lax.optimization_barrier((gs, hid_t))
    theirs = hop(second(gs), 0, 1, False)

    mine = back(gs, w_dn, upslope, act, w_gu, 1)
    theirs, mine = lax.optimization_barrier((theirs, mine))
    gs = [theirs] + gs
    right = (zhop(ring(owners // 2, 0, here, gs, hid_t, (), owners), 1),)
    left = ring(owners // 2, 1, here, gs, hid_t, (), owners)
    left = (zhop(left, owners - 1),)
    theirs = back([theirs], w_dn, upslope, act, w_gu, 0)
    theirs, right, left = lax.optimization_barrier((theirs, right, left))
    theirs = hop(theirs, 0, 1, False)
    ret = pair(mine, theirs)
    ret = [hop(a, h, 0, False, True) if h else a for a, (h, _) in zip(ret, STEPS)]
    for by in range(owners // 2 - 1, 0, -1):
        right = (zhop(ring(by, 0, here, gs, hid_t, right, owners), 1),)
        left = (zhop(ring(owners - by, 1, here, gs, hid_t, left, owners), owners - 1),)
    down_grad = ring(0, 0, here, gs, hid_t, right + left, owners)

    own, *others = combine(sel_t, ret)
    others = [hop(a, j, 0, True, True) for j, a in zip((2, 1, 3), others)]
    token_grad = own
    for a in others:
        token_grad = token_grad + a.astype(F32)
    return token_grad.astype(BF16), down_grad[None]


def solution(mesh):
    rows = P(("expert", "dp"), None)
    per = P("expert", None, None)
    return jax.shard_map(
        on_device,
        mesh=mesh,
        in_specs=(rows, rows, rows, rows, per, per, per, per),
        out_specs=(rows, P("expert", "dp", None)),
        check_vma=False,
    )
```

```python
import jax
import jax.numpy as jnp
from jax import lax
from jax.experimental import pallas as pl
from jax.experimental.pallas import tpu as pltpu
from jax.sharding import PartitionSpec as P

F32 = jnp.float32
BF16 = jnp.bfloat16
SIDE = 4
CORES = 2
MOST = 24
BLK = SIDE * MOST
STEPS = ((2, 1), (1, 1), (3, 1), (0, 1), (2, 0), (1, 0), (3, 0), (0, 0))
NB = len(STEPS)
SLOTS = NB * BLK
GROUP = 4


def place(x, y, c):
    return (x * SIDE + y) * CORES + c


def route(hops, flip, first):
    pairs = []
    for x in range(SIDE):
        for y in range(SIDE):
            for c in range(CORES):
                if (c == 0) == first:
                    to = place((x + hops) % SIDE, y, c ^ flip)
                else:
                    to = place(x, (y + hops) % SIDE, c ^ flip)
                pairs.append((place(x, y, c), to))
    return pairs


def hop(a, hops, flip, first, back=False):
    pairs = route(hops, flip, first)
    if back:
        pairs = [(t, s) for s, t in pairs]
    return lax.ppermute(a, "expert", pairs)


VM = pl.BlockSpec(memory_space=pltpu.VMEM)
SM = pl.BlockSpec(memory_space=pltpu.SMEM)
HBM = pl.BlockSpec(memory_space=pltpu.HBM)


def params(mib=28):
    return pltpu.CompilerParams(vmem_limit_bytes=mib * 2**20)


def cost(flops, nbytes):
    return pl.CostEstimate(flops=int(flops), bytes_accessed=int(nbytes), transcendentals=0)


def gather(blocks, rows, cols=slice(None)):
    theirs, blocks = blocks[0], blocks[1:]
    half = theirs.shape[0]
    rows[0:half, :] = theirs[:, cols]
    for i, b in enumerate(blocks):
        rows[half + i * BLK : half + (i + 1) * BLK, :] = b[0:BLK, cols]


def pack_kernel(tok, grad, ids, probs, out, got, pad, tail, sems):
    n = tok.shape[0]
    top = ids.shape[0]
    copies = [
        pltpu.make_async_copy(ids, got.at[0], sems.at[0]),
        pltpu.make_async_copy(probs, pad.at[1], sems.at[1]),
        pltpu.make_async_copy(tok, out.at[0:n, :], sems.at[2]),
        pltpu.make_async_copy(grad, out.at[n : 2 * n, :], sems.at[3]),
    ]
    for c in copies:
        c.start()
    tail[...] = jnp.zeros_like(tail)
    for c in copies[:2]:
        c.wait()
    pad[0] = got[0].astype(F32)
    zero = jnp.zeros((16 - top, n), F32)
    tail[:, 0:n] = jnp.concatenate([pad[0], zero], axis=0).astype(BF16)
    rest = jnp.concatenate([pad[1], zero], axis=0)
    for i in (1, 2, 3):
        term = rest.astype(BF16)
        tail[:, i * 128 : i * 128 + n] = term
        rest = rest - term.astype(F32)
    last = pltpu.make_async_copy(tail, out.at[2 * n :, :], sems.at[4])
    last.start()
    for c in copies[2:] + [last]:
        c.wait()


def pack(tok, grad, ids, probs):
    n, d = tok.shape
    top = ids.shape[1]
    return pl.pallas_call(
        pack_kernel,
        out_shape=jax.ShapeDtypeStruct((2 * n + 16, d), BF16),
        in_specs=[HBM] * 4,
        out_specs=HBM,
        scratch_shapes=[
            pltpu.VMEM((1, top, n), jnp.int32),
            pltpu.VMEM((2, top, n), F32),
            pltpu.VMEM((16, d), BF16),
            pltpu.SemaphoreType.DMA((5,)),
        ],
        compiler_params=params(56),
        cost_estimate=cost(0, 8 * n * d),
        name="pack",
    )(tok, grad, ids.T, probs.T)


def experts(here):
    e = here[0]
    c, y, x = lax.rem(e, CORES), lax.rem(lax.div(e, CORES), SIDE), lax.div(e, CORES * SIDE)
    found = []
    for hops, flip in STEPS:
        one = place(x, lax.rem(y + hops, SIDE), flip)
        two = place(lax.rem(x + hops, SIDE), y, 1 - flip)
        found.append(jnp.where(c == 0, one, two).astype(F32))
    return found


def slots(ex, metas, n):
    total = SIDE * n

    def along(lo):
        parts = [metas[j, :, lo : lo + 128].astype(F32) for j in range(SIDE)]
        low = lax.broadcasted_iota(jnp.int32, parts[0].shape, 1) < n
        pairs = [jnp.where(low, parts[j], pltpu.roll(parts[j + 1], n, 1)) for j in (0, 2)]
        return jnp.concatenate(pairs, axis=1)[0:8, :]

    ids = along(0)
    probs = (along(128) + along(256)) + along(384)
    hits, weights = [], []
    for i in range(NB):
        eq = ids == ex[i]
        hits.append(jnp.max(jnp.where(eq, 1.0, 0.0), axis=0, keepdims=True))
        weights.append(jnp.sum(jnp.where(eq, probs, 0.0), axis=0, keepdims=True))
    hit = jnp.concatenate(hits, axis=0)
    s_at = lax.broadcasted_iota(jnp.int32, (total, total), 0)
    t_at = lax.broadcasted_iota(jnp.int32, (total, total), 1)
    before = jnp.where((s_at < t_at) & (s_at // n == t_at // n), 1.0, 0.0).astype(BF16)
    rank = jnp.dot(hit.astype(BF16), before, preferred_element_type=F32)
    group = (lax.broadcasted_iota(jnp.int32, (NB, total), 1) // n).astype(F32)
    return jnp.where(hit > 0.0, rank + MOST * group, -1.0), weights


def select_kernel(scaled, here, *refs):
    packed, refs = refs[:SIDE], refs[SIDE:]
    if scaled:
        outs, (sel_t, rows, metas, sel) = refs[:GROUP], refs[GROUP:]
    else:
        outs, (rows, metas, sel) = refs[:GROUP], refs[GROUP:]
    n = rows.shape[0] // SIDE
    d = rows.shape[1]
    total = SIDE * n
    for j in range(SIDE):
        metas[j] = packed[j][2 * n :, 0 : metas.shape[2]]
        rows[j * n : (j + 1) * n, :] = packed[j][n : 2 * n, :] if scaled else packed[j][0:n, :]
    slot, weights = slots(experts(here), metas, n)
    at = lax.broadcasted_iota(jnp.int32, (BLK, total), 0).astype(F32)
    scale = []
    for i in range(NB):
        one = at == slot[i : i + 1, :]
        sel[i * BLK : (i + 1) * BLK, :] = jnp.where(one, 1.0, 0.0).astype(BF16)
        if scaled:
            scale.append(jnp.sum(jnp.where(one, weights[i], 0.0), axis=1, keepdims=True))
    width = 512
    for k in range(d // width):
        cols = slice(k * width, (k + 1) * width)
        got = jnp.dot(sel[...], rows[:, cols], preferred_element_type=F32)
        for i in range(NB):
            part = got[i * BLK : (i + 1) * BLK, :]
            if scaled:
                part = part * scale[i]
            lo = 0 if i >= GROUP else BLK
            outs[i % GROUP][lo : lo + BLK, cols] = part.astype(BF16)
    if scaled:
        sel_t[...] = jnp.transpose(sel[...].astype(F32)).astype(BF16)


def select(scaled, here, packed):
    n, d = (packed[0].shape[0] - 16) // 2, packed[0].shape[1]
    total = SIDE * n
    out = [jax.ShapeDtypeStruct((2 * BLK, d), BF16)] * GROUP
    if scaled:
        out = out + [jax.ShapeDtypeStruct((total, SLOTS), BF16)]
    return pl.pallas_call(
        lambda *refs: select_kernel(scaled, *refs),
        out_shape=out,
        in_specs=[SM] + [VM] * SIDE,
        out_specs=[VM] * len(out),
        scratch_shapes=[
            pltpu.VMEM((total, d), BF16),
            pltpu.VMEM((SIDE, 16, 512), BF16),
            pltpu.VMEM((SLOTS, total), BF16),
        ],
        compiler_params=params(),
        cost_estimate=cost(2 * SLOTS * total * d, 2 * d * (SLOTS + total)),
        name="select_g" if scaled else "select_x",
    )(here, *packed)


def weights_kernel(per, gs, ds, gu, dn, w_gu, w_dn):
    side = gu.shape[0] // per
    step = pl.program_id(0)
    for i in range(per):
        at = slice(i * side, (i + 1) * side)
        for codes, scales, out in ((gu, gs, w_gu), (dn, ds, w_dn)):
            for j in range(codes.shape[1] // side):
                cols = slice(j * side, (j + 1) * side)
                scale = scales[j, 0, step * per + i]
                out[at, cols] = (codes[at, cols].astype(F32) * scale).astype(BF16)


def weights(gu, dn, gs, ds):
    d, f2 = gu.shape
    f = dn.shape[1]
    nblk = gs.shape[1]
    per = 2
    side = d // nblk * per
    blocks = [pl.BlockSpec((side, f2), lambda i: (i, 0)), pl.BlockSpec((side, f), lambda i: (i, 0))]
    return pl.pallas_call(
        lambda *refs: weights_kernel(per, *refs),
        grid=(nblk // per,),
        out_shape=[jax.ShapeDtypeStruct((d, f2), BF16), jax.ShapeDtypeStruct((d, f), BF16)],
        in_specs=[SM] * 2 + blocks,
        out_specs=blocks,
        compiler_params=params(),
        cost_estimate=cost(d * f2 * 6, 4 * d * (f2 + f)),
        name="weights",
    )(gs.transpose(2, 0, 1), ds.transpose(2, 0, 1), gu, dn)


def forward_kernel(*refs):
    xs, (w_gu, hid_t, upslope, act, rows) = refs[: GROUP + 1], refs[GROUP + 1 :]
    f = hid_t.shape[0]
    width = 256
    gather(xs, rows)
    for k in range(f // width):
        lo, hi = k * width, (k + 1) * width
        gate = jnp.dot(rows[...], w_gu[:, lo:hi], preferred_element_type=F32)
        up = jnp.dot(rows[...], w_gu[:, f + lo : f + hi], preferred_element_type=F32)
        s = jax.nn.sigmoid(gate)
        a = gate * s
        act[:, lo:hi] = a
        upslope[:, lo:hi] = up * (s * (1.0 + gate * (1.0 - s)))
        hid_t[lo:hi, :] = jnp.transpose(a * up).astype(BF16)


def forward(xs, w_gu):
    d, f2 = w_gu.shape
    f = f2 // 2
    return pl.pallas_call(
        forward_kernel,
        out_shape=[
            jax.ShapeDtypeStruct((f, SLOTS), BF16),
            jax.ShapeDtypeStruct((SLOTS, f), F32),
            jax.ShapeDtypeStruct((SLOTS, f), F32),
        ],
        in_specs=[VM] * (GROUP + 2),
        out_specs=[VM] * 3,
        scratch_shapes=[pltpu.VMEM((SLOTS, d), BF16)],
        compiler_params=params(),
        cost_estimate=cost(2 * SLOTS * d * f2, 2 * d * (SLOTS + f2) + 10 * SLOTS * f),
        name="forward",
    )(*xs, w_gu)


def ring_kernel(by, owners, here, *refs):
    gs, hid_t, refs = refs[: GROUP + 1], refs[GROUP + 1], refs[GROUP + 2 :]
    arrived, out, rows = refs[:-2], refs[-2], refs[-1]
    width = rows.shape[1]
    cols = pl.ds(pl.multiple_of(lax.rem(here[1] + by, owners) * width, width), width)
    gather(gs, rows, cols)
    f = hid_t.shape[0]
    half = f // 2
    got = jnp.dot(hid_t[...], rows[...], preferred_element_type=F32)
    if len(arrived) == 2:
        got = got + arrived[0][...].astype(F32) + arrived[1][...].astype(F32)
        out[...] = jnp.transpose(got)
    elif arrived[0].shape[0] < f:
        mine, rest = slice(0, half), slice(half, f)
        if 2 * by > owners:
            mine, rest = rest, mine
        out[mine, :] = (got[mine, :] + arrived[0][...].astype(F32)).astype(BF16)
        out[rest, :] = got[rest, :].astype(BF16)
    else:
        out[...] = (got + arrived[0][...].astype(F32)).astype(BF16)


def ring_first_kernel(part, owners, here, *refs):
    gs, (hid_t, out, rows) = refs[: GROUP + 1], refs[GROUP + 1 :]
    width = rows.shape[1]
    cols = pl.ds(pl.multiple_of(lax.rem(here[1] + owners // 2, owners) * width, width), width)
    gather(gs, rows, cols)
    n = out.shape[0]
    mine = hid_t[part * n : (part + 1) * n, :]
    out[...] = jnp.dot(mine, rows[...], preferred_element_type=F32).astype(BF16)


def ring(by, part, here, gs, hid_t, arrived, owners):
    f = hid_t.shape[0]
    width = gs[0].shape[1] // owners
    if not arrived:
        out = jax.ShapeDtypeStruct((f // 2, width), BF16)
        kernel = lambda *refs: ring_first_kernel(part, owners, *refs)
    else:
        kernel = lambda *refs: ring_kernel(by, owners, *refs)
        last = len(arrived) == 2
        out = jax.ShapeDtypeStruct((width, f) if last else (f, width), F32 if last else BF16)
    return pl.pallas_call(
        kernel,
        out_shape=out,
        in_specs=[SM] + [VM] * (GROUP + 2 + len(arrived)),
        out_specs=VM,
        scratch_shapes=[pltpu.VMEM((SLOTS, width), BF16)],
        compiler_params=params(),
        cost_estimate=cost(2 * SLOTS * width * f, 2 * SLOTS * (f + width) + 4 * f * width),
        name="ring",
    )(here, *gs, hid_t, *arrived)


def zhop(a, by):
    n = lax.axis_size("dp")
    return lax.ppermute(a, "dp", [(i, (i + by) % n) for i in range(n)])


def back_kernel(at, *refs):
    gs, refs = refs[:-7], refs[-7:]
    w_dn, upslope, act, w_gu, out, rows, dp = refs
    count = GROUP * BLK
    d, f = w_dn.shape
    mine = slice(at * count, (at + 1) * count)
    if len(gs) == 1:
        rows[...] = gs[0][...]
    else:
        for i, g in enumerate(gs):
            rows[i * BLK : (i + 1) * BLK, :] = g[0:BLK, :]
    fw, dw = 256, 512
    for k in range(f // fw):
        lo, hi = k * fw, (k + 1) * fw
        dh = jnp.dot(rows[...], w_dn[:, lo:hi], preferred_element_type=F32)
        dp[:, lo:hi] = (dh * upslope[mine, lo:hi]).astype(BF16)
        dp[:, f + lo : f + hi] = (dh * act[mine, lo:hi]).astype(BF16)
    for k in range(d // dw):
        cols = slice(k * dw, (k + 1) * dw)
        got = lax.dot_general(
            dp[...], w_gu[cols, :], (((1,), (1,)), ((), ())), preferred_element_type=F32
        )
        out[:, cols] = got.astype(BF16)


def back(gs, w_dn, upslope, act, w_gu, at):
    d, f = w_dn.shape
    rows = GROUP * BLK
    return pl.pallas_call(
        lambda *refs: back_kernel(at, *refs),
        out_shape=jax.ShapeDtypeStruct((rows, d), BF16),
        in_specs=[VM] * (len(gs) + 4),
        out_specs=VM,
        scratch_shapes=[pltpu.VMEM((rows, d), BF16), pltpu.VMEM((rows, 2 * f), BF16)],
        compiler_params=params(),
        cost_estimate=cost(6 * rows * d * f, 2 * d * (2 * rows + 3 * f) + 8 * rows * f),
        name="back",
    )(*gs, w_dn, upslope, act, w_gu)


def second_kernel(at, *refs):
    out = refs[-1]
    if len(refs) == 2:
        out[...] = jnp.zeros_like(out)
    else:
        out[...] = refs[1][...]
    out[at * BLK : (at + 1) * BLK, :] = refs[0][BLK:, :]


def second(blocks):
    d = blocks[0].shape[1]
    out = ()
    for at in (GROUP - 1,) + tuple(range(GROUP - 1)):
        out = (
            pl.pallas_call(
                lambda *refs, at=at: second_kernel(at, *refs),
                out_shape=jax.ShapeDtypeStruct((GROUP * BLK, d), BF16),
                in_specs=[VM] * (1 + len(out)),
                out_specs=VM,
                compiler_params=params(),
                cost_estimate=cost(0, 0),
                name="second",
            )(blocks[at], *out),
        )
    return out[0]


def spread(blocks):
    return [hop(a, h, 0, False) if h else a for a, (h, _) in zip(blocks, STEPS)]


def pair_kernel(mine, theirs, *outs):
    for i, out in enumerate(outs):
        at = slice(i * BLK, (i + 1) * BLK)
        out[0:BLK, :] = mine[at, :]
        out[BLK:, :] = theirs[at, :]


def pair(mine, theirs):
    d = mine.shape[1]
    return pl.pallas_call(
        pair_kernel,
        out_shape=[jax.ShapeDtypeStruct((2 * BLK, d), BF16)] * GROUP,
        in_specs=[VM] * 2,
        out_specs=[VM] * GROUP,
        compiler_params=params(),
        cost_estimate=cost(0, 8 * GROUP * BLK * d),
        name="pair",
    )(mine, theirs)


def combine_kernel(sel_t, *refs):
    ret, refs = refs[:GROUP], refs[GROUP:]
    outs, rows = refs[:SIDE], refs[SIDE]
    n, d = outs[0].shape
    for i, r in enumerate(ret):
        near, far = (GROUP + i) * BLK, i * BLK
        rows[near : near + BLK, :] = r[0:BLK, :]
        rows[far : far + BLK, :] = r[BLK:, :]
    width = 512
    for k in range(d // width):
        cols = slice(k * width, (k + 1) * width)
        got = jnp.dot(sel_t[...], rows[:, cols], preferred_element_type=F32)
        outs[0][:, cols] = got[0:n, :]
        for j in range(1, SIDE):
            outs[j][:, cols] = got[j * n : (j + 1) * n, :].astype(BF16)


def combine(sel_t, ret):
    total = sel_t.shape[0]
    n = total // SIDE
    d = ret[0].shape[1]
    return pl.pallas_call(
        combine_kernel,
        out_shape=[jax.ShapeDtypeStruct((n, d), F32)]
        + [jax.ShapeDtypeStruct((n, d), BF16)] * (SIDE - 1),
        in_specs=[VM] * (GROUP + 1),
        out_specs=[VM] * SIDE,
        scratch_shapes=[pltpu.VMEM((SLOTS, d), BF16)],
        compiler_params=params(),
        cost_estimate=cost(2 * SLOTS * d * total, 2 * d * (SLOTS + 2 * total)),
        name="combine",
    )(sel_t, *ret)


def on_device(tokens, out_grad, expert_ids, gate_probs, gu_codes, gu_scales, down_codes, down_scales):
    owners = lax.axis_size("dp")
    here = jnp.stack([lax.axis_index("expert"), lax.axis_index("dp")]).astype(jnp.int32)
    tokens, here = lax.optimization_barrier((tokens, here))

    mine = pack(tokens, out_grad, expert_ids, gate_probs)
    packed = [mine] + [hop(mine, j, 0, True) for j in (2, 1, 3)]
    w = weights(gu_codes[0], down_codes[0], gu_scales, down_scales)
    packed, (w_gu, w_dn) = lax.optimization_barrier((packed, w))
    xs = select(False, here, packed)
    xs, packed = lax.optimization_barrier((xs, packed))
    xs = spread(xs)
    *gs, sel_t = select(True, here, packed)
    xs[2], _ = lax.optimization_barrier((xs[2], gs))
    gs = spread(gs)
    xs = [hop(second(xs), 0, 1, False)] + xs
    hid_t, upslope, act = forward(xs, w_gu)
    gs, hid_t = lax.optimization_barrier((gs, hid_t))
    theirs = hop(second(gs), 0, 1, False)

    mine = back(gs, w_dn, upslope, act, w_gu, 1)
    theirs, mine = lax.optimization_barrier((theirs, mine))
    gs = [theirs] + gs
    right = (zhop(ring(owners // 2, 0, here, gs, hid_t, (), owners), 1),)
    left = ring(owners // 2, 1, here, gs, hid_t, (), owners)
    left = (zhop(left, owners - 1),)
    theirs = back([theirs], w_dn, upslope, act, w_gu, 0)
    theirs, right, left = lax.optimization_barrier((theirs, right, left))
    theirs = hop(theirs, 0, 1, False)
    ret = pair(mine, theirs)
    ret = [hop(a, h, 0, False, True) if h else a for a, (h, _) in zip(ret, STEPS)]
    for by in range(owners // 2 - 1, 0, -1):
        right = (zhop(ring(by, 0, here, gs, hid_t, right, owners), 1),)
        left = (zhop(ring(owners - by, 1, here, gs, hid_t, left, owners), owners - 1),)
    down_grad = ring(0, 0, here, gs, hid_t, right + left, owners)

    own, *others = combine(sel_t, ret)
    others = [hop(a, j, 0, True, True) for j, a in zip((2, 1, 3), others)]
    token_grad = own
    for a in others:
        token_grad = token_grad + a.astype(F32)
    return token_grad.astype(BF16), down_grad[None]


def solution(mesh):
    rows = P(("expert", "dp"), None)
    per = P("expert", None, None)
    return jax.shard_map(
        on_device,
        mesh=mesh,
        in_specs=(rows, rows, rows, rows, per, per, per, per),
        out_specs=(rows, P("expert", "dp", None)),
        check_vma=False,
    )
```

```python
import jax
import jax.numpy as jnp
from jax import lax
from jax.experimental import pallas as pl
from jax.experimental.pallas import tpu as pltpu
from jax.sharding import PartitionSpec as P

F32 = jnp.float32
BF16 = jnp.bfloat16
SIDE = 4
CORES = 2
MOST = 24
BLK = SIDE * MOST
STEPS = ((2, 1), (1, 1), (3, 1), (0, 1), (2, 0), (1, 0), (3, 0), (0, 0))
NB = len(STEPS)
SLOTS = NB * BLK
GROUP = 4


def place(x, y, c):
    return (x * SIDE + y) * CORES + c


def route(hops, flip, first):
    pairs = []
    for x in range(SIDE):
        for y in range(SIDE):
            for c in range(CORES):
                if (c == 0) == first:
                    to = place((x + hops) % SIDE, y, c ^ flip)
                else:
                    to = place(x, (y + hops) % SIDE, c ^ flip)
                pairs.append((place(x, y, c), to))
    return pairs


def hop(a, hops, flip, first, back=False):
    pairs = route(hops, flip, first)
    if back:
        pairs = [(t, s) for s, t in pairs]
    return lax.ppermute(a, "expert", pairs)


VM = pl.BlockSpec(memory_space=pltpu.VMEM)
SM = pl.BlockSpec(memory_space=pltpu.SMEM)
HBM = pl.BlockSpec(memory_space=pltpu.HBM)


def params(mib=28):
    return pltpu.CompilerParams(vmem_limit_bytes=mib * 2**20)


def cost(flops, nbytes):
    return pl.CostEstimate(flops=int(flops), bytes_accessed=int(nbytes), transcendentals=0)


def gather(blocks, rows, cols=slice(None)):
    theirs, blocks = blocks[0], blocks[1:]
    half = theirs.shape[0]
    rows[0:half, :] = theirs[:, cols]
    for i, b in enumerate(blocks):
        rows[half + i * BLK : half + (i + 1) * BLK, :] = b[0:BLK, cols]


def pack_kernel(tok, grad, ids, probs, out, got, pad, sems):
    n = tok.shape[0]
    tail = slice(2 * n, 2 * n + 16)
    top = ids.shape[0]
    copies = [
        pltpu.make_async_copy(ids, got.at[0], sems.at[0]),
        pltpu.make_async_copy(probs, pad.at[1], sems.at[1]),
        pltpu.make_async_copy(tok, out.at[0:n, :], sems.at[2]),
        pltpu.make_async_copy(grad, out.at[n : 2 * n, :], sems.at[3]),
    ]
    for c in copies:
        c.start()
    out[tail, :] = jnp.zeros((16, out.shape[1]), BF16)
    pad[0] = jnp.zeros(pad.shape[1:], F32)
    for c in copies[:2]:
        c.wait()
    pad[0] = got[0].astype(F32)
    zero = jnp.zeros((16 - top, n), F32)
    out[tail, 0:n] = jnp.concatenate([pad[0], zero], axis=0).astype(BF16)
    rest = jnp.concatenate([pad[1], zero], axis=0)
    for i in (1, 2, 3):
        term = rest.astype(BF16)
        out[tail, i * 128 : i * 128 + n] = term
        rest = rest - term.astype(F32)
    for c in copies[2:]:
        c.wait()


def pack(tok, grad, ids, probs):
    n, d = tok.shape
    top = ids.shape[1]
    return pl.pallas_call(
        pack_kernel,
        out_shape=jax.ShapeDtypeStruct((2 * n + 16, d), BF16),
        in_specs=[HBM] * 4,
        out_specs=VM,
        scratch_shapes=[
            pltpu.VMEM((1, top, n), jnp.int32),
            pltpu.VMEM((2, top, n), F32),
            pltpu.SemaphoreType.DMA((4,)),
        ],
        compiler_params=params(56),
        cost_estimate=cost(0, 4 * n * d),
        name="pack",
    )(tok, grad, ids.T, probs.T)


def experts(here):
    e = here[0]
    c, y, x = lax.rem(e, CORES), lax.rem(lax.div(e, CORES), SIDE), lax.div(e, CORES * SIDE)
    found = []
    for hops, flip in STEPS:
        one = place(x, lax.rem(y + hops, SIDE), flip)
        two = place(lax.rem(x + hops, SIDE), y, 1 - flip)
        found.append(jnp.where(c == 0, one, two).astype(F32))
    return found


def slots(ex, metas, n):
    total = SIDE * n

    def along(lo):
        parts = [metas[j, :, lo : lo + 128].astype(F32) for j in range(SIDE)]
        low = lax.broadcasted_iota(jnp.int32, parts[0].shape, 1) < n
        pairs = [jnp.where(low, parts[j], pltpu.roll(parts[j + 1], n, 1)) for j in (0, 2)]
        return jnp.concatenate(pairs, axis=1)[0:8, :]

    ids = along(0)
    probs = (along(128) + along(256)) + along(384)
    hits, weights = [], []
    for i in range(NB):
        eq = ids == ex[i]
        hits.append(jnp.max(jnp.where(eq, 1.0, 0.0), axis=0, keepdims=True))
        weights.append(jnp.sum(jnp.where(eq, probs, 0.0), axis=0, keepdims=True))
    hit = jnp.concatenate(hits, axis=0)
    s_at = lax.broadcasted_iota(jnp.int32, (total, total), 0)
    t_at = lax.broadcasted_iota(jnp.int32, (total, total), 1)
    before = jnp.where((s_at < t_at) & (s_at // n == t_at // n), 1.0, 0.0).astype(BF16)
    rank = jnp.dot(hit.astype(BF16), before, preferred_element_type=F32)
    group = (lax.broadcasted_iota(jnp.int32, (NB, total), 1) // n).astype(F32)
    return jnp.where(hit > 0.0, rank + MOST * group, -1.0), weights


def select_kernel(scaled, here, *refs):
    packed, refs = refs[:SIDE], refs[SIDE:]
    if scaled:
        outs, (sel_t, rows, metas, sel) = refs[:GROUP], refs[GROUP:]
    else:
        outs, (rows, metas, sel) = refs[:GROUP], refs[GROUP:]
    n = rows.shape[0] // SIDE
    d = rows.shape[1]
    total = SIDE * n
    for j in range(SIDE):
        metas[j] = packed[j][2 * n :, 0 : metas.shape[2]]
        rows[j * n : (j + 1) * n, :] = packed[j][n : 2 * n, :] if scaled else packed[j][0:n, :]
    slot, weights = slots(experts(here), metas, n)
    at = lax.broadcasted_iota(jnp.int32, (BLK, total), 0).astype(F32)
    scale = []
    for i in range(NB):
        one = at == slot[i : i + 1, :]
        sel[i * BLK : (i + 1) * BLK, :] = jnp.where(one, 1.0, 0.0).astype(BF16)
        if scaled:
            scale.append(jnp.sum(jnp.where(one, weights[i], 0.0), axis=1, keepdims=True))
    width = 512
    for k in range(d // width):
        cols = slice(k * width, (k + 1) * width)
        got = jnp.dot(sel[...], rows[:, cols], preferred_element_type=F32)
        for i in range(NB):
            part = got[i * BLK : (i + 1) * BLK, :]
            if scaled:
                part = part * scale[i]
            lo = 0 if i >= GROUP else BLK
            outs[i % GROUP][lo : lo + BLK, cols] = part.astype(BF16)
    if scaled:
        sel_t[...] = jnp.transpose(sel[...].astype(F32)).astype(BF16)


def select(scaled, here, packed):
    n, d = (packed[0].shape[0] - 16) // 2, packed[0].shape[1]
    total = SIDE * n
    out = [jax.ShapeDtypeStruct((2 * BLK, d), BF16)] * GROUP
    if scaled:
        out = out + [jax.ShapeDtypeStruct((total, SLOTS), BF16)]
    return pl.pallas_call(
        lambda *refs: select_kernel(scaled, *refs),
        out_shape=out,
        in_specs=[SM] + [VM] * SIDE,
        out_specs=[VM] * len(out),
        scratch_shapes=[
            pltpu.VMEM((total, d), BF16),
            pltpu.VMEM((SIDE, 16, 512), BF16),
            pltpu.VMEM((SLOTS, total), BF16),
        ],
        compiler_params=params(),
        cost_estimate=cost(2 * SLOTS * total * d, 2 * d * (SLOTS + total)),
        name="select_g" if scaled else "select_x",
    )(here, *packed)


def weights_kernel(per, gs, ds, gu, dn, w_gu, w_dn):
    side = gu.shape[0] // per
    step = pl.program_id(0)
    for i in range(per):
        at = slice(i * side, (i + 1) * side)
        for codes, scales, out in ((gu, gs, w_gu), (dn, ds, w_dn)):
            for j in range(codes.shape[1] // side):
                cols = slice(j * side, (j + 1) * side)
                scale = scales[j, 0, step * per + i]
                out[at, cols] = (codes[at, cols].astype(F32) * scale).astype(BF16)


def weights(gu, dn, gs, ds):
    d, f2 = gu.shape
    f = dn.shape[1]
    nblk = gs.shape[1]
    per = 2
    side = d // nblk * per
    blocks = [pl.BlockSpec((side, f2), lambda i: (i, 0)), pl.BlockSpec((side, f), lambda i: (i, 0))]
    return pl.pallas_call(
        lambda *refs: weights_kernel(per, *refs),
        grid=(nblk // per,),
        out_shape=[jax.ShapeDtypeStruct((d, f2), BF16), jax.ShapeDtypeStruct((d, f), BF16)],
        in_specs=[SM] * 2 + blocks,
        out_specs=blocks,
        compiler_params=params(),
        cost_estimate=cost(d * f2 * 6, 4 * d * (f2 + f)),
        name="weights",
    )(gs.transpose(2, 0, 1), ds.transpose(2, 0, 1), gu, dn)


def forward_kernel(*refs):
    xs, (w_gu, hid_t, upslope, act, rows) = refs[: GROUP + 1], refs[GROUP + 1 :]
    f = hid_t.shape[0]
    width = 256
    gather(xs, rows)
    for k in range(f // width):
        lo, hi = k * width, (k + 1) * width
        gate = jnp.dot(rows[...], w_gu[:, lo:hi], preferred_element_type=F32)
        up = jnp.dot(rows[...], w_gu[:, f + lo : f + hi], preferred_element_type=F32)
        s = jax.nn.sigmoid(gate)
        a = gate * s
        act[:, lo:hi] = a
        upslope[:, lo:hi] = up * (s * (1.0 + gate * (1.0 - s)))
        hid_t[lo:hi, :] = jnp.transpose(a * up).astype(BF16)


def forward(xs, w_gu):
    d, f2 = w_gu.shape
    f = f2 // 2
    return pl.pallas_call(
        forward_kernel,
        out_shape=[
            jax.ShapeDtypeStruct((f, SLOTS), BF16),
            jax.ShapeDtypeStruct((SLOTS, f), F32),
            jax.ShapeDtypeStruct((SLOTS, f), F32),
        ],
        in_specs=[VM] * (GROUP + 2),
        out_specs=[VM] * 3,
        scratch_shapes=[pltpu.VMEM((SLOTS, d), BF16)],
        compiler_params=params(),
        cost_estimate=cost(2 * SLOTS * d * f2, 2 * d * (SLOTS + f2) + 10 * SLOTS * f),
        name="forward",
    )(*xs, w_gu)


def product(by, owners, here, gs, hid_t, rows):
    width = rows.shape[1]
    cols = pl.ds(pl.multiple_of(lax.rem(here[1] + by, owners) * width, width), width)
    gather(gs, rows, cols)
    return jnp.dot(hid_t, rows[...], preferred_element_type=F32)


def ring_first_kernel(part, owners, here, *refs):
    gs, (hid_t, out, rows) = refs[: GROUP + 1], refs[GROUP + 1 :]
    n = out.shape[0]
    mine = hid_t[part * n : (part + 1) * n, :]
    out[...] = product(owners // 2, owners, here, gs, mine, rows).astype(BF16)


def ring_second_kernel(part, owners, here, *refs):
    gs, (hid_t, arrived, out, rows) = refs[: GROUP + 1], refs[GROUP + 1 :]
    by = owners // 2 + (1 if part else -1)
    got = product(by, owners, here, gs, hid_t[...], rows)
    half = arrived.shape[0]
    mine, rest = slice(part * half, (part + 1) * half), slice((1 - part) * half, (2 - part) * half)
    out[mine, :] = (got[mine, :] + arrived[...].astype(F32)).astype(BF16)
    out[rest, :] = got[rest, :].astype(BF16)


def ring(part, here, gs, hid_t, arrived, owners):
    f = hid_t.shape[0]
    width = gs[0].shape[1] // owners
    kernel = ring_second_kernel if arrived else ring_first_kernel
    return pl.pallas_call(
        lambda *refs: kernel(part, owners, *refs),
        out_shape=jax.ShapeDtypeStruct((f if arrived else f // 2, width), BF16),
        in_specs=[SM] + [VM] * (GROUP + 2 + len(arrived)),
        out_specs=VM,
        scratch_shapes=[pltpu.VMEM((SLOTS, width), BF16)],
        compiler_params=params(),
        cost_estimate=cost(2 * SLOTS * width * f, 2 * SLOTS * (f + width) + 4 * f * width),
        name="ring",
    )(here, *gs, hid_t, *arrived)


def products_kernel(bys, owners, here, *refs):
    gs, hid_t, outs, rows = refs[: GROUP + 1], refs[GROUP + 1], refs[GROUP + 2 : -1], refs[-1]
    for by, out in zip(bys, outs):
        out[...] = product(by, owners, here, gs, hid_t[...], rows)


def products(bys, here, gs, hid_t, owners):
    f = hid_t.shape[0]
    width = gs[0].shape[1] // owners
    return pl.pallas_call(
        lambda *refs: products_kernel(bys, owners, *refs),
        out_shape=[jax.ShapeDtypeStruct((f, width), F32)] * len(bys),
        in_specs=[SM] + [VM] * (GROUP + 2),
        out_specs=[VM] * len(bys),
        scratch_shapes=[pltpu.VMEM((SLOTS, width), BF16)],
        compiler_params=params(),
        cost_estimate=cost(2 * SLOTS * width * f * len(bys), 2 * SLOTS * f + 6 * f * width * len(bys)),
        name="products",
    )(here, *gs, hid_t)


def add_kernel(mine, *refs):
    arrived, out = refs[:-1], refs[-1]
    total = mine[...]
    for a in arrived:
        total = total + a[...].astype(F32)
    out[...] = total.astype(BF16) if len(arrived) == 1 else jnp.transpose(total)


def add(mine, *arrived):
    f, width = mine.shape
    if len(arrived) == 1:
        out = jax.ShapeDtypeStruct((f, width), BF16)
    else:
        out = jax.ShapeDtypeStruct((width, f), F32)
    return pl.pallas_call(
        add_kernel,
        out_shape=out,
        in_specs=[VM] * (1 + len(arrived)),
        out_specs=VM,
        compiler_params=params(),
        cost_estimate=cost(4 * f * width, 10 * f * width),
        name="add",
    )(mine, *arrived)


def zhop(a, by):
    n = lax.axis_size("dp")
    return lax.ppermute(a, "dp", [(i, (i + by) % n) for i in range(n)])


def back_kernel(at, *refs):
    gs, refs = refs[:-7], refs[-7:]
    w_dn, upslope, act, w_gu, out, rows, dp = refs
    count = GROUP * BLK
    d, f = w_dn.shape
    mine = slice(at * count, (at + 1) * count)
    if len(gs) == 1:
        rows[...] = gs[0][...]
    else:
        for i, g in enumerate(gs):
            rows[i * BLK : (i + 1) * BLK, :] = g[0:BLK, :]
    fw, dw = 256, 512
    for k in range(f // fw):
        lo, hi = k * fw, (k + 1) * fw
        dh = jnp.dot(rows[...], w_dn[:, lo:hi], preferred_element_type=F32)
        dp[:, lo:hi] = (dh * upslope[mine, lo:hi]).astype(BF16)
        dp[:, f + lo : f + hi] = (dh * act[mine, lo:hi]).astype(BF16)
    for k in range(d // dw):
        cols = slice(k * dw, (k + 1) * dw)
        got = lax.dot_general(
            dp[...], w_gu[cols, :], (((1,), (1,)), ((), ())), preferred_element_type=F32
        )
        out[:, cols] = got.astype(BF16)


def back(gs, w_dn, upslope, act, w_gu, at):
    d, f = w_dn.shape
    rows = GROUP * BLK
    return pl.pallas_call(
        lambda *refs: back_kernel(at, *refs),
        out_shape=jax.ShapeDtypeStruct((rows, d), BF16),
        in_specs=[VM] * (len(gs) + 4),
        out_specs=VM,
        scratch_shapes=[pltpu.VMEM((rows, d), BF16), pltpu.VMEM((rows, 2 * f), BF16)],
        compiler_params=params(),
        cost_estimate=cost(6 * rows * d * f, 2 * d * (2 * rows + 3 * f) + 8 * rows * f),
        name="back",
    )(*gs, w_dn, upslope, act, w_gu)


def second_kernel(*refs):
    blocks, out = refs[:-1], refs[-1]
    for i, b in enumerate(blocks):
        out[i * BLK : (i + 1) * BLK, :] = b[BLK:, :]


def second(blocks):
    d = blocks[0].shape[1]
    return pl.pallas_call(
        second_kernel,
        out_shape=jax.ShapeDtypeStruct((len(blocks) * BLK, d), BF16),
        in_specs=[VM] * len(blocks),
        out_specs=VM,
        compiler_params=params(),
        cost_estimate=cost(0, 4 * len(blocks) * BLK * d),
        name="second",
    )(*blocks)


def spread(blocks):
    return [hop(a, h, 0, False) if h else a for a, (h, _) in zip(blocks, STEPS)]


def pair_kernel(mine, theirs, *outs):
    for i, out in enumerate(outs):
        at = slice(i * BLK, (i + 1) * BLK)
        out[0:BLK, :] = mine[at, :]
        out[BLK:, :] = theirs[at, :]


def pair(mine, theirs):
    d = mine.shape[1]
    return pl.pallas_call(
        pair_kernel,
        out_shape=[jax.ShapeDtypeStruct((2 * BLK, d), BF16)] * GROUP,
        in_specs=[VM] * 2,
        out_specs=[VM] * GROUP,
        compiler_params=params(),
        cost_estimate=cost(0, 8 * GROUP * BLK * d),
        name="pair",
    )(mine, theirs)


def combine_kernel(sel_t, *refs):
    ret, refs = refs[:GROUP], refs[GROUP:]
    outs, rows = refs[:SIDE], refs[SIDE]
    n, d = outs[0].shape
    for i, r in enumerate(ret):
        near, far = (GROUP + i) * BLK, i * BLK
        rows[near : near + BLK, :] = r[0:BLK, :]
        rows[far : far + BLK, :] = r[BLK:, :]
    width = 512
    for k in range(d // width):
        cols = slice(k * width, (k + 1) * width)
        got = jnp.dot(sel_t[...], rows[:, cols], preferred_element_type=F32)
        outs[0][:, cols] = got[0:n, :]
        for j in range(1, SIDE):
            outs[j][:, cols] = got[j * n : (j + 1) * n, :].astype(BF16)


def combine(sel_t, ret):
    total = sel_t.shape[0]
    n = total // SIDE
    d = ret[0].shape[1]
    return pl.pallas_call(
        combine_kernel,
        out_shape=[jax.ShapeDtypeStruct((n, d), F32)]
        + [jax.ShapeDtypeStruct((n, d), BF16)] * (SIDE - 1),
        in_specs=[VM] * (GROUP + 1),
        out_specs=[VM] * SIDE,
        scratch_shapes=[pltpu.VMEM((SLOTS, d), BF16)],
        compiler_params=params(),
        cost_estimate=cost(2 * SLOTS * d * total, 2 * d * (SLOTS + 2 * total)),
        name="combine",
    )(sel_t, *ret)


def on_device(tokens, out_grad, expert_ids, gate_probs, gu_codes, gu_scales, down_codes, down_scales):
    owners = lax.axis_size("dp")
    here = jnp.stack([lax.axis_index("expert"), lax.axis_index("dp")]).astype(jnp.int32)
    tokens, here = lax.optimization_barrier((tokens, here))

    mine = pack(tokens, out_grad, expert_ids, gate_probs)
    packed = [mine] + [hop(mine, j, 0, True) for j in (2, 1, 3)]
    w = weights(gu_codes[0], down_codes[0], gu_scales, down_scales)
    packed, (w_gu, w_dn) = lax.optimization_barrier((packed, w))
    xs = select(False, here, packed)
    xs, packed = lax.optimization_barrier((xs, packed))
    xs = spread(xs)
    *gs, sel_t = select(True, here, packed)
    gs = spread(gs)
    xs, gs[0] = lax.optimization_barrier((xs, gs[0]))
    xs = [hop(second(xs), 0, 1, False)] + xs
    hid_t, upslope, act = forward(xs, w_gu)
    gs, hid_t = lax.optimization_barrier((gs, hid_t))
    theirs = hop(second(gs), 0, 1, False)

    mine = back(gs, w_dn, upslope, act, w_gu, 1)
    theirs, mine = lax.optimization_barrier((theirs, mine))
    gs = [theirs] + gs
    right = ring(0, here, gs, hid_t, (), owners)
    left = ring(1, here, gs, hid_t, (), owners)
    right, left = zhop(right, 1), zhop(left, owners - 1)
    theirs = back([theirs], w_dn, upslope, act, w_gu, 0)
    theirs, right, left = lax.optimization_barrier((theirs, right, left))
    theirs = hop(theirs, 0, 1, False)
    ret = pair(mine, theirs)
    ret = [hop(a, h, 0, False, True) if h else a for a, (h, _) in zip(ret, STEPS)]
    right = ring(0, here, gs, hid_t, (right,), owners)
    left = ring(1, here, gs, hid_t, (left,), owners)
    right, left, hid_t = lax.optimization_barrier((right, left, hid_t))
    right, left = zhop(right, 1), zhop(left, owners - 1)
    bys = [b for by in range(owners // 2 - 2, 0, -1) for b in (by, owners - by)] + [0]
    *more, last = products(bys, here, gs, hid_t, owners)
    for at in range(0, len(more), 2):
        right = zhop(add(more[at], right), 1)
        left = zhop(add(more[at + 1], left), owners - 1)
    down_grad = add(last, right, left)

    own, *others = combine(sel_t, ret)
    others = [hop(a, j, 0, True, True) for j, a in zip((2, 1, 3), others)]
    token_grad = own
    for a in others:
        token_grad = token_grad + a.astype(F32)
    return token_grad.astype(BF16), down_grad[None]


def solution(mesh):
    rows = P(("expert", "dp"), None)
    per = P("expert", None, None)
    return jax.shard_map(
        on_device,
        mesh=mesh,
        in_specs=(rows, rows, rows, rows, per, per, per, per),
        out_specs=(rows, P("expert", "dp", None)),
        check_vma=False,
    )
```

```python
import jax
import jax.numpy as jnp
from jax import lax
from jax.experimental import pallas as pl
from jax.experimental.pallas import tpu as pltpu
from jax.sharding import PartitionSpec as P

F32 = jnp.float32
BF16 = jnp.bfloat16
SIDE = 4
CORES = 2
MOST = 24
BLK = SIDE * MOST
STEPS = ((2, 1), (1, 1), (3, 1), (0, 1), (2, 0), (1, 0), (3, 0), (0, 0))
NB = len(STEPS)
SLOTS = NB * BLK
GROUP = 4


def place(x, y, c):
    return (x * SIDE + y) * CORES + c


def route(hops, flip, first):
    pairs = []
    for x in range(SIDE):
        for y in range(SIDE):
            for c in range(CORES):
                if (c == 0) == first:
                    to = place((x + hops) % SIDE, y, c ^ flip)
                else:
                    to = place(x, (y + hops) % SIDE, c ^ flip)
                pairs.append((place(x, y, c), to))
    return pairs


def hop(a, hops, flip, first, back=False):
    pairs = route(hops, flip, first)
    if back:
        pairs = [(t, s) for s, t in pairs]
    return lax.ppermute(a, "expert", pairs)


VM = pl.BlockSpec(memory_space=pltpu.VMEM)
SM = pl.BlockSpec(memory_space=pltpu.SMEM)
HBM = pl.BlockSpec(memory_space=pltpu.HBM)


def params(mib=28):
    return pltpu.CompilerParams(vmem_limit_bytes=mib * 2**20)


def cost(flops, nbytes):
    return pl.CostEstimate(flops=int(flops), bytes_accessed=int(nbytes), transcendentals=0)


def gather(blocks, rows, cols=slice(None)):
    theirs, blocks = blocks[0], blocks[1:]
    half = theirs.shape[0]
    rows[0:half, :] = theirs[:, cols]
    for i, b in enumerate(blocks):
        rows[half + i * BLK : half + (i + 1) * BLK, :] = b[0:BLK, cols]


LANES = 512


def pack_kernel(tok, grad, ids, probs, out, got, pad, sems):
    n, d = tok.shape
    top = ids.shape[0]
    lo = 2 * n * (d // LANES)
    tail = slice(lo, lo + 16)
    copies = [
        pltpu.make_async_copy(ids, got.at[0], sems.at[0]),
        pltpu.make_async_copy(probs, pad.at[1], sems.at[1]),
    ]
    at = 0
    for part in (tok, grad):
        for k in range(d // LANES):
            source = part.at[:, k * LANES : (k + 1) * LANES]
            copies.append(pltpu.make_async_copy(source, out.at[at * n : (at + 1) * n, :], sems.at[2 + at]))
            at += 1
    for c in copies:
        c.start()
    out[tail, :] = jnp.zeros((16, LANES), BF16)
    for c in copies[:2]:
        c.wait()
    pad[0] = got[0].astype(F32)
    zero = jnp.zeros((16 - top, n), F32)
    out[tail, 0:n] = jnp.concatenate([pad[0], zero], axis=0).astype(BF16)
    rest = jnp.concatenate([pad[1], zero], axis=0)
    for i in (1, 2, 3):
        term = rest.astype(BF16)
        out[tail, i * 128 : i * 128 + n] = term
        rest = rest - term.astype(F32)
    for c in copies[2:]:
        c.wait()


def pack(tok, grad, ids, probs):
    n, d = tok.shape
    top = ids.shape[1]
    blocks = d // LANES
    return pl.pallas_call(
        pack_kernel,
        out_shape=jax.ShapeDtypeStruct((2 * n * blocks + 16, LANES), BF16),
        in_specs=[HBM] * 4,
        out_specs=VM,
        scratch_shapes=[
            pltpu.VMEM((1, top, n), jnp.int32),
            pltpu.VMEM((2, top, n), F32),
            pltpu.SemaphoreType.DMA((2 + 2 * blocks,)),
        ],
        compiler_params=params(56),
        cost_estimate=cost(0, 8 * n * d),
        name="pack",
    )(tok, grad, ids.T, probs.T)


def experts(here):
    e = here[0]
    c, y, x = lax.rem(e, CORES), lax.rem(lax.div(e, CORES), SIDE), lax.div(e, CORES * SIDE)
    found = []
    for hops, flip in STEPS:
        one = place(x, lax.rem(y + hops, SIDE), flip)
        two = place(lax.rem(x + hops, SIDE), y, 1 - flip)
        found.append(jnp.where(c == 0, one, two).astype(F32))
    return found


def slots(ex, metas, n):
    total = SIDE * n

    def along(lo):
        parts = [metas[j, :, lo : lo + 128].astype(F32) for j in range(SIDE)]
        low = lax.broadcasted_iota(jnp.int32, parts[0].shape, 1) < n
        pairs = [jnp.where(low, parts[j], pltpu.roll(parts[j + 1], n, 1)) for j in (0, 2)]
        return jnp.concatenate(pairs, axis=1)[0:8, :]

    ids = along(0)
    probs = (along(128) + along(256)) + along(384)
    hits, weights = [], []
    for i in range(NB):
        eq = ids == ex[i]
        hits.append(jnp.max(jnp.where(eq, 1.0, 0.0), axis=0, keepdims=True))
        weights.append(jnp.sum(jnp.where(eq, probs, 0.0), axis=0, keepdims=True))
    hit = jnp.concatenate(hits, axis=0)
    s_at = lax.broadcasted_iota(jnp.int32, (total, total), 0)
    t_at = lax.broadcasted_iota(jnp.int32, (total, total), 1)
    before = jnp.where((s_at < t_at) & (s_at // n == t_at // n), 1.0, 0.0).astype(BF16)
    rank = jnp.dot(hit.astype(BF16), before, preferred_element_type=F32)
    group = (lax.broadcasted_iota(jnp.int32, (NB, total), 1) // n).astype(F32)
    return jnp.where(hit > 0.0, rank + MOST * group, -1.0), weights


def select_kernel(scaled, here, *refs):
    packed, refs = refs[:SIDE], refs[SIDE:]
    if scaled:
        outs, (sel_t, rows, metas, sel) = refs[:GROUP], refs[GROUP:]
    else:
        outs, (rows, metas, sel) = refs[:GROUP], refs[GROUP:]
    n = rows.shape[0] // SIDE
    d = rows.shape[1]
    total = SIDE * n
    blocks = d // LANES
    for j in range(SIDE):
        metas[j] = packed[j][2 * blocks * n :, :]
        for k in range(blocks):
            lo = (k + blocks if scaled else k) * n
            rows[j * n : (j + 1) * n, k * LANES : (k + 1) * LANES] = packed[j][lo : lo + n, :]
    slot, weights = slots(experts(here), metas, n)
    at = lax.broadcasted_iota(jnp.int32, (BLK, total), 0).astype(F32)
    scale = []
    for i in range(NB):
        one = at == slot[i : i + 1, :]
        sel[i * BLK : (i + 1) * BLK, :] = jnp.where(one, 1.0, 0.0).astype(BF16)
        if scaled:
            scale.append(jnp.sum(jnp.where(one, weights[i], 0.0), axis=1, keepdims=True))
    width = 512
    for k in range(d // width):
        cols = slice(k * width, (k + 1) * width)
        got = jnp.dot(sel[...], rows[:, cols], preferred_element_type=F32)
        for i in range(NB):
            part = got[i * BLK : (i + 1) * BLK, :]
            if scaled:
                part = part * scale[i]
            lo = 0 if i >= GROUP else BLK
            outs[i % GROUP][lo : lo + BLK, cols] = part.astype(BF16)
    if scaled:
        sel_t[...] = jnp.transpose(sel[...].astype(F32)).astype(BF16)


def select(scaled, here, packed, d):
    n = (packed[0].shape[0] - 16) * LANES // (2 * d)
    total = SIDE * n
    out = [jax.ShapeDtypeStruct((2 * BLK, d), BF16)] * GROUP
    if scaled:
        out = out + [jax.ShapeDtypeStruct((total, SLOTS), BF16)]
    return pl.pallas_call(
        lambda *refs: select_kernel(scaled, *refs),
        out_shape=out,
        in_specs=[SM] + [VM] * SIDE,
        out_specs=[VM] * len(out),
        scratch_shapes=[
            pltpu.VMEM((total, d), BF16),
            pltpu.VMEM((SIDE, 16, LANES), BF16),
            pltpu.VMEM((SLOTS, total), BF16),
        ],
        compiler_params=params(),
        cost_estimate=cost(2 * SLOTS * total * d, 2 * d * (SLOTS + total)),
        name="select_g" if scaled else "select_x",
    )(here, *packed)


def weights_kernel(per, gs, ds, gu, dn, w_gu, w_dn):
    side = gu.shape[0] // per
    step = pl.program_id(0)
    for i in range(per):
        at = slice(i * side, (i + 1) * side)
        for codes, scales, out in ((gu, gs, w_gu), (dn, ds, w_dn)):
            for j in range(codes.shape[1] // side):
                cols = slice(j * side, (j + 1) * side)
                scale = scales[j, 0, step * per + i]
                out[at, cols] = (codes[at, cols].astype(F32) * scale).astype(BF16)


def weights(gu, dn, gs, ds):
    d, f2 = gu.shape
    f = dn.shape[1]
    nblk = gs.shape[1]
    per = 2
    side = d // nblk * per
    blocks = [pl.BlockSpec((side, f2), lambda i: (i, 0)), pl.BlockSpec((side, f), lambda i: (i, 0))]
    return pl.pallas_call(
        lambda *refs: weights_kernel(per, *refs),
        grid=(nblk // per,),
        out_shape=[jax.ShapeDtypeStruct((d, f2), BF16), jax.ShapeDtypeStruct((d, f), BF16)],
        in_specs=[SM] * 2 + blocks,
        out_specs=blocks,
        compiler_params=params(),
        cost_estimate=cost(d * f2 * 6, 4 * d * (f2 + f)),
        name="weights",
    )(gs.transpose(2, 0, 1), ds.transpose(2, 0, 1), gu, dn)


def forward_kernel(*refs):
    xs, (w_gu, hid_t, upslope, act, rows) = refs[: GROUP + 1], refs[GROUP + 1 :]
    f = hid_t.shape[0]
    width = 256
    gather(xs, rows)
    for k in range(f // width):
        lo, hi = k * width, (k + 1) * width
        gate = jnp.dot(rows[...], w_gu[:, lo:hi], preferred_element_type=F32)
        up = jnp.dot(rows[...], w_gu[:, f + lo : f + hi], preferred_element_type=F32)
        s = jax.nn.sigmoid(gate)
        a = gate * s
        act[:, lo:hi] = a
        upslope[:, lo:hi] = up * (s * (1.0 + gate * (1.0 - s)))
        hid_t[lo:hi, :] = jnp.transpose(a * up).astype(BF16)


def forward(xs, w_gu):
    d, f2 = w_gu.shape
    f = f2 // 2
    return pl.pallas_call(
        forward_kernel,
        out_shape=[
            jax.ShapeDtypeStruct((f, SLOTS), BF16),
            jax.ShapeDtypeStruct((SLOTS, f), F32),
            jax.ShapeDtypeStruct((SLOTS, f), F32),
        ],
        in_specs=[VM] * (GROUP + 2),
        out_specs=[VM] * 3,
        scratch_shapes=[pltpu.VMEM((SLOTS, d), BF16)],
        compiler_params=params(),
        cost_estimate=cost(2 * SLOTS * d * f2, 2 * d * (SLOTS + f2) + 10 * SLOTS * f),
        name="forward",
    )(*xs, w_gu)


def product(by, owners, here, gs, hid_t, rows):
    width = rows.shape[1]
    cols = pl.ds(pl.multiple_of(lax.rem(here[1] + by, owners) * width, width), width)
    gather(gs, rows, cols)
    return jnp.dot(hid_t, rows[...], preferred_element_type=F32)


def ring_first_kernel(owners, here, *refs):
    gs, (hid_t, up, down, rows) = refs[: GROUP + 1], refs[GROUP + 1 :]
    got = product(owners // 2, owners, here, gs, hid_t[...], rows)
    half = up.shape[0]
    up[...] = got[:half, :].astype(BF16)
    down[...] = got[half:, :].astype(BF16)


def ring_first(here, gs, hid_t, owners):
    f = hid_t.shape[0]
    width = gs[0].shape[1] // owners
    return pl.pallas_call(
        lambda *refs: ring_first_kernel(owners, *refs),
        out_shape=[jax.ShapeDtypeStruct((f // 2, width), BF16)] * 2,
        in_specs=[SM] + [VM] * (GROUP + 2),
        out_specs=[VM] * 2,
        scratch_shapes=[pltpu.VMEM((SLOTS, width), BF16)],
        compiler_params=params(),
        cost_estimate=cost(2 * SLOTS * width * f, 2 * SLOTS * (f + width) + 2 * f * width),
        name="ring_first",
    )(here, *gs, hid_t)


def ring_second_kernel(part, owners, here, *refs):
    gs, (hid_t, arrived, out, rows) = refs[: GROUP + 1], refs[GROUP + 1 :]
    by = owners // 2 + (1 if part else -1)
    got = product(by, owners, here, gs, hid_t[...], rows)
    half = arrived.shape[0]
    mine, rest = slice(part * half, (part + 1) * half), slice((1 - part) * half, (2 - part) * half)
    out[mine, :] = (got[mine, :] + arrived[...].astype(F32)).astype(BF16)
    out[rest, :] = got[rest, :].astype(BF16)


def ring_second(part, here, gs, hid_t, arrived, owners):
    f = hid_t.shape[0]
    width = gs[0].shape[1] // owners
    return pl.pallas_call(
        lambda *refs: ring_second_kernel(part, owners, *refs),
        out_shape=jax.ShapeDtypeStruct((f, width), BF16),
        in_specs=[SM] + [VM] * (GROUP + 3),
        out_specs=VM,
        scratch_shapes=[pltpu.VMEM((SLOTS, width), BF16)],
        compiler_params=params(),
        cost_estimate=cost(2 * SLOTS * width * f, 2 * SLOTS * (f + width) + 4 * f * width),
        name="ring_second",
    )(here, *gs, hid_t, arrived)


def products_kernel(bys, owners, here, *refs):
    gs, hid_t, outs, rows = refs[: GROUP + 1], refs[GROUP + 1], refs[GROUP + 2 : -1], refs[-1]
    for by, out in zip(bys, outs):
        out[...] = product(by, owners, here, gs, hid_t[...], rows)


def products(bys, here, gs, hid_t, owners):
    f = hid_t.shape[0]
    width = gs[0].shape[1] // owners
    return pl.pallas_call(
        lambda *refs: products_kernel(bys, owners, *refs),
        out_shape=[jax.ShapeDtypeStruct((f, width), F32)] * len(bys),
        in_specs=[SM] + [VM] * (GROUP + 2),
        out_specs=[VM] * len(bys),
        scratch_shapes=[pltpu.VMEM((SLOTS, width), BF16)],
        compiler_params=params(),
        cost_estimate=cost(2 * SLOTS * width * f * len(bys), 2 * SLOTS * f + 6 * f * width * len(bys)),
        name="products",
    )(here, *gs, hid_t)


def add_kernel(mine, *refs):
    arrived, out = refs[:-1], refs[-1]
    total = mine[...]
    for a in arrived:
        total = total + a[...].astype(F32)
    out[...] = total.astype(BF16) if len(arrived) == 1 else jnp.transpose(total)


def add(mine, *arrived):
    f, width = mine.shape
    if len(arrived) == 1:
        out = jax.ShapeDtypeStruct((f, width), BF16)
    else:
        out = jax.ShapeDtypeStruct((width, f), F32)
    return pl.pallas_call(
        add_kernel,
        out_shape=out,
        in_specs=[VM] * (1 + len(arrived)),
        out_specs=VM,
        compiler_params=params(),
        cost_estimate=cost(4 * f * width, 10 * f * width),
        name="add",
    )(mine, *arrived)


def zhop(a, by):
    n = lax.axis_size("dp")
    return lax.ppermute(a, "dp", [(i, (i + by) % n) for i in range(n)])


def back_kernel(at, *refs):
    gs, refs = refs[:-7], refs[-7:]
    w_dn, upslope, act, w_gu, out, rows, dp = refs
    count = GROUP * BLK
    d, f = w_dn.shape
    mine = slice(at * count, (at + 1) * count)
    if len(gs) == 1:
        rows[...] = gs[0][...]
    else:
        for i, g in enumerate(gs):
            rows[i * BLK : (i + 1) * BLK, :] = g[0:BLK, :]
    fw, dw = 256, 512
    for k in range(f // fw):
        lo, hi = k * fw, (k + 1) * fw
        dh = jnp.dot(rows[...], w_dn[:, lo:hi], preferred_element_type=F32)
        dp[:, lo:hi] = (dh * upslope[mine, lo:hi]).astype(BF16)
        dp[:, f + lo : f + hi] = (dh * act[mine, lo:hi]).astype(BF16)
    for k in range(d // dw):
        cols = slice(k * dw, (k + 1) * dw)
        got = lax.dot_general(
            dp[...], w_gu[cols, :], (((1,), (1,)), ((), ())), preferred_element_type=F32
        )
        out[:, cols] = got.astype(BF16)


def back(gs, w_dn, upslope, act, w_gu, at):
    d, f = w_dn.shape
    rows = GROUP * BLK
    return pl.pallas_call(
        lambda *refs: back_kernel(at, *refs),
        out_shape=jax.ShapeDtypeStruct((rows, d), BF16),
        in_specs=[VM] * (len(gs) + 4),
        out_specs=VM,
        scratch_shapes=[pltpu.VMEM((rows, d), BF16), pltpu.VMEM((rows, 2 * f), BF16)],
        compiler_params=params(),
        cost_estimate=cost(6 * rows * d * f, 2 * d * (2 * rows + 3 * f) + 8 * rows * f),
        name="back",
    )(*gs, w_dn, upslope, act, w_gu)


def second_kernel(*refs):
    blocks, out = refs[:-1], refs[-1]
    for i, b in enumerate(blocks):
        out[i * BLK : (i + 1) * BLK, :] = b[BLK:, :]


def second(blocks):
    d = blocks[0].shape[1]
    return pl.pallas_call(
        second_kernel,
        out_shape=jax.ShapeDtypeStruct((len(blocks) * BLK, d), BF16),
        in_specs=[VM] * len(blocks),
        out_specs=VM,
        compiler_params=params(),
        cost_estimate=cost(0, 4 * len(blocks) * BLK * d),
        name="second",
    )(*blocks)


def spread(blocks):
    return [hop(a, h, 0, False) if h else a for a, (h, _) in zip(blocks, STEPS)]


def pair_kernel(mine, theirs, *outs):
    for i, out in enumerate(outs):
        at = slice(i * BLK, (i + 1) * BLK)
        out[0:BLK, :] = mine[at, :]
        out[BLK:, :] = theirs[at, :]


def pair(mine, theirs):
    d = mine.shape[1]
    return pl.pallas_call(
        pair_kernel,
        out_shape=[jax.ShapeDtypeStruct((2 * BLK, d), BF16)] * GROUP,
        in_specs=[VM] * 2,
        out_specs=[VM] * GROUP,
        compiler_params=params(),
        cost_estimate=cost(0, 8 * GROUP * BLK * d),
        name="pair",
    )(mine, theirs)


def combine_kernel(sel_t, *refs):
    ret, refs = refs[:GROUP], refs[GROUP:]
    outs, rows = refs[:SIDE], refs[SIDE]
    n, d = outs[0].shape
    for i, r in enumerate(ret):
        near, far = (GROUP + i) * BLK, i * BLK
        rows[near : near + BLK, :] = r[0:BLK, :]
        rows[far : far + BLK, :] = r[BLK:, :]
    width = 512
    for k in range(d // width):
        cols = slice(k * width, (k + 1) * width)
        got = jnp.dot(sel_t[...], rows[:, cols], preferred_element_type=F32)
        outs[0][:, cols] = got[0:n, :]
        for j in range(1, SIDE):
            outs[j][:, cols] = got[j * n : (j + 1) * n, :].astype(BF16)


def combine(sel_t, ret):
    total = sel_t.shape[0]
    n = total // SIDE
    d = ret[0].shape[1]
    return pl.pallas_call(
        combine_kernel,
        out_shape=[jax.ShapeDtypeStruct((n, d), F32)]
        + [jax.ShapeDtypeStruct((n, d), BF16)] * (SIDE - 1),
        in_specs=[VM] * (GROUP + 1),
        out_specs=[VM] * SIDE,
        scratch_shapes=[pltpu.VMEM((SLOTS, d), BF16)],
        compiler_params=params(),
        cost_estimate=cost(2 * SLOTS * d * total, 2 * d * (SLOTS + 2 * total)),
        name="combine",
    )(sel_t, *ret)


def on_device(tokens, out_grad, expert_ids, gate_probs, gu_codes, gu_scales, down_codes, down_scales):
    owners = lax.axis_size("dp")
    here = jnp.stack([lax.axis_index("expert"), lax.axis_index("dp")]).astype(jnp.int32)
    tokens, here = lax.optimization_barrier((tokens, here))

    mine = pack(tokens, out_grad, expert_ids, gate_probs)
    packed = [mine] + [hop(mine, j, 0, True) for j in (2, 1, 3)]
    w = weights(gu_codes[0], down_codes[0], gu_scales, down_scales)
    packed, (w_gu, w_dn) = lax.optimization_barrier((packed, w))
    xs = select(False, here, packed, tokens.shape[1])
    xs, packed = lax.optimization_barrier((xs, packed))
    xs = spread(xs)
    *gs, sel_t = select(True, here, packed, tokens.shape[1])
    gs = spread(gs)
    xs, gs[0] = lax.optimization_barrier((xs, gs[0]))
    xs = [hop(second(xs), 0, 1, False)] + xs
    hid_t, upslope, act = forward(xs, w_gu)
    gs, hid_t = lax.optimization_barrier((gs, hid_t))
    theirs = hop(second(gs), 0, 1, False)

    mine = back(gs, w_dn, upslope, act, w_gu, 1)
    theirs, mine = lax.optimization_barrier((theirs, mine))
    gs = [theirs] + gs
    right, left = ring_first(here, gs, hid_t, owners)
    right, left = zhop(right, 1), zhop(left, owners - 1)
    theirs = back([theirs], w_dn, upslope, act, w_gu, 0)
    theirs, right, left = lax.optimization_barrier((theirs, right, left))
    theirs = hop(theirs, 0, 1, False)
    ret = pair(mine, theirs)
    ret = [hop(a, h, 0, False, True) if h else a for a, (h, _) in zip(ret, STEPS)]
    right = ring_second(0, here, gs, hid_t, right, owners)
    left = ring_second(1, here, gs, hid_t, left, owners)
    right, left, hid_t = lax.optimization_barrier((right, left, hid_t))
    right, left = zhop(right, 1), zhop(left, owners - 1)
    bys = [b for by in range(owners // 2 - 2, 0, -1) for b in (by, owners - by)] + [0]
    *more, last = products(bys, here, gs, hid_t, owners)
    for at in range(0, len(more), 2):
        right = zhop(add(more[at], right), 1)
        left = zhop(add(more[at + 1], left), owners - 1)
    down_grad = add(last, right, left)

    own, *others = combine(sel_t, ret)
    others = [hop(a, j, 0, True, True) for j, a in zip((2, 1, 3), others)]
    token_grad = own
    for a in others:
        token_grad = token_grad + a.astype(F32)
    return token_grad.astype(BF16), down_grad[None]


def solution(mesh):
    rows = P(("expert", "dp"), None)
    per = P("expert", None, None)
    return jax.shard_map(
        on_device,
        mesh=mesh,
        in_specs=(rows, rows, rows, rows, per, per, per, per),
        out_specs=(rows, P("expert", "dp", None)),
        check_vma=False,
    )
```

```python
import jax
import jax.numpy as jnp
from jax import lax
from jax.experimental import pallas as pl
from jax.experimental.pallas import tpu as pltpu
from jax.sharding import PartitionSpec as P

F32 = jnp.float32
BF16 = jnp.bfloat16
SIDE = 4
CORES = 2
MOST = 24
BLK = SIDE * MOST
STEPS = ((2, 1), (1, 1), (3, 1), (0, 1), (2, 0), (1, 0), (3, 0), (0, 0))
NB = len(STEPS)
SLOTS = NB * BLK
GROUP = 4


def place(x, y, c):
    return (x * SIDE + y) * CORES + c


def route(hops, flip, first):
    pairs = []
    for x in range(SIDE):
        for y in range(SIDE):
            for c in range(CORES):
                if (c == 0) == first:
                    to = place((x + hops) % SIDE, y, c ^ flip)
                else:
                    to = place(x, (y + hops) % SIDE, c ^ flip)
                pairs.append((place(x, y, c), to))
    return pairs


def hop(a, hops, flip, first, back=False):
    pairs = route(hops, flip, first)
    if back:
        pairs = [(t, s) for s, t in pairs]
    return lax.ppermute(a, "expert", pairs)


VM = pl.BlockSpec(memory_space=pltpu.VMEM)
SM = pl.BlockSpec(memory_space=pltpu.SMEM)
HBM = pl.BlockSpec(memory_space=pltpu.HBM)


def params(mib=28):
    return pltpu.CompilerParams(vmem_limit_bytes=mib * 2**20)


def cost(flops, nbytes):
    return pl.CostEstimate(flops=int(flops), bytes_accessed=int(nbytes), transcendentals=0)


def gather(blocks, rows, cols=slice(None)):
    theirs, blocks = blocks[:-GROUP], blocks[-GROUP:]
    at = 0
    for t in theirs:
        rows[at : at + t.shape[0], :] = t[:, cols]
        at += t.shape[0]
    for b in blocks:
        rows[at : at + BLK, :] = b[0:BLK, cols]
        at += BLK


LANES = 512


def pack_kernel(tok, grad, ids, probs, out, got, pad, sems):
    n, d = tok.shape
    top = ids.shape[0]
    lo = 2 * n * (d // LANES)
    tail = slice(lo, lo + 16)
    copies = [
        pltpu.make_async_copy(ids, got.at[0], sems.at[0]),
        pltpu.make_async_copy(probs, pad.at[1], sems.at[1]),
    ]
    at = 0
    for part in (tok, grad):
        for k in range(d // LANES):
            source = part.at[:, k * LANES : (k + 1) * LANES]
            copies.append(pltpu.make_async_copy(source, out.at[at * n : (at + 1) * n, :], sems.at[2 + at]))
            at += 1
    for c in copies:
        c.start()
    out[tail, :] = jnp.zeros((16, LANES), BF16)
    for c in copies[:2]:
        c.wait()
    pad[0] = got[0].astype(F32)
    zero = jnp.zeros((16 - top, n), F32)
    out[tail, 0:n] = jnp.concatenate([pad[0], zero], axis=0).astype(BF16)
    rest = jnp.concatenate([pad[1], zero], axis=0)
    for i in (1, 2, 3):
        term = rest.astype(BF16)
        out[tail, i * 128 : i * 128 + n] = term
        rest = rest - term.astype(F32)
    for c in copies[2:]:
        c.wait()


def pack(tok, grad, ids, probs):
    n, d = tok.shape
    top = ids.shape[1]
    blocks = d // LANES
    return pl.pallas_call(
        pack_kernel,
        out_shape=jax.ShapeDtypeStruct((2 * n * blocks + 16, LANES), BF16),
        in_specs=[HBM] * 4,
        out_specs=VM,
        scratch_shapes=[
            pltpu.VMEM((1, top, n), jnp.int32),
            pltpu.VMEM((2, top, n), F32),
            pltpu.SemaphoreType.DMA((2 + 2 * blocks,)),
        ],
        compiler_params=params(56),
        cost_estimate=cost(0, 8 * n * d),
        name="pack",
    )(tok, grad, ids.T, probs.T)


def experts(here):
    e = here[0]
    c, y, x = lax.rem(e, CORES), lax.rem(lax.div(e, CORES), SIDE), lax.div(e, CORES * SIDE)
    found = []
    for hops, flip in STEPS:
        one = place(x, lax.rem(y + hops, SIDE), flip)
        two = place(lax.rem(x + hops, SIDE), y, 1 - flip)
        found.append(jnp.where(c == 0, one, two).astype(F32))
    return found


def slots(ex, metas, n):
    total = SIDE * n

    def along(lo):
        parts = [metas[j, :, lo : lo + 128].astype(F32) for j in range(SIDE)]
        low = lax.broadcasted_iota(jnp.int32, parts[0].shape, 1) < n
        pairs = [jnp.where(low, parts[j], pltpu.roll(parts[j + 1], n, 1)) for j in (0, 2)]
        return jnp.concatenate(pairs, axis=1)[0:8, :]

    ids = along(0)
    probs = (along(128) + along(256)) + along(384)
    hits, weights = [], []
    for i in range(NB):
        eq = ids == ex[i]
        hits.append(jnp.max(jnp.where(eq, 1.0, 0.0), axis=0, keepdims=True))
        weights.append(jnp.sum(jnp.where(eq, probs, 0.0), axis=0, keepdims=True))
    hit = jnp.concatenate(hits, axis=0)
    s_at = lax.broadcasted_iota(jnp.int32, (total, total), 0)
    t_at = lax.broadcasted_iota(jnp.int32, (total, total), 1)
    before = jnp.where((s_at < t_at) & (s_at // n == t_at // n), 1.0, 0.0).astype(BF16)
    rank = jnp.dot(hit.astype(BF16), before, preferred_element_type=F32)
    group = (lax.broadcasted_iota(jnp.int32, (NB, total), 1) // n).astype(F32)
    return jnp.where(hit > 0.0, rank + MOST * group, -1.0), weights


def select_kernel(scaled, here, *refs):
    packed, refs = refs[:SIDE], refs[SIDE:]
    if scaled:
        outs, (sel_t, rows, metas, sel) = refs[:GROUP], refs[GROUP:]
    else:
        outs, (rows, metas, sel) = refs[:GROUP], refs[GROUP:]
    n = rows.shape[0] // SIDE
    d = rows.shape[1]
    total = SIDE * n
    blocks = d // LANES
    for j in range(SIDE):
        metas[j] = packed[j][2 * blocks * n :, :]
        for k in range(blocks):
            lo = (k + blocks if scaled else k) * n
            rows[j * n : (j + 1) * n, k * LANES : (k + 1) * LANES] = packed[j][lo : lo + n, :]
    slot, weights = slots(experts(here), metas, n)
    at = lax.broadcasted_iota(jnp.int32, (BLK, total), 0).astype(F32)
    scale = []
    for i in range(NB):
        one = at == slot[i : i + 1, :]
        sel[i * BLK : (i + 1) * BLK, :] = jnp.where(one, 1.0, 0.0).astype(BF16)
        if scaled:
            scale.append(jnp.sum(jnp.where(one, weights[i], 0.0), axis=1, keepdims=True))
    width = 512
    for k in range(d // width):
        cols = slice(k * width, (k + 1) * width)
        got = jnp.dot(sel[...], rows[:, cols], preferred_element_type=F32)
        for i in range(NB):
            part = got[i * BLK : (i + 1) * BLK, :]
            if scaled:
                part = part * scale[i]
            lo = 0 if i >= GROUP else BLK
            outs[i % GROUP][lo : lo + BLK, cols] = part.astype(BF16)
    if scaled:
        sel_t[...] = jnp.transpose(sel[...].astype(F32)).astype(BF16)


def select(scaled, here, packed, d):
    n = (packed[0].shape[0] - 16) * LANES // (2 * d)
    total = SIDE * n
    out = [jax.ShapeDtypeStruct((2 * BLK, d), BF16)] * GROUP
    if scaled:
        out = out + [jax.ShapeDtypeStruct((total, SLOTS), BF16)]
    return pl.pallas_call(
        lambda *refs: select_kernel(scaled, *refs),
        out_shape=out,
        in_specs=[SM] + [VM] * SIDE,
        out_specs=[VM] * len(out),
        scratch_shapes=[
            pltpu.VMEM((total, d), BF16),
            pltpu.VMEM((SIDE, 16, LANES), BF16),
            pltpu.VMEM((SLOTS, total), BF16),
        ],
        compiler_params=params(),
        cost_estimate=cost(2 * SLOTS * total * d, 2 * d * (SLOTS + total)),
        name="select_g" if scaled else "select_x",
    )(here, *packed)


def weights_kernel(per, gs, ds, gu, dn, w_gu, w_dn):
    side = gu.shape[0] // per
    step = pl.program_id(0)
    for i in range(per):
        at = slice(i * side, (i + 1) * side)
        for codes, scales, out in ((gu, gs, w_gu), (dn, ds, w_dn)):
            for j in range(codes.shape[1] // side):
                cols = slice(j * side, (j + 1) * side)
                scale = scales[j, 0, step * per + i]
                out[at, cols] = (codes[at, cols].astype(F32) * scale).astype(BF16)


def weights(gu, dn, gs, ds):
    d, f2 = gu.shape
    f = dn.shape[1]
    nblk = gs.shape[1]
    per = 2
    side = d // nblk * per
    blocks = [pl.BlockSpec((side, f2), lambda i: (i, 0)), pl.BlockSpec((side, f), lambda i: (i, 0))]
    return pl.pallas_call(
        lambda *refs: weights_kernel(per, *refs),
        grid=(nblk // per,),
        out_shape=[jax.ShapeDtypeStruct((d, f2), BF16), jax.ShapeDtypeStruct((d, f), BF16)],
        in_specs=[SM] * 2 + blocks,
        out_specs=blocks,
        compiler_params=params(),
        cost_estimate=cost(d * f2 * 6, 4 * d * (f2 + f)),
        name="weights",
    )(gs.transpose(2, 0, 1), ds.transpose(2, 0, 1), gu, dn)


def forward_kernel(*refs):
    xs, (w_gu, hid_t, upslope, act, rows) = refs[:-5], refs[-5:]
    f = hid_t.shape[0]
    width = 256
    gather(xs, rows)
    for k in range(f // width):
        lo, hi = k * width, (k + 1) * width
        gate = jnp.dot(rows[...], w_gu[:, lo:hi], preferred_element_type=F32)
        up = jnp.dot(rows[...], w_gu[:, f + lo : f + hi], preferred_element_type=F32)
        s = jax.nn.sigmoid(gate)
        a = gate * s
        act[:, lo:hi] = a
        upslope[:, lo:hi] = up * (s * (1.0 + gate * (1.0 - s)))
        hid_t[lo:hi, :] = jnp.transpose(a * up).astype(BF16)


def forward(xs, w_gu):
    d, f2 = w_gu.shape
    f = f2 // 2
    return pl.pallas_call(
        forward_kernel,
        out_shape=[
            jax.ShapeDtypeStruct((f, SLOTS), BF16),
            jax.ShapeDtypeStruct((SLOTS, f), F32),
            jax.ShapeDtypeStruct((SLOTS, f), F32),
        ],
        in_specs=[VM] * (len(xs) + 1),
        out_specs=[VM] * 3,
        scratch_shapes=[pltpu.VMEM((SLOTS, d), BF16)],
        compiler_params=params(),
        cost_estimate=cost(0, 0),
        name="forward",
    )(*xs, w_gu)


def product(by, owners, here, gs, hid_t, rows):
    width = rows.shape[1]
    cols = pl.ds(pl.multiple_of(lax.rem(here[1] + by, owners) * width, width), width)
    gather(gs, rows, cols)
    return jnp.dot(hid_t, rows[...], preferred_element_type=F32)


def ring_first_kernel(owners, here, *refs):
    gs, (hid_t, up, down, rows) = refs[: GROUP + 1], refs[GROUP + 1 :]
    got = product(owners // 2, owners, here, gs, hid_t[...], rows)
    half = up.shape[0]
    up[...] = got[:half, :].astype(BF16)
    down[...] = got[half:, :].astype(BF16)


def ring_first(here, gs, hid_t, owners):
    f = hid_t.shape[0]
    width = gs[0].shape[1] // owners
    return pl.pallas_call(
        lambda *refs: ring_first_kernel(owners, *refs),
        out_shape=[jax.ShapeDtypeStruct((f // 2, width), BF16)] * 2,
        in_specs=[SM] + [VM] * (GROUP + 2),
        out_specs=[VM] * 2,
        scratch_shapes=[pltpu.VMEM((SLOTS, width), BF16)],
        compiler_params=params(),
        cost_estimate=cost(2 * SLOTS * width * f, 2 * SLOTS * (f + width) + 2 * f * width),
        name="ring_first",
    )(here, *gs, hid_t)


def ring_second_kernel(part, owners, here, *refs):
    gs, (hid_t, arrived, out, rows) = refs[: GROUP + 1], refs[GROUP + 1 :]
    by = owners // 2 + (1 if part else -1)
    got = product(by, owners, here, gs, hid_t[...], rows)
    half = arrived.shape[0]
    mine, rest = slice(part * half, (part + 1) * half), slice((1 - part) * half, (2 - part) * half)
    out[mine, :] = (got[mine, :] + arrived[...].astype(F32)).astype(BF16)
    out[rest, :] = got[rest, :].astype(BF16)


def ring_second(part, here, gs, hid_t, arrived, owners):
    f = hid_t.shape[0]
    width = gs[0].shape[1] // owners
    return pl.pallas_call(
        lambda *refs: ring_second_kernel(part, owners, *refs),
        out_shape=jax.ShapeDtypeStruct((f, width), BF16),
        in_specs=[SM] + [VM] * (GROUP + 3),
        out_specs=VM,
        scratch_shapes=[pltpu.VMEM((SLOTS, width), BF16)],
        compiler_params=params(),
        cost_estimate=cost(2 * SLOTS * width * f, 2 * SLOTS * (f + width) + 4 * f * width),
        name="ring_second",
    )(here, *gs, hid_t, arrived)


def products_kernel(bys, owners, here, *refs):
    gs, hid_t, outs, rows = refs[: GROUP + 1], refs[GROUP + 1], refs[GROUP + 2 : -1], refs[-1]
    for by, out in zip(bys, outs):
        out[...] = product(by, owners, here, gs, hid_t[...], rows)


def products(bys, here, gs, hid_t, owners):
    f = hid_t.shape[0]
    width = gs[0].shape[1] // owners
    return pl.pallas_call(
        lambda *refs: products_kernel(bys, owners, *refs),
        out_shape=[jax.ShapeDtypeStruct((f, width), F32)] * len(bys),
        in_specs=[SM] + [VM] * (GROUP + 2),
        out_specs=[VM] * len(bys),
        scratch_shapes=[pltpu.VMEM((SLOTS, width), BF16)],
        compiler_params=params(),
        cost_estimate=cost(2 * SLOTS * width * f * len(bys), 2 * SLOTS * f + 6 * f * width * len(bys)),
        name="products",
    )(here, *gs, hid_t)


def add_kernel(mine, *refs):
    arrived, out = refs[:-1], refs[-1]
    total = mine[...]
    for a in arrived:
        total = total + a[...].astype(F32)
    out[...] = total.astype(BF16) if len(arrived) == 1 else jnp.transpose(total)


def add(mine, *arrived):
    f, width = mine.shape
    if len(arrived) == 1:
        out = jax.ShapeDtypeStruct((f, width), BF16)
    else:
        out = jax.ShapeDtypeStruct((width, f), F32)
    return pl.pallas_call(
        add_kernel,
        out_shape=out,
        in_specs=[VM] * (1 + len(arrived)),
        out_specs=VM,
        compiler_params=params(),
        cost_estimate=cost(4 * f * width, 10 * f * width),
        name="add",
    )(mine, *arrived)


def zhop(a, by):
    n = lax.axis_size("dp")
    return lax.ppermute(a, "dp", [(i, (i + by) % n) for i in range(n)])


def back_kernel(at, *refs):
    gs, refs = refs[:-7], refs[-7:]
    w_dn, upslope, act, w_gu, out, rows, dp = refs
    count = GROUP * BLK
    d, f = w_dn.shape
    mine = slice(at * count, (at + 1) * count)
    if len(gs) == 1:
        rows[...] = gs[0][...]
    else:
        for i, g in enumerate(gs):
            rows[i * BLK : (i + 1) * BLK, :] = g[0:BLK, :]
    fw, dw = 256, 512
    for k in range(f // fw):
        lo, hi = k * fw, (k + 1) * fw
        dh = jnp.dot(rows[...], w_dn[:, lo:hi], preferred_element_type=F32)
        dp[:, lo:hi] = (dh * upslope[mine, lo:hi]).astype(BF16)
        dp[:, f + lo : f + hi] = (dh * act[mine, lo:hi]).astype(BF16)
    for k in range(d // dw):
        cols = slice(k * dw, (k + 1) * dw)
        got = lax.dot_general(
            dp[...], w_gu[cols, :], (((1,), (1,)), ((), ())), preferred_element_type=F32
        )
        out[:, cols] = got.astype(BF16)


def back(gs, w_dn, upslope, act, w_gu, at):
    d, f = w_dn.shape
    rows = GROUP * BLK
    return pl.pallas_call(
        lambda *refs: back_kernel(at, *refs),
        out_shape=jax.ShapeDtypeStruct((rows, d), BF16),
        in_specs=[VM] * (len(gs) + 4),
        out_specs=VM,
        scratch_shapes=[pltpu.VMEM((rows, d), BF16), pltpu.VMEM((rows, 2 * f), BF16)],
        compiler_params=params(),
        cost_estimate=cost(6 * rows * d * f, 2 * d * (2 * rows + 3 * f) + 8 * rows * f),
        name="back",
    )(*gs, w_dn, upslope, act, w_gu)


def second_kernel(*refs):
    blocks, outs = refs[:GROUP], refs[GROUP:]
    rows = outs[0].shape[0]
    for i, b in enumerate(blocks):
        for lo in range(i * BLK, (i + 1) * BLK, 16):
            at = lo % rows
            outs[lo // rows][at : at + 16, :] = b[BLK + lo - i * BLK : BLK + lo - i * BLK + 16, :]


def second(blocks, pieces):
    d = blocks[0].shape[1]
    rows = GROUP * BLK // pieces
    return pl.pallas_call(
        second_kernel,
        out_shape=[jax.ShapeDtypeStruct((rows, d), BF16)] * pieces,
        in_specs=[VM] * GROUP,
        out_specs=[VM] * pieces,
        compiler_params=params(),
        cost_estimate=cost(0, 4 * GROUP * BLK * d),
        name="second",
    )(*blocks)


def spread(blocks):
    return [hop(a, h, 0, False) if h else a for a, (h, _) in zip(blocks, STEPS)]


def pair_kernel(mine, theirs, *outs):
    for i, out in enumerate(outs):
        at = slice(i * BLK, (i + 1) * BLK)
        out[0:BLK, :] = mine[at, :]
        out[BLK:, :] = theirs[at, :]


def pair(mine, theirs):
    d = mine.shape[1]
    return pl.pallas_call(
        pair_kernel,
        out_shape=[jax.ShapeDtypeStruct((2 * BLK, d), BF16)] * GROUP,
        in_specs=[VM] * 2,
        out_specs=[VM] * GROUP,
        compiler_params=params(),
        cost_estimate=cost(0, 8 * GROUP * BLK * d),
        name="pair",
    )(mine, theirs)


def combine_kernel(sel_t, *refs):
    ret, refs = refs[:GROUP], refs[GROUP:]
    outs, rows = refs[:SIDE], refs[SIDE]
    n, d = outs[0].shape
    for i, r in enumerate(ret):
        near, far = (GROUP + i) * BLK, i * BLK
        rows[near : near + BLK, :] = r[0:BLK, :]
        rows[far : far + BLK, :] = r[BLK:, :]
    width = 512
    for k in range(d // width):
        cols = slice(k * width, (k + 1) * width)
        got = jnp.dot(sel_t[...], rows[:, cols], preferred_element_type=F32)
        outs[0][:, cols] = got[0:n, :]
        for j in range(1, SIDE):
            outs[j][:, cols] = got[j * n : (j + 1) * n, :].astype(BF16)


def combine(sel_t, ret):
    total = sel_t.shape[0]
    n = total // SIDE
    d = ret[0].shape[1]
    return pl.pallas_call(
        combine_kernel,
        out_shape=[jax.ShapeDtypeStruct((n, d), F32)]
        + [jax.ShapeDtypeStruct((n, d), BF16)] * (SIDE - 1),
        in_specs=[VM] * (GROUP + 1),
        out_specs=[VM] * SIDE,
        scratch_shapes=[pltpu.VMEM((SLOTS, d), BF16)],
        compiler_params=params(),
        cost_estimate=cost(2 * SLOTS * d * total, 2 * d * (SLOTS + 2 * total)),
        name="combine",
    )(sel_t, *ret)


def on_device(tokens, out_grad, expert_ids, gate_probs, gu_codes, gu_scales, down_codes, down_scales):
    owners = lax.axis_size("dp")
    here = jnp.stack([lax.axis_index("expert"), lax.axis_index("dp")]).astype(jnp.int32)
    tokens, here = lax.optimization_barrier((tokens, here))

    mine = pack(tokens, out_grad, expert_ids, gate_probs)
    packed = [mine] + [hop(mine, j, 0, True) for j in (2, 1, 3)]
    w = weights(gu_codes[0], down_codes[0], gu_scales, down_scales)
    packed, (w_gu, w_dn) = lax.optimization_barrier((packed, w))
    xs = select(False, here, packed, tokens.shape[1])
    xs, packed = lax.optimization_barrier((xs, packed))
    xs = spread(xs)
    *gs, sel_t = select(True, here, packed, tokens.shape[1])
    gs = spread(gs)
    xs, gs[0] = lax.optimization_barrier((xs, gs[0]))
    xs = [hop(a, 0, 1, False) for a in second(xs, 3)] + xs
    hid_t, upslope, act = forward(xs, w_gu)
    gs, hid_t = lax.optimization_barrier((gs, hid_t))
    theirs = hop(second(gs, 1)[0], 0, 1, False)

    mine = back(gs, w_dn, upslope, act, w_gu, 1)
    theirs, mine = lax.optimization_barrier((theirs, mine))
    gs = [theirs] + gs
    right, left = ring_first(here, gs, hid_t, owners)
    right, left = zhop(right, 1), zhop(left, owners - 1)
    theirs = back([theirs], w_dn, upslope, act, w_gu, 0)
    theirs, right, left = lax.optimization_barrier((theirs, right, left))
    theirs = hop(theirs, 0, 1, False)
    ret = pair(mine, theirs)
    ret = [hop(a, h, 0, False, True) if h else a for a, (h, _) in zip(ret, STEPS)]
    right = ring_second(0, here, gs, hid_t, right, owners)
    left = ring_second(1, here, gs, hid_t, left, owners)
    right, left, hid_t = lax.optimization_barrier((right, left, hid_t))
    right, left = zhop(right, 1), zhop(left, owners - 1)
    bys = [b for by in range(owners // 2 - 2, 0, -1) for b in (by, owners - by)] + [0]
    *more, last = products(bys, here, gs, hid_t, owners)
    for at in range(0, len(more), 2):
        right = zhop(add(more[at], right), 1)
        left = zhop(add(more[at + 1], left), owners - 1)
    down_grad = add(last, right, left)

    own, *others = combine(sel_t, ret)
    others = [hop(a, j, 0, True, True) for j, a in zip((2, 1, 3), others)]
    token_grad = own
    for a in others:
        token_grad = token_grad + a.astype(F32)
    return token_grad.astype(BF16), down_grad[None]


def solution(mesh):
    rows = P(("expert", "dp"), None)
    per = P("expert", None, None)
    return jax.shard_map(
        on_device,
        mesh=mesh,
        in_specs=(rows, rows, rows, rows, per, per, per, per),
        out_specs=(rows, P("expert", "dp", None)),
        check_vma=False,
    )
```

```python
import jax
import jax.numpy as jnp
from jax import lax
from jax.experimental import pallas as pl
from jax.experimental.pallas import tpu as pltpu
from jax.sharding import PartitionSpec as P

F32 = jnp.float32
BF16 = jnp.bfloat16
SIDE = 4
CORES = 2
MOST = 24
BLK = SIDE * MOST
STEPS = ((2, 1), (1, 1), (3, 1), (0, 1), (2, 0), (1, 0), (3, 0), (0, 0))
NB = len(STEPS)
SLOTS = NB * BLK
GROUP = 4


def place(x, y, c):
    return (x * SIDE + y) * CORES + c


def route(hops, flip, first):
    pairs = []
    for x in range(SIDE):
        for y in range(SIDE):
            for c in range(CORES):
                if (c == 0) == first:
                    to = place((x + hops) % SIDE, y, c ^ flip)
                else:
                    to = place(x, (y + hops) % SIDE, c ^ flip)
                pairs.append((place(x, y, c), to))
    return pairs


def hop(a, hops, flip, first, back=False):
    pairs = route(hops, flip, first)
    if back:
        pairs = [(t, s) for s, t in pairs]
    return lax.ppermute(a, "expert", pairs)


VM = pl.BlockSpec(memory_space=pltpu.VMEM)
SM = pl.BlockSpec(memory_space=pltpu.SMEM)
HBM = pl.BlockSpec(memory_space=pltpu.HBM)


def params(mib=28):
    return pltpu.CompilerParams(vmem_limit_bytes=mib * 2**20)


def cost(flops, nbytes):
    return pl.CostEstimate(flops=int(flops), bytes_accessed=int(nbytes), transcendentals=0)


def gather(blocks, rows, cols=slice(None)):
    theirs, blocks = blocks[:-GROUP], blocks[-GROUP:]
    at = 0
    for t in theirs:
        rows[at : at + t.shape[0], :] = t[:, cols]
        at += t.shape[0]
    for b in blocks:
        rows[at : at + BLK, :] = b[0:BLK, cols]
        at += BLK


LANES = 512


def pack_kernel(tok, ids, probs, out, got, pad, sems):
    n, d = tok.shape
    top = ids.shape[0]
    lo = n * (d // LANES)
    tail = slice(lo, lo + 16)
    copies = [
        pltpu.make_async_copy(ids, got.at[0], sems.at[0]),
        pltpu.make_async_copy(probs, pad.at[1], sems.at[1]),
    ]
    for k in range(d // LANES):
        source = tok.at[:, k * LANES : (k + 1) * LANES]
        copies.append(pltpu.make_async_copy(source, out.at[k * n : (k + 1) * n, :], sems.at[2 + k]))
    for c in copies:
        c.start()
    out[tail, :] = jnp.zeros((16, LANES), BF16)
    for c in copies[:2]:
        c.wait()
    pad[0] = got[0].astype(F32)
    zero = jnp.zeros((16 - top, n), F32)
    out[tail, 0:n] = jnp.concatenate([pad[0], zero], axis=0).astype(BF16)
    rest = jnp.concatenate([pad[1], zero], axis=0)
    for i in (1, 2, 3):
        term = rest.astype(BF16)
        out[tail, i * 128 : i * 128 + n] = term
        rest = rest - term.astype(F32)
    for c in copies[2:]:
        c.wait()


def pack(tok, ids, probs):
    n, d = tok.shape
    top = ids.shape[1]
    blocks = d // LANES
    return pl.pallas_call(
        pack_kernel,
        out_shape=jax.ShapeDtypeStruct((n * blocks + 16, LANES), BF16),
        in_specs=[HBM] * 3,
        out_specs=VM,
        scratch_shapes=[
            pltpu.VMEM((1, top, n), jnp.int32),
            pltpu.VMEM((2, top, n), F32),
            pltpu.SemaphoreType.DMA((2 + blocks,)),
        ],
        compiler_params=params(56),
        cost_estimate=cost(0, 8 * n * d),
        name="pack",
    )(tok, ids.T, probs.T)


def experts(here):
    e = here[0]
    c, y, x = lax.rem(e, CORES), lax.rem(lax.div(e, CORES), SIDE), lax.div(e, CORES * SIDE)
    found = []
    for hops, flip in STEPS:
        one = place(x, lax.rem(y + hops, SIDE), flip)
        two = place(lax.rem(x + hops, SIDE), y, 1 - flip)
        found.append(jnp.where(c == 0, one, two).astype(F32))
    return found


def slots(ex, metas, n):
    total = SIDE * n

    def along(lo):
        parts = [metas[j, :, lo : lo + 128].astype(F32) for j in range(SIDE)]
        low = lax.broadcasted_iota(jnp.int32, parts[0].shape, 1) < n
        pairs = [jnp.where(low, parts[j], pltpu.roll(parts[j + 1], n, 1)) for j in (0, 2)]
        return jnp.concatenate(pairs, axis=1)[0:8, :]

    ids = along(0)
    probs = (along(128) + along(256)) + along(384)
    hits, weights = [], []
    for i in range(NB):
        eq = ids == ex[i]
        hits.append(jnp.max(jnp.where(eq, 1.0, 0.0), axis=0, keepdims=True))
        weights.append(jnp.sum(jnp.where(eq, probs, 0.0), axis=0, keepdims=True))
    hit = jnp.concatenate(hits, axis=0)
    s_at = lax.broadcasted_iota(jnp.int32, (total, total), 0)
    t_at = lax.broadcasted_iota(jnp.int32, (total, total), 1)
    before = jnp.where((s_at < t_at) & (s_at // n == t_at // n), 1.0, 0.0).astype(BF16)
    rank = jnp.dot(hit.astype(BF16), before, preferred_element_type=F32)
    group = (lax.broadcasted_iota(jnp.int32, (NB, total), 1) // n).astype(F32)
    return jnp.where(hit > 0.0, rank + MOST * group, -1.0), weights


def select_kernel(scaled, here, *refs):
    packed, refs = refs[:SIDE], refs[SIDE:]
    if scaled:
        grads, refs = refs[:SIDE], refs[SIDE:]
        outs, (sel_t, rows, metas, sel) = refs[:GROUP], refs[GROUP:]
    else:
        outs, (rows, metas, sel) = refs[:GROUP], refs[GROUP:]
    n = rows.shape[0] // SIDE
    d = rows.shape[1]
    total = SIDE * n
    blocks = d // LANES
    for j in range(SIDE):
        metas[j] = packed[j][blocks * n :, :]
        for k in range(blocks):
            cols = slice(k * LANES, (k + 1) * LANES)
            block = grads[j][:, cols] if scaled else packed[j][k * n : (k + 1) * n, :]
            rows[j * n : (j + 1) * n, cols] = block
    slot, weights = slots(experts(here), metas, n)
    at = lax.broadcasted_iota(jnp.int32, (BLK, total), 0).astype(F32)
    scale = []
    for i in range(NB):
        one = at == slot[i : i + 1, :]
        sel[i * BLK : (i + 1) * BLK, :] = jnp.where(one, 1.0, 0.0).astype(BF16)
        if scaled:
            scale.append(jnp.sum(jnp.where(one, weights[i], 0.0), axis=1, keepdims=True))
    width = 512
    for k in range(d // width):
        cols = slice(k * width, (k + 1) * width)
        got = jnp.dot(sel[...], rows[:, cols], preferred_element_type=F32)
        for i in range(NB):
            part = got[i * BLK : (i + 1) * BLK, :]
            if scaled:
                part = part * scale[i]
            lo = 0 if i >= GROUP else BLK
            outs[i % GROUP][lo : lo + BLK, cols] = part.astype(BF16)
    if scaled:
        sel_t[...] = jnp.transpose(sel[...].astype(F32)).astype(BF16)


def select(here, packed, d, grads=()):
    scaled = len(grads) > 0
    n = (packed[0].shape[0] - 16) * LANES // d
    total = SIDE * n
    out = [jax.ShapeDtypeStruct((2 * BLK, d), BF16)] * GROUP
    if scaled:
        out = out + [jax.ShapeDtypeStruct((total, SLOTS), BF16)]
    return pl.pallas_call(
        lambda *refs: select_kernel(scaled, *refs),
        out_shape=out,
        in_specs=[SM] + [VM] * (SIDE + len(grads)),
        out_specs=[VM] * len(out),
        scratch_shapes=[
            pltpu.VMEM((total, d), BF16),
            pltpu.VMEM((SIDE, 16, LANES), BF16),
            pltpu.VMEM((SLOTS, total), BF16),
        ],
        compiler_params=params(),
        cost_estimate=cost(0, 0),
        name="select_g" if scaled else "select_x",
    )(here, *packed, *grads)


def weights_kernel(per, gs, ds, gu, dn, w_gu, w_dn):
    side = gu.shape[0] // per
    step = pl.program_id(0)
    for i in range(per):
        at = slice(i * side, (i + 1) * side)
        for codes, scales, out in ((gu, gs, w_gu), (dn, ds, w_dn)):
            for j in range(codes.shape[1] // side):
                cols = slice(j * side, (j + 1) * side)
                scale = scales[j, 0, step * per + i]
                out[at, cols] = (codes[at, cols].astype(F32) * scale).astype(BF16)


def weights(gu, dn, gs, ds):
    d, f2 = gu.shape
    f = dn.shape[1]
    nblk = gs.shape[1]
    per = 2
    side = d // nblk * per
    blocks = [pl.BlockSpec((side, f2), lambda i: (i, 0)), pl.BlockSpec((side, f), lambda i: (i, 0))]
    return pl.pallas_call(
        lambda *refs: weights_kernel(per, *refs),
        grid=(nblk // per,),
        out_shape=[jax.ShapeDtypeStruct((d, f2), BF16), jax.ShapeDtypeStruct((d, f), BF16)],
        in_specs=[SM] * 2 + blocks,
        out_specs=blocks,
        compiler_params=params(),
        cost_estimate=cost(0, 0),
        name="weights",
    )(gs.transpose(2, 0, 1), ds.transpose(2, 0, 1), gu, dn)


def forward_kernel(*refs):
    xs, (w_gu, hid_t, upslope, act, rows) = refs[:-5], refs[-5:]
    f = hid_t.shape[0]
    width = 256
    gather(xs, rows)
    for k in range(f // width):
        lo, hi = k * width, (k + 1) * width
        gate = jnp.dot(rows[...], w_gu[:, lo:hi], preferred_element_type=F32)
        up = jnp.dot(rows[...], w_gu[:, f + lo : f + hi], preferred_element_type=F32)
        s = jax.nn.sigmoid(gate)
        a = gate * s
        act[:, lo:hi] = a
        upslope[:, lo:hi] = up * (s * (1.0 + gate * (1.0 - s)))
        hid_t[lo:hi, :] = jnp.transpose(a * up).astype(BF16)


def forward(xs, w_gu):
    d, f2 = w_gu.shape
    f = f2 // 2
    return pl.pallas_call(
        forward_kernel,
        out_shape=[
            jax.ShapeDtypeStruct((f, SLOTS), BF16),
            jax.ShapeDtypeStruct((SLOTS, f), F32),
            jax.ShapeDtypeStruct((SLOTS, f), F32),
        ],
        in_specs=[VM] * (len(xs) + 1),
        out_specs=[VM] * 3,
        scratch_shapes=[pltpu.VMEM((SLOTS, d), BF16)],
        compiler_params=params(),
        cost_estimate=cost(0, 0),
        name="forward",
    )(*xs, w_gu)


def product(by, owners, here, gs, hid_t, rows):
    width = rows.shape[1]
    cols = pl.ds(pl.multiple_of(lax.rem(here[1] + by, owners) * width, width), width)
    gather(gs, rows, cols)
    return jnp.dot(hid_t, rows[...], preferred_element_type=F32)


def ring_first_kernel(owners, here, *refs):
    gs, (hid_t, up, down, rows) = refs[: GROUP + 1], refs[GROUP + 1 :]
    got = product(owners // 2, owners, here, gs, hid_t[...], rows)
    half = up.shape[0]
    up[...] = got[:half, :].astype(BF16)
    down[...] = got[half:, :].astype(BF16)


def ring_first(here, gs, hid_t, owners):
    f = hid_t.shape[0]
    width = gs[0].shape[1] // owners
    return pl.pallas_call(
        lambda *refs: ring_first_kernel(owners, *refs),
        out_shape=[jax.ShapeDtypeStruct((f // 2, width), BF16)] * 2,
        in_specs=[SM] + [VM] * (GROUP + 2),
        out_specs=[VM] * 2,
        scratch_shapes=[pltpu.VMEM((SLOTS, width), BF16)],
        compiler_params=params(),
        cost_estimate=cost(2 * SLOTS * width * f, 2 * SLOTS * (f + width) + 2 * f * width),
        name="ring_first",
    )(here, *gs, hid_t)


def ring_second_kernel(part, owners, here, *refs):
    gs, (hid_t, arrived, out, rows) = refs[: GROUP + 1], refs[GROUP + 1 :]
    by = owners // 2 + (1 if part else -1)
    got = product(by, owners, here, gs, hid_t[...], rows)
    half = arrived.shape[0]
    mine, rest = slice(part * half, (part + 1) * half), slice((1 - part) * half, (2 - part) * half)
    out[mine, :] = (got[mine, :] + arrived[...].astype(F32)).astype(BF16)
    out[rest, :] = got[rest, :].astype(BF16)


def ring_second(part, here, gs, hid_t, arrived, owners):
    f = hid_t.shape[0]
    width = gs[0].shape[1] // owners
    return pl.pallas_call(
        lambda *refs: ring_second_kernel(part, owners, *refs),
        out_shape=jax.ShapeDtypeStruct((f, width), BF16),
        in_specs=[SM] + [VM] * (GROUP + 3),
        out_specs=VM,
        scratch_shapes=[pltpu.VMEM((SLOTS, width), BF16)],
        compiler_params=params(),
        cost_estimate=cost(2 * SLOTS * width * f, 2 * SLOTS * (f + width) + 4 * f * width),
        name="ring_second",
    )(here, *gs, hid_t, arrived)


def products_kernel(bys, owners, here, *refs):
    gs, hid_t, outs, rows = refs[: GROUP + 1], refs[GROUP + 1], refs[GROUP + 2 : -1], refs[-1]
    for by, out in zip(bys, outs):
        out[...] = product(by, owners, here, gs, hid_t[...], rows)


def products(bys, here, gs, hid_t, owners):
    f = hid_t.shape[0]
    width = gs[0].shape[1] // owners
    return pl.pallas_call(
        lambda *refs: products_kernel(bys, owners, *refs),
        out_shape=[jax.ShapeDtypeStruct((f, width), F32)] * len(bys),
        in_specs=[SM] + [VM] * (GROUP + 2),
        out_specs=[VM] * len(bys),
        scratch_shapes=[pltpu.VMEM((SLOTS, width), BF16)],
        compiler_params=params(),
        cost_estimate=cost(2 * SLOTS * width * f * len(bys), 2 * SLOTS * f + 6 * f * width * len(bys)),
        name="products",
    )(here, *gs, hid_t)


def add_kernel(mine, *refs):
    arrived, out = refs[:-1], refs[-1]
    total = mine[...]
    for a in arrived:
        total = total + a[...].astype(F32)
    out[...] = total.astype(BF16) if len(arrived) == 1 else jnp.transpose(total)


def add(mine, *arrived):
    f, width = mine.shape
    if len(arrived) == 1:
        out = jax.ShapeDtypeStruct((f, width), BF16)
    else:
        out = jax.ShapeDtypeStruct((width, f), F32)
    return pl.pallas_call(
        add_kernel,
        out_shape=out,
        in_specs=[VM] * (1 + len(arrived)),
        out_specs=VM,
        compiler_params=params(),
        cost_estimate=cost(4 * f * width, 10 * f * width),
        name="add",
    )(mine, *arrived)


def zhop(a, by):
    n = lax.axis_size("dp")
    return lax.ppermute(a, "dp", [(i, (i + by) % n) for i in range(n)])


def back_kernel(at, *refs):
    gs, refs = refs[:-7], refs[-7:]
    w_dn, upslope, act, w_gu, out, rows, dp = refs
    count = GROUP * BLK
    d, f = w_dn.shape
    mine = slice(at * count, (at + 1) * count)
    if len(gs) == 1:
        rows[...] = gs[0][...]
    else:
        for i, g in enumerate(gs):
            rows[i * BLK : (i + 1) * BLK, :] = g[0:BLK, :]
    fw, dw = 256, 512
    for k in range(f // fw):
        lo, hi = k * fw, (k + 1) * fw
        dh = jnp.dot(rows[...], w_dn[:, lo:hi], preferred_element_type=F32)
        dp[:, lo:hi] = (dh * upslope[mine, lo:hi]).astype(BF16)
        dp[:, f + lo : f + hi] = (dh * act[mine, lo:hi]).astype(BF16)
    for k in range(d // dw):
        cols = slice(k * dw, (k + 1) * dw)
        got = lax.dot_general(
            dp[...], w_gu[cols, :], (((1,), (1,)), ((), ())), preferred_element_type=F32
        )
        out[:, cols] = got.astype(BF16)


def back(gs, w_dn, upslope, act, w_gu, at):
    d, f = w_dn.shape
    rows = GROUP * BLK
    return pl.pallas_call(
        lambda *refs: back_kernel(at, *refs),
        out_shape=jax.ShapeDtypeStruct((rows, d), BF16),
        in_specs=[VM] * (len(gs) + 4),
        out_specs=VM,
        scratch_shapes=[pltpu.VMEM((rows, d), BF16), pltpu.VMEM((rows, 2 * f), BF16)],
        compiler_params=params(),
        cost_estimate=cost(6 * rows * d * f, 2 * d * (2 * rows + 3 * f) + 8 * rows * f),
        name="back",
    )(*gs, w_dn, upslope, act, w_gu)


def second_kernel(*refs):
    blocks, outs = refs[:GROUP], refs[GROUP:]
    rows = outs[0].shape[0]
    for i, b in enumerate(blocks):
        for lo in range(i * BLK, (i + 1) * BLK, 16):
            at = lo % rows
            outs[lo // rows][at : at + 16, :] = b[BLK + lo - i * BLK : BLK + lo - i * BLK + 16, :]


def second(blocks, pieces):
    d = blocks[0].shape[1]
    rows = GROUP * BLK // pieces
    return pl.pallas_call(
        second_kernel,
        out_shape=[jax.ShapeDtypeStruct((rows, d), BF16)] * pieces,
        in_specs=[VM] * GROUP,
        out_specs=[VM] * pieces,
        compiler_params=params(),
        cost_estimate=cost(0, 4 * GROUP * BLK * d),
        name="second",
    )(*blocks)


def spread(blocks):
    return [hop(a, h, 0, False) if h else a for a, (h, _) in zip(blocks, STEPS)]


def pair_kernel(mine, theirs, *outs):
    for i, out in enumerate(outs):
        at = slice(i * BLK, (i + 1) * BLK)
        out[0:BLK, :] = mine[at, :]
        out[BLK:, :] = theirs[at, :]


def pair(mine, theirs):
    d = mine.shape[1]
    return pl.pallas_call(
        pair_kernel,
        out_shape=[jax.ShapeDtypeStruct((2 * BLK, d), BF16)] * GROUP,
        in_specs=[VM] * 2,
        out_specs=[VM] * GROUP,
        compiler_params=params(),
        cost_estimate=cost(0, 8 * GROUP * BLK * d),
        name="pair",
    )(mine, theirs)


def combine_kernel(sel_t, *refs):
    ret, refs = refs[:GROUP], refs[GROUP:]
    outs, rows = refs[:SIDE], refs[SIDE]
    n, d = outs[0].shape
    for i, r in enumerate(ret):
        near, far = (GROUP + i) * BLK, i * BLK
        rows[near : near + BLK, :] = r[0:BLK, :]
        rows[far : far + BLK, :] = r[BLK:, :]
    width = 512
    for k in range(d // width):
        cols = slice(k * width, (k + 1) * width)
        got = jnp.dot(sel_t[...], rows[:, cols], preferred_element_type=F32)
        outs[0][:, cols] = got[0:n, :]
        for j in range(1, SIDE):
            outs[j][:, cols] = got[j * n : (j + 1) * n, :].astype(BF16)


def combine(sel_t, ret):
    total = sel_t.shape[0]
    n = total // SIDE
    d = ret[0].shape[1]
    return pl.pallas_call(
        combine_kernel,
        out_shape=[jax.ShapeDtypeStruct((n, d), F32)]
        + [jax.ShapeDtypeStruct((n, d), BF16)] * (SIDE - 1),
        in_specs=[VM] * (GROUP + 1),
        out_specs=[VM] * SIDE,
        scratch_shapes=[pltpu.VMEM((SLOTS, d), BF16)],
        compiler_params=params(),
        cost_estimate=cost(2 * SLOTS * d * total, 2 * d * (SLOTS + 2 * total)),
        name="combine",
    )(sel_t, *ret)


def on_device(tokens, out_grad, expert_ids, gate_probs, gu_codes, gu_scales, down_codes, down_scales):
    owners = lax.axis_size("dp")
    here = jnp.stack([lax.axis_index("expert"), lax.axis_index("dp")]).astype(jnp.int32)
    tokens, here = lax.optimization_barrier((tokens, here))

    mine = pack(tokens, expert_ids, gate_probs)
    packed = [mine] + [hop(mine, j, 0, True) for j in (2, 1, 3)]
    grads = [out_grad] + [hop(out_grad, j, 0, True) for j in (2, 1, 3)]
    xs = select(here, packed, tokens.shape[1])
    xs, packed, codes = lax.optimization_barrier((xs, packed, (gu_codes, down_codes)))
    w_gu, w_dn = weights(codes[0][0], codes[1][0], gu_scales, down_scales)
    xs = spread(xs)
    *gs, sel_t = select(here, packed, tokens.shape[1], grads)
    gs = spread(gs)
    xs, gs[0], w_gu, w_dn = lax.optimization_barrier((xs, gs[0], w_gu, w_dn))
    xs = [hop(a, 0, 1, False) for a in second(xs, 3)] + xs
    hid_t, upslope, act = forward(xs, w_gu)
    gs, hid_t = lax.optimization_barrier((gs, hid_t))
    theirs = hop(second(gs, 1)[0], 0, 1, False)

    mine = back(gs, w_dn, upslope, act, w_gu, 1)
    theirs, mine = lax.optimization_barrier((theirs, mine))
    gs = [theirs] + gs
    right, left = ring_first(here, gs, hid_t, owners)
    right, left = zhop(right, 1), zhop(left, owners - 1)
    theirs = back([theirs], w_dn, upslope, act, w_gu, 0)
    theirs, right, left = lax.optimization_barrier((theirs, right, left))
    theirs = hop(theirs, 0, 1, False)
    ret = pair(mine, theirs)
    ret = [hop(a, h, 0, False, True) if h else a for a, (h, _) in zip(ret, STEPS)]
    right = ring_second(0, here, gs, hid_t, right, owners)
    left = ring_second(1, here, gs, hid_t, left, owners)
    right, left, hid_t = lax.optimization_barrier((right, left, hid_t))
    right, left = zhop(right, 1), zhop(left, owners - 1)
    bys = [b for by in range(owners // 2 - 2, 0, -1) for b in (by, owners - by)] + [0]
    *more, last = products(bys, here, gs, hid_t, owners)
    for at in range(0, len(more), 2):
        right = zhop(add(more[at], right), 1)
        left = zhop(add(more[at + 1], left), owners - 1)
    down_grad = add(last, right, left)

    own, *others = combine(sel_t, ret)
    others = [hop(a, j, 0, True, True) for j, a in zip((2, 1, 3), others)]
    token_grad = own
    for a in others:
        token_grad = token_grad + a.astype(F32)
    return token_grad.astype(BF16), down_grad[None]


def solution(mesh):
    rows = P(("expert", "dp"), None)
    per = P("expert", None, None)
    return jax.shard_map(
        on_device,
        mesh=mesh,
        in_specs=(rows, rows, rows, rows, per, per, per, per),
        out_specs=(rows, P("expert", "dp", None)),
        check_vma=False,
    )
```

```python
import jax
import jax.numpy as jnp
from jax import lax
from jax.experimental import pallas as pl
from jax.experimental.pallas import tpu as pltpu
from jax.sharding import PartitionSpec as P

F32 = jnp.float32
BF16 = jnp.bfloat16
SIDE = 4
CORES = 2
MOST = 24
BLK = SIDE * MOST
STEPS = ((2, 1), (1, 1), (3, 1), (0, 1), (2, 0), (1, 0), (3, 0), (0, 0))
NB = len(STEPS)
SLOTS = NB * BLK
GROUP = 4


def place(x, y, c):
    return (x * SIDE + y) * CORES + c


def route(hops, flip, first):
    pairs = []
    for x in range(SIDE):
        for y in range(SIDE):
            for c in range(CORES):
                if (c == 0) == first:
                    to = place((x + hops) % SIDE, y, c ^ flip)
                else:
                    to = place(x, (y + hops) % SIDE, c ^ flip)
                pairs.append((place(x, y, c), to))
    return pairs


def hop(a, hops, flip, first, back=False):
    pairs = route(hops, flip, first)
    if back:
        pairs = [(t, s) for s, t in pairs]
    return lax.ppermute(a, "expert", pairs)


VM = pl.BlockSpec(memory_space=pltpu.VMEM)
SM = pl.BlockSpec(memory_space=pltpu.SMEM)
HBM = pl.BlockSpec(memory_space=pltpu.HBM)


def params(mib=28):
    return pltpu.CompilerParams(vmem_limit_bytes=mib * 2**20)


def cost(flops, nbytes):
    return pl.CostEstimate(flops=int(flops), bytes_accessed=int(nbytes), transcendentals=0)


def gather(blocks, rows, cols=slice(None)):
    theirs, blocks = blocks[:-GROUP], blocks[-GROUP:]
    at = 0
    for t in theirs:
        rows[at : at + t.shape[0], :] = t[:, cols]
        at += t.shape[0]
    for b in blocks:
        rows[at : at + BLK, :] = b[0:BLK, cols]
        at += BLK


LANES = 512


def pack_kernel(tok, grad, ids, probs, out, grad_out, got, pad, sems):
    n, d = tok.shape
    top = ids.shape[0]
    lo = n * (d // LANES)
    tail = slice(lo, lo + 16)
    copies = [
        pltpu.make_async_copy(ids, got.at[0], sems.at[0]),
        pltpu.make_async_copy(probs, pad.at[1], sems.at[1]),
    ]
    for k in range(d // LANES):
        source = tok.at[:, k * LANES : (k + 1) * LANES]
        copies.append(pltpu.make_async_copy(source, out.at[k * n : (k + 1) * n, :], sems.at[3 + k]))
    copies.append(pltpu.make_async_copy(grad, grad_out, sems.at[2]))
    for c in copies:
        c.start()
    out[tail, :] = jnp.zeros((16, LANES), BF16)
    for c in copies[:2]:
        c.wait()
    pad[0] = got[0].astype(F32)
    zero = jnp.zeros((16 - top, n), F32)
    out[tail, 0:n] = jnp.concatenate([pad[0], zero], axis=0).astype(BF16)
    rest = jnp.concatenate([pad[1], zero], axis=0)
    for i in (1, 2, 3):
        term = rest.astype(BF16)
        out[tail, i * 128 : i * 128 + n] = term
        rest = rest - term.astype(F32)
    for c in copies[2:]:
        c.wait()


def pack(tok, grad, ids, probs):
    n, d = tok.shape
    top = ids.shape[1]
    blocks = d // LANES
    return pl.pallas_call(
        pack_kernel,
        out_shape=[
            jax.ShapeDtypeStruct((n * blocks + 16, LANES), BF16),
            jax.ShapeDtypeStruct((n, d), BF16),
        ],
        in_specs=[HBM] * 4,
        out_specs=[VM] * 2,
        scratch_shapes=[
            pltpu.VMEM((1, top, n), jnp.int32),
            pltpu.VMEM((2, top, n), F32),
            pltpu.SemaphoreType.DMA((3 + blocks,)),
        ],
        compiler_params=params(56),
        cost_estimate=cost(0, 8 * n * d),
        name="pack",
    )(tok, grad, ids.T, probs.T)


def experts(here):
    e = here[0]
    c, y, x = lax.rem(e, CORES), lax.rem(lax.div(e, CORES), SIDE), lax.div(e, CORES * SIDE)
    found = []
    for hops, flip in STEPS:
        one = place(x, lax.rem(y + hops, SIDE), flip)
        two = place(lax.rem(x + hops, SIDE), y, 1 - flip)
        found.append(jnp.where(c == 0, one, two).astype(F32))
    return found


def slots(ex, metas, n):
    total = SIDE * n

    def along(lo):
        parts = [metas[j, :, lo : lo + 128].astype(F32) for j in range(SIDE)]
        low = lax.broadcasted_iota(jnp.int32, parts[0].shape, 1) < n
        pairs = [jnp.where(low, parts[j], pltpu.roll(parts[j + 1], n, 1)) for j in (0, 2)]
        return jnp.concatenate(pairs, axis=1)[0:8, :]

    ids = along(0)
    probs = (along(128) + along(256)) + along(384)
    hits, weights = [], []
    for i in range(NB):
        eq = ids == ex[i]
        hits.append(jnp.max(jnp.where(eq, 1.0, 0.0), axis=0, keepdims=True))
        weights.append(jnp.sum(jnp.where(eq, probs, 0.0), axis=0, keepdims=True))
    hit = jnp.concatenate(hits, axis=0)
    s_at = lax.broadcasted_iota(jnp.int32, (total, total), 0)
    t_at = lax.broadcasted_iota(jnp.int32, (total, total), 1)
    before = jnp.where((s_at < t_at) & (s_at // n == t_at // n), 1.0, 0.0).astype(BF16)
    rank = jnp.dot(hit.astype(BF16), before, preferred_element_type=F32)
    group = (lax.broadcasted_iota(jnp.int32, (NB, total), 1) // n).astype(F32)
    return jnp.where(hit > 0.0, rank + MOST * group, -1.0), weights


def select_kernel(scaled, here, *refs):
    packed, refs = refs[:SIDE], refs[SIDE:]
    if scaled:
        grads, refs = refs[:SIDE], refs[SIDE:]
        outs, (sel_t, rows, metas, sel) = refs[:GROUP], refs[GROUP:]
    else:
        outs, (rows, metas, sel) = refs[:GROUP], refs[GROUP:]
    n = rows.shape[0] // SIDE
    d = rows.shape[1]
    total = SIDE * n
    blocks = d // LANES
    for j in range(SIDE):
        metas[j] = packed[j][blocks * n :, :]
        for k in range(blocks):
            cols = slice(k * LANES, (k + 1) * LANES)
            block = grads[j][:, cols] if scaled else packed[j][k * n : (k + 1) * n, :]
            rows[j * n : (j + 1) * n, cols] = block
    slot, weights = slots(experts(here), metas, n)
    at = lax.broadcasted_iota(jnp.int32, (BLK, total), 0).astype(F32)
    scale = []
    for i in range(NB):
        one = at == slot[i : i + 1, :]
        sel[i * BLK : (i + 1) * BLK, :] = jnp.where(one, 1.0, 0.0).astype(BF16)
        if scaled:
            scale.append(jnp.sum(jnp.where(one, weights[i], 0.0), axis=1, keepdims=True))
    width = 512
    for k in range(d // width):
        cols = slice(k * width, (k + 1) * width)
        got = jnp.dot(sel[...], rows[:, cols], preferred_element_type=F32)
        for i in range(NB):
            part = got[i * BLK : (i + 1) * BLK, :]
            if scaled:
                part = part * scale[i]
            lo = 0 if i >= GROUP else BLK
            outs[i % GROUP][lo : lo + BLK, cols] = part.astype(BF16)
    if scaled:
        sel_t[...] = jnp.transpose(sel[...].astype(F32)).astype(BF16)


def select(here, packed, d, grads=()):
    scaled = len(grads) > 0
    n = (packed[0].shape[0] - 16) * LANES // d
    total = SIDE * n
    out = [jax.ShapeDtypeStruct((2 * BLK, d), BF16)] * GROUP
    if scaled:
        out = out + [jax.ShapeDtypeStruct((total, SLOTS), BF16)]
    return pl.pallas_call(
        lambda *refs: select_kernel(scaled, *refs),
        out_shape=out,
        in_specs=[SM] + [VM] * (SIDE + len(grads)),
        out_specs=[VM] * len(out),
        scratch_shapes=[
            pltpu.VMEM((total, d), BF16),
            pltpu.VMEM((SIDE, 16, LANES), BF16),
            pltpu.VMEM((SLOTS, total), BF16),
        ],
        compiler_params=params(),
        cost_estimate=cost(0, 0),
        name="select_g" if scaled else "select_x",
    )(here, *packed, *grads)


def weights_kernel(per, gs, ds, gu, dn, w_gu, w_dn):
    side = gu.shape[0] // per
    step = pl.program_id(0)
    for i in range(per):
        at = slice(i * side, (i + 1) * side)
        for codes, scales, out in ((gu, gs, w_gu), (dn, ds, w_dn)):
            for j in range(codes.shape[1] // side):
                cols = slice(j * side, (j + 1) * side)
                scale = scales[j, 0, step * per + i]
                out[at, cols] = (codes[at, cols].astype(F32) * scale).astype(BF16)


def weights(gu, dn, gs, ds):
    d, f2 = gu.shape
    f = dn.shape[1]
    nblk = gs.shape[1]
    per = 2
    side = d // nblk * per
    blocks = [pl.BlockSpec((side, f2), lambda i: (i, 0)), pl.BlockSpec((side, f), lambda i: (i, 0))]
    return pl.pallas_call(
        lambda *refs: weights_kernel(per, *refs),
        grid=(nblk // per,),
        out_shape=[jax.ShapeDtypeStruct((d, f2), BF16), jax.ShapeDtypeStruct((d, f), BF16)],
        in_specs=[SM] * 2 + blocks,
        out_specs=blocks,
        compiler_params=params(),
        cost_estimate=cost(0, 0),
        name="weights",
    )(gs.transpose(2, 0, 1), ds.transpose(2, 0, 1), gu, dn)


def forward_kernel(*refs):
    xs, (w_gu, hid_t, upslope, act, rows) = refs[:-5], refs[-5:]
    f = hid_t.shape[0]
    width = 256
    gather(xs, rows)
    for k in range(f // width):
        lo, hi = k * width, (k + 1) * width
        gate = jnp.dot(rows[...], w_gu[:, lo:hi], preferred_element_type=F32)
        up = jnp.dot(rows[...], w_gu[:, f + lo : f + hi], preferred_element_type=F32)
        s = jax.nn.sigmoid(gate)
        a = gate * s
        act[:, lo:hi] = a
        upslope[:, lo:hi] = up * (s * (1.0 + gate * (1.0 - s)))
        hid_t[lo:hi, :] = jnp.transpose(a * up).astype(BF16)


def forward(xs, w_gu):
    d, f2 = w_gu.shape
    f = f2 // 2
    return pl.pallas_call(
        forward_kernel,
        out_shape=[
            jax.ShapeDtypeStruct((f, SLOTS), BF16),
            jax.ShapeDtypeStruct((SLOTS, f), F32),
            jax.ShapeDtypeStruct((SLOTS, f), F32),
        ],
        in_specs=[VM] * (len(xs) + 1),
        out_specs=[VM] * 3,
        scratch_shapes=[pltpu.VMEM((SLOTS, d), BF16)],
        compiler_params=params(),
        cost_estimate=cost(0, 0),
        name="forward",
    )(*xs, w_gu)


def product(by, owners, here, gs, hid_t, rows):
    width = rows.shape[1]
    cols = pl.ds(pl.multiple_of(lax.rem(here[1] + by, owners) * width, width), width)
    gather(gs, rows, cols)
    return jnp.dot(hid_t, rows[...], preferred_element_type=F32)


def ring_first_kernel(owners, here, *refs):
    gs, (hid_t, up, down, rows) = refs[: GROUP + 1], refs[GROUP + 1 :]
    got = product(owners // 2, owners, here, gs, hid_t[...], rows)
    half = up.shape[0]
    up[...] = got[:half, :].astype(BF16)
    down[...] = got[half:, :].astype(BF16)


def ring_first(here, gs, hid_t, owners):
    f = hid_t.shape[0]
    width = gs[0].shape[1] // owners
    return pl.pallas_call(
        lambda *refs: ring_first_kernel(owners, *refs),
        out_shape=[jax.ShapeDtypeStruct((f // 2, width), BF16)] * 2,
        in_specs=[SM] + [VM] * (GROUP + 2),
        out_specs=[VM] * 2,
        scratch_shapes=[pltpu.VMEM((SLOTS, width), BF16)],
        compiler_params=params(),
        cost_estimate=cost(2 * SLOTS * width * f, 2 * SLOTS * (f + width) + 2 * f * width),
        name="ring_first",
    )(here, *gs, hid_t)


def ring_second_kernel(part, owners, here, *refs):
    gs, (hid_t, arrived, out, rows) = refs[: GROUP + 1], refs[GROUP + 1 :]
    by = owners // 2 + (1 if part else -1)
    got = product(by, owners, here, gs, hid_t[...], rows)
    half = arrived.shape[0]
    mine, rest = slice(part * half, (part + 1) * half), slice((1 - part) * half, (2 - part) * half)
    out[mine, :] = (got[mine, :] + arrived[...].astype(F32)).astype(BF16)
    out[rest, :] = got[rest, :].astype(BF16)


def ring_second(part, here, gs, hid_t, arrived, owners):
    f = hid_t.shape[0]
    width = gs[0].shape[1] // owners
    return pl.pallas_call(
        lambda *refs: ring_second_kernel(part, owners, *refs),
        out_shape=jax.ShapeDtypeStruct((f, width), BF16),
        in_specs=[SM] + [VM] * (GROUP + 3),
        out_specs=VM,
        scratch_shapes=[pltpu.VMEM((SLOTS, width), BF16)],
        compiler_params=params(),
        cost_estimate=cost(2 * SLOTS * width * f, 2 * SLOTS * (f + width) + 4 * f * width),
        name="ring_second",
    )(here, *gs, hid_t, arrived)


def products_kernel(bys, owners, here, *refs):
    gs, hid_t, outs, rows = refs[: GROUP + 1], refs[GROUP + 1], refs[GROUP + 2 : -1], refs[-1]
    for by, out in zip(bys, outs):
        out[...] = product(by, owners, here, gs, hid_t[...], rows)


def products(bys, here, gs, hid_t, owners):
    f = hid_t.shape[0]
    width = gs[0].shape[1] // owners
    return pl.pallas_call(
        lambda *refs: products_kernel(bys, owners, *refs),
        out_shape=[jax.ShapeDtypeStruct((f, width), F32)] * len(bys),
        in_specs=[SM] + [VM] * (GROUP + 2),
        out_specs=[VM] * len(bys),
        scratch_shapes=[pltpu.VMEM((SLOTS, width), BF16)],
        compiler_params=params(),
        cost_estimate=cost(2 * SLOTS * width * f * len(bys), 2 * SLOTS * f + 6 * f * width * len(bys)),
        name="products",
    )(here, *gs, hid_t)


def add_kernel(mine, *refs):
    arrived, out = refs[:-1], refs[-1]
    total = mine[...]
    for a in arrived:
        total = total + a[...].astype(F32)
    out[...] = total.astype(BF16) if len(arrived) == 1 else jnp.transpose(total)


def add(mine, *arrived):
    f, width = mine.shape
    if len(arrived) == 1:
        out = jax.ShapeDtypeStruct((f, width), BF16)
    else:
        out = jax.ShapeDtypeStruct((width, f), F32)
    return pl.pallas_call(
        add_kernel,
        out_shape=out,
        in_specs=[VM] * (1 + len(arrived)),
        out_specs=VM,
        compiler_params=params(),
        cost_estimate=cost(4 * f * width, 10 * f * width),
        name="add",
    )(mine, *arrived)


def zhop(a, by):
    n = lax.axis_size("dp")
    return lax.ppermute(a, "dp", [(i, (i + by) % n) for i in range(n)])


def back_kernel(at, *refs):
    gs, refs = refs[:-7], refs[-7:]
    w_dn, upslope, act, w_gu, out, rows, dp = refs
    count = GROUP * BLK
    d, f = w_dn.shape
    mine = slice(at * count, (at + 1) * count)
    if len(gs) == 1:
        rows[...] = gs[0][...]
    else:
        for i, g in enumerate(gs):
            rows[i * BLK : (i + 1) * BLK, :] = g[0:BLK, :]
    fw, dw = 256, 512
    for k in range(f // fw):
        lo, hi = k * fw, (k + 1) * fw
        dh = jnp.dot(rows[...], w_dn[:, lo:hi], preferred_element_type=F32)
        dp[:, lo:hi] = (dh * upslope[mine, lo:hi]).astype(BF16)
        dp[:, f + lo : f + hi] = (dh * act[mine, lo:hi]).astype(BF16)
    for k in range(d // dw):
        cols = slice(k * dw, (k + 1) * dw)
        got = lax.dot_general(
            dp[...], w_gu[cols, :], (((1,), (1,)), ((), ())), preferred_element_type=F32
        )
        out[:, cols] = got.astype(BF16)


def back(gs, w_dn, upslope, act, w_gu, at):
    d, f = w_dn.shape
    rows = GROUP * BLK
    return pl.pallas_call(
        lambda *refs: back_kernel(at, *refs),
        out_shape=jax.ShapeDtypeStruct((rows, d), BF16),
        in_specs=[VM] * (len(gs) + 4),
        out_specs=VM,
        scratch_shapes=[pltpu.VMEM((rows, d), BF16), pltpu.VMEM((rows, 2 * f), BF16)],
        compiler_params=params(),
        cost_estimate=cost(6 * rows * d * f, 2 * d * (2 * rows + 3 * f) + 8 * rows * f),
        name="back",
    )(*gs, w_dn, upslope, act, w_gu)


def second_kernel(*refs):
    blocks, outs = refs[:GROUP], refs[GROUP:]
    rows = outs[0].shape[0]
    for i, b in enumerate(blocks):
        for lo in range(i * BLK, (i + 1) * BLK, 16):
            at = lo % rows
            outs[lo // rows][at : at + 16, :] = b[BLK + lo - i * BLK : BLK + lo - i * BLK + 16, :]


def second(blocks, pieces):
    d = blocks[0].shape[1]
    rows = GROUP * BLK // pieces
    return pl.pallas_call(
        second_kernel,
        out_shape=[jax.ShapeDtypeStruct((rows, d), BF16)] * pieces,
        in_specs=[VM] * GROUP,
        out_specs=[VM] * pieces,
        compiler_params=params(),
        cost_estimate=cost(0, 4 * GROUP * BLK * d),
        name="second",
    )(*blocks)


def spread(blocks):
    return [hop(a, h, 0, False) if h else a for a, (h, _) in zip(blocks, STEPS)]


def pair_kernel(mine, theirs, *outs):
    for i, out in enumerate(outs):
        at = slice(i * BLK, (i + 1) * BLK)
        out[0:BLK, :] = mine[at, :]
        out[BLK:, :] = theirs[at, :]


def pair(mine, theirs):
    d = mine.shape[1]
    return pl.pallas_call(
        pair_kernel,
        out_shape=[jax.ShapeDtypeStruct((2 * BLK, d), BF16)] * GROUP,
        in_specs=[VM] * 2,
        out_specs=[VM] * GROUP,
        compiler_params=params(),
        cost_estimate=cost(0, 8 * GROUP * BLK * d),
        name="pair",
    )(mine, theirs)


def combine_kernel(sel_t, *refs):
    ret, refs = refs[:GROUP], refs[GROUP:]
    outs, rows = refs[:SIDE], refs[SIDE]
    n, d = outs[0].shape
    for i, r in enumerate(ret):
        near, far = (GROUP + i) * BLK, i * BLK
        rows[near : near + BLK, :] = r[0:BLK, :]
        rows[far : far + BLK, :] = r[BLK:, :]
    width = 512
    for k in range(d // width):
        cols = slice(k * width, (k + 1) * width)
        got = jnp.dot(sel_t[...], rows[:, cols], preferred_element_type=F32)
        outs[0][:, cols] = got[0:n, :]
        for j in range(1, SIDE):
            outs[j][:, cols] = got[j * n : (j + 1) * n, :].astype(BF16)


def combine(sel_t, ret):
    total = sel_t.shape[0]
    n = total // SIDE
    d = ret[0].shape[1]
    return pl.pallas_call(
        combine_kernel,
        out_shape=[jax.ShapeDtypeStruct((n, d), F32)]
        + [jax.ShapeDtypeStruct((n, d), BF16)] * (SIDE - 1),
        in_specs=[VM] * (GROUP + 1),
        out_specs=[VM] * SIDE,
        scratch_shapes=[pltpu.VMEM((SLOTS, d), BF16)],
        compiler_params=params(),
        cost_estimate=cost(2 * SLOTS * d * total, 2 * d * (SLOTS + 2 * total)),
        name="combine",
    )(sel_t, *ret)


def on_device(tokens, out_grad, expert_ids, gate_probs, gu_codes, gu_scales, down_codes, down_scales):
    owners = lax.axis_size("dp")
    here = jnp.stack([lax.axis_index("expert"), lax.axis_index("dp")]).astype(jnp.int32)
    tokens, here = lax.optimization_barrier((tokens, here))

    mine, out_grad = pack(tokens, out_grad, expert_ids, gate_probs)
    packed = [mine] + [hop(mine, j, 0, True) for j in (2, 1, 3)]
    grads = [out_grad] + [hop(out_grad, j, 0, True) for j in (2, 1, 3)]
    xs = select(here, packed, tokens.shape[1])
    xs, packed, codes = lax.optimization_barrier((xs, packed, (gu_codes, down_codes)))
    w_gu, w_dn = weights(codes[0][0], codes[1][0], gu_scales, down_scales)
    xs = spread(xs)
    *gs, sel_t = select(here, packed, tokens.shape[1], grads)
    gs = spread(gs)
    xs, gs[0], w_gu, w_dn = lax.optimization_barrier((xs, gs[0], w_gu, w_dn))
    xs = [hop(a, 0, 1, False) for a in second(xs, 3)] + xs
    hid_t, upslope, act = forward(xs, w_gu)
    gs, hid_t = lax.optimization_barrier((gs, hid_t))
    theirs = hop(second(gs, 1)[0], 0, 1, False)

    mine = back(gs, w_dn, upslope, act, w_gu, 1)
    theirs, mine = lax.optimization_barrier((theirs, mine))
    gs = [theirs] + gs
    right, left = ring_first(here, gs, hid_t, owners)
    right, left = zhop(right, 1), zhop(left, owners - 1)
    theirs = back([theirs], w_dn, upslope, act, w_gu, 0)
    theirs, right, left = lax.optimization_barrier((theirs, right, left))
    theirs = hop(theirs, 0, 1, False)
    ret = pair(mine, theirs)
    ret = [hop(a, h, 0, False, True) if h else a for a, (h, _) in zip(ret, STEPS)]
    right = ring_second(0, here, gs, hid_t, right, owners)
    left = ring_second(1, here, gs, hid_t, left, owners)
    right, left, hid_t = lax.optimization_barrier((right, left, hid_t))
    right, left = zhop(right, 1), zhop(left, owners - 1)
    bys = [b for by in range(owners // 2 - 2, 0, -1) for b in (by, owners - by)] + [0]
    *more, last = products(bys, here, gs, hid_t, owners)
    for at in range(0, len(more), 2):
        right = zhop(add(more[at], right), 1)
        left = zhop(add(more[at + 1], left), owners - 1)
    down_grad = add(last, right, left)

    own, *others = combine(sel_t, ret)
    others = [hop(a, j, 0, True, True) for j, a in zip((2, 1, 3), others)]
    token_grad = own
    for a in others:
        token_grad = token_grad + a.astype(F32)
    return token_grad.astype(BF16), down_grad[None]


def solution(mesh):
    rows = P(("expert", "dp"), None)
    per = P("expert", None, None)
    return jax.shard_map(
        on_device,
        mesh=mesh,
        in_specs=(rows, rows, rows, rows, per, per, per, per),
        out_specs=(rows, P("expert", "dp", None)),
        check_vma=False,
    )
```
